32 devices in a mesh: expert: 16 (over z, x, core), tensor: 2 (over y).
Axes of the slice: x: 2, y: 2, z: 4, core: 2. Of those that a mesh axis runs over, the one named last changes fastest.
Arguments:
- tokens: bfloat16 [4096, 5120], P('expert', 'tensor'), may hold values from -6 to 6
- router: bfloat16 [5120, 8], replicated, may hold values from -0.078125 to 0.078125
- gate_weight: bfloat16 [16, 5120, 2048], P('expert', None, 'tensor'), may hold values from -0.078125 to 0.078125
- up_weight: bfloat16 [16, 5120, 2048], P('expert', None, 'tensor'), may hold values from -0.078125 to 0.078125
- down_weight: bfloat16 [16, 2048, 5120], P('expert', 'tensor'), may hold values from -0.125 to 0.125
- routes: int32 [4096, 1], P('expert'), may hold values from 0 to 7; in each aligned block of 256 rows (0 to 255, 256 to 511, ...) at most 64 rows name the same one
Outputs:
- mixed: bfloat16 [4096, 5120], P('expert', 'tensor')
The draws below stay inside these ranges and needn't reach their ends.
Inputs may be any that keep to these rules, and one draw needn't show every extreme that they name: `routes`: among the 256 tokens of each index of expert, no expert is named more than 64 times, and in every draw some expert is named exactly 64 times by the tokens of some index.
All inputs are finite; a program needn't handle non-finite values.
Results may differ from the reference program's by a relative error of at most 0.009.
Values may be sent and summed in bfloat16 or wider, within the bound.
No kernel may reach another device: no remote copies, remote signals or barrier semaphores. Data moves between devices by JAX's collectives and lax.ppermute only.
A program may use at most 192 MiB of HBM per device.

```python
import math
import jax
import jax.numpy as jnp
import numpy as np
from jax import lax

D = 5120
FF = 4096
TOK_DEV = 256
EXPERTS = 8
CAP = 64
TOKENS = 4096
N_EXPERT = 16
N_TENSOR = 2


def with_spikes(values, rng, source, target, shards_of, factor):
    def block_of(position):
        return (jnp.arange(values.shape[position]) // (values.shape[position] // shards_of)).reshape((-1,) + (1,) * (values.ndim - 1 - position))

    first = jax.random.permutation(rng, shards_of)[block_of(target)]
    other_side = (block_of(target) + shards_of // 2) % shards_of
    return jnp.where((block_of(source) == first) | (block_of(source) == other_side), factor * values, values)


def block_scale(key, extent, cuts, smallest, largest):
    level, own = 1.0, jax.random.fold_in(key, 6)
    for position, blocks in cuts:
        heights = jnp.exp(jax.random.uniform(jax.random.fold_in(own, position), (blocks,), jnp.float32, smallest / len(cuts), largest / len(cuts)))
        level = level * jnp.repeat(heights, extent[position] // blocks).reshape([-1 if axis == position else 1 for axis in range(len(extent))])
    return level


def assign_block(key, own, number, rows, amount, top, reach, slope):
    order = jax.random.permutation(key, amount)
    crowded, ordinary = load_shares(amount, rows * top, reach, slope, True), load_shares(amount, rows * top, reach, slope, False)
    places = jnp.arange(amount)

    def named(sizes, rotation):
        used = int((sizes > 0).sum())
        fixed = max(1, used // 4)
        moved = fixed + (places - fixed + rotation * (used - fixed)) % max(1, amount - fixed)
        return jnp.zeros((amount,), jnp.int32).at[order[jnp.where(places < fixed, places, moved)]].set(jnp.asarray(sizes, jnp.int32))

    sizes = jnp.where(number % 4 == 0, named(crowded, number // 4), named(ordinary, number - number // 4 - 1))
    mixed = jax.random.permutation(jax.random.fold_in(own, 3), amount)
    donor, sink = mixed[0:amount // 2 * 2:2], mixed[1:amount // 2 * 2:2]
    margin = jnp.minimum(sizes[donor] - 1, reach - sizes[sink]) // 2
    margin = jnp.where((donor == order[0]) | (sink == order[0]) | (sizes[sink] == 0), 0, jnp.maximum(margin, 0))
    moved = jax.random.randint(jax.random.fold_in(own, 4), (amount // 2,), 0, 1 << 20) % (margin + 1)
    sizes = sizes.at[donor].add(-moved).at[sink].add(moved)
    items = jnp.searchsorted(jnp.cumsum(sizes), jnp.arange(rows * top), side="right").astype(jnp.int32)
    listing = items.reshape(top, rows).T
    listing = listing[jax.random.permutation(jax.random.fold_in(own, 1), rows)]
    rotation = jax.random.randint(jax.random.fold_in(own, 2), (rows, 1), 0, top)
    return jnp.take_along_axis(listing, (jnp.arange(top)[None, :] + rotation) % top, axis=1)


def load_shares(amount, total, bound, skew, full):
    loads = [(1 << 20) // math.isqrt(rank ** skew) + 1 for rank in range(1, amount + 1)]
    largest = bound if full else min(bound, max(-(-total // amount), total * loads[0] // sum(loads)))
    least = 1 if total - largest >= amount - 1 else 0
    given, surplus = [largest] + [least] * (amount - 1), total - largest - least * (amount - 1)
    while surplus > 0:
        free = [i for i in range(1, amount) if given[i] < largest] or [i for i in range(1, amount) if given[i] < bound]
        pool, remaining = sum([loads[i] for i in free]), surplus
        for i in free:
            addition = min(bound - given[i], max(1, remaining * loads[i] // pool), surplus)
            given[i] = given[i] + addition
            surplus = surplus - addition
    return np.array(given)


def centred(rng, dims, width, most, split=(), kind=jnp.bfloat16):
    drawn = width * jax.random.normal(rng, dims, jnp.float32)
    if split:
        drawn = drawn * block_scale(rng, dims, split, -0.22, 0.18)
    return jnp.clip(drawn, -most, most).astype(kind)


def bell_draw_with(rng, extent, scale, reach, shards, heavy, held_as=jnp.bfloat16):
    values = scale * jax.random.normal(rng, extent, jnp.float32)
    if shards:
        values = values * block_scale(rng, extent, shards, -0.22, 0.18)
    return jnp.clip(with_spikes(values, jax.random.fold_in(rng, 3), *heavy), -reach, reach).astype(held_as)


def setup_inputs(seed: int = 0) -> dict:
    seeds = jax.random.split(jax.random.key(seed), 7)
    tokens = centred(seeds[0], (TOKENS, D), 1.0, 6.0, ((0, 16), (1, 2)))
    router = centred(seeds[1], (D, EXPERTS), D ** -0.5, 0.078125)
    gate_weight = centred(seeds[2], (N_EXPERT, D, FF // 2), D ** -0.5, 0.078125, ((0, 16), (2, 2)))
    up_weight = centred(seeds[3], (N_EXPERT, D, FF // 2), D ** -0.5, 0.078125, ((0, 16), (2, 2)))
    down_weight = bell_draw_with(seeds[4], (N_EXPERT, FF // 2, D), FF ** -0.5, 0.125, ((0, 16), (1, 2)), (1, 2, 2, 2.0))
    routes_keys = jax.random.split(jax.random.fold_in(seeds[5], 1), TOKENS // TOK_DEV)
    routes_turns = jax.random.permutation(jax.random.fold_in(seeds[5], 3), TOKENS // TOK_DEV)
    routes = jax.vmap(lambda own, number: assign_block(jax.random.fold_in(seeds[5], 2), own, number, TOK_DEV, EXPERTS, 1, CAP, 2))(routes_keys, routes_turns).reshape((TOKENS, 1))
    return dict(tokens=tokens, router=router, gate_weight=gate_weight, up_weight=up_weight, down_weight=down_weight, routes=routes)


def reference(tokens, router, gate_weight, up_weight, down_weight, routes):
    chosen = routes[:, 0].astype(jnp.int32)
    logits = jnp.dot(tokens, router, preferred_element_type=jnp.float32)
    scores = jnp.take_along_axis(logits, chosen[:, None], axis=1)[:, 0]
    scaled = (tokens.astype(jnp.float32) * jax.nn.sigmoid(scores)[:, None]).astype(jnp.bfloat16)
    onehot = (chosen[:, None] == jnp.arange(EXPERTS, dtype=jnp.int32)[None, :]).astype(jnp.int32)
    blocks = onehot.reshape(N_EXPERT, TOK_DEV, EXPERTS)
    ranking = jnp.sum((jnp.cumsum(blocks, axis=1) - blocks) * blocks, axis=2).reshape(TOKENS)
    owners = jnp.arange(TOKENS, dtype=jnp.int32) // TOK_DEV
    column = (owners * CAP + ranking).astype(jnp.int32)
    slot_table = jnp.full((EXPERTS, N_EXPERT * CAP), TOKENS, jnp.int32)
    slot_table = slot_table.at[chosen, column].set(jnp.arange(TOKENS, dtype=jnp.int32))
    padded = jnp.concatenate([scaled, jnp.zeros((1, D), scaled.dtype)], axis=0)
    pieces = 2 * N_TENSOR
    piece_width = FF // pieces

    def expert_out(expert):
        gathered = jnp.take(padded, slot_table[expert], axis=0)
        gate_pair = lax.dynamic_slice_in_dim(gate_weight, 2 * expert, 2, 0)
        up_pair = lax.dynamic_slice_in_dim(up_weight, 2 * expert, 2, 0)
        down_pair = lax.dynamic_slice_in_dim(down_weight, 2 * expert, 2, 0)
        gate_full = jnp.concatenate([gate_pair[0], gate_pair[1]], axis=1)
        up_full = jnp.concatenate([up_pair[0], up_pair[1]], axis=1)
        gate_proj = jnp.dot(gathered, gate_full, preferred_element_type=jnp.float32)
        up_proj = jnp.dot(gathered, up_full, preferred_element_type=jnp.float32)
        hidden = (jax.nn.silu(gate_proj) * up_proj).astype(jnp.bfloat16)
        down_full = down_pair.reshape(pieces, piece_width, D)
        partials = jnp.einsum("spf,pfd->spd", hidden.reshape(-1, pieces, piece_width).astype(jnp.float32), down_full.astype(jnp.float32))
        partials = lax.optimization_barrier(partials.astype(jnp.bfloat16))
        return jnp.sum(partials.astype(jnp.float32), axis=1).astype(jnp.bfloat16)

    expert_outputs = lax.map(expert_out, jnp.arange(EXPERTS, dtype=jnp.int32))
    result = jnp.zeros((TOKENS + 1, D), expert_outputs.dtype)
    result = result.at[slot_table.reshape(-1)].set(expert_outputs.reshape(-1, D))
    return result[:TOKENS]
```

```python
import functools

import jax
import jax.numpy as jnp
from jax import lax
from jax.experimental import pallas as pl
from jax.experimental.pallas import tpu as pltpu
from jax.sharding import PartitionSpec as P

CHUNKS = 4
MIB = 1 << 20
HBM = pl.BlockSpec(memory_space=pl.ANY)
SMEM = pl.BlockSpec(memory_space=pltpu.SMEM)


def to_expert(value, mask):
    if mask == 0:
        return value
    pairs = [(i, i ^ (2 * mask)) for i in range(lax.axis_size("expert"))]
    return lax.ppermute(value, "expert", pairs)


def to_pair(value):
    return lax.ppermute(value, "expert", [(i, i ^ 1) for i in range(lax.axis_size("expert"))])


def to_tensor(value, shift):
    size = lax.axis_size("tensor")
    return lax.ppermute(value, "tensor", [(i, (i + shift) % size) for i in range(size)])


def placing_of(column, total):
    places = lax.broadcasted_iota(jnp.int32, (column.shape[0], total), 1)
    return (column == places).astype(jnp.float32).astype(jnp.bfloat16)


def pack_kernel(experts, slots, info, routes, tokens, *outs):
    blocks, column = outs[:experts], outs[experts]
    chosen = routes[...]
    rows = chosen.shape[0]
    names = lax.broadcasted_iota(jnp.int32, (rows, experts), 1)
    onehot = (chosen == names).astype(jnp.float32)
    earlier = lax.broadcasted_iota(jnp.int32, (rows, rows), 1) < lax.broadcasted_iota(
        jnp.int32, (rows, rows), 0
    )
    counts = jnp.dot(
        earlier.astype(jnp.float32).astype(jnp.bfloat16),
        onehot.astype(jnp.bfloat16),
        preferred_element_type=jnp.float32,
    )
    ranking = jnp.sum(counts * onehot, axis=1, keepdims=True).astype(jnp.int32)
    place = (chosen ^ info[0]) * slots + ranking
    column[...] = place
    packed = lax.dot_general(
        placing_of(place, experts * slots),
        tokens[...],
        (((0,), (0,)), ((), ())),
        preferred_element_type=jnp.float32,
    ).astype(jnp.bfloat16)
    for m in range(experts):
        blocks[m][...] = packed[m * slots : (m + 1) * slots]


def pack(info, routes, tokens, experts, slots):
    rows, width = tokens.shape
    steps = 2 if width % 256 == 0 else 1
    band = width // steps
    outs = pl.pallas_call(
        functools.partial(pack_kernel, experts, slots),
        grid=(steps,),
        in_specs=[
            SMEM,
            pl.BlockSpec((rows, 1), lambda i: (0, 0)),
            pl.BlockSpec((rows, band), lambda i: (0, i)),
        ],
        out_specs=[pl.BlockSpec((slots, band), lambda i: (0, i))] * experts
        + [pl.BlockSpec((rows, 1), lambda i: (0, 0))],
        out_shape=[jax.ShapeDtypeStruct((slots, width), jnp.bfloat16)] * experts
        + [jax.ShapeDtypeStruct((rows, 1), jnp.int32)],
        compiler_params=pltpu.CompilerParams(vmem_limit_bytes=24 * MIB),
        cost_estimate=pl.CostEstimate(
            flops=2 * rows * experts * slots * width, bytes_accessed=6 * rows * width, transcendentals=0
        ),
        name="pack",
    )(info, routes, tokens)
    return outs[:experts], outs[experts]


def unpack_kernel(experts, slots, column, *refs):
    blocks, mixed = refs[:experts], refs[experts]
    ordered = jnp.concatenate([b[...] for b in blocks], axis=0)
    mixed[...] = jnp.dot(
        placing_of(column[...], experts * slots), ordered, preferred_element_type=jnp.float32
    ).astype(jnp.bfloat16)


def unpack(column, blocks):
    experts = len(blocks)
    slots, width = blocks[0].shape
    rows = column.shape[0]
    steps = 2 if width % 256 == 0 else 1
    band = width // steps
    return pl.pallas_call(
        functools.partial(unpack_kernel, experts, slots),
        grid=(steps,),
        in_specs=[pl.BlockSpec((rows, 1), lambda i: (0, 0))]
        + [pl.BlockSpec((slots, band), lambda i: (0, i))] * experts,
        out_specs=pl.BlockSpec((rows, band), lambda i: (0, i)),
        out_shape=jax.ShapeDtypeStruct((rows, width), jnp.bfloat16),
        compiler_params=pltpu.CompilerParams(vmem_limit_bytes=24 * MIB),
        cost_estimate=pl.CostEstimate(
            flops=2 * rows * experts * slots * width, bytes_accessed=6 * rows * width, transcendentals=0
        ),
        name="unpack",
    )(column, *blocks)


def expert_kernel(parts, hid_step, out_step, info, *refs):
    xs, (router_t, wg, wu, wd) = refs[: 2 * parts], refs[2 * parts : 2 * parts + 4]
    outs = refs[2 * parts + 4 : 4 * parts + 4]
    (x_all, g_buf, u_buf, d_buf, h_all, o_buf, x_sem, w_sem, d_sem, o_sem) = refs[4 * parts + 4 :]
    half, width = xs[0].shape
    hidden = wg.shape[2]
    steps = hidden // hid_step
    mine, expert = info[0], info[1]

    def owner(t):
        return lax.rem(mine + t, parts)

    def span(t):
        return pl.ds(pl.multiple_of(owner(t) * width, 128), width)

    x_copies = [
        pltpu.make_async_copy(
            xs[r * parts + t], x_all.at[pl.ds(r * half, half), span(t)], x_sem.at[r * parts + t]
        )
        for r in range(2)
        for t in range(parts)
    ]
    for copy in x_copies:
        copy.start()
    g_copies, u_copies = [], []
    for j in range(steps):
        cols = pl.ds(j * hid_step, hid_step)
        g_copies.append(pltpu.make_async_copy(wg.at[0, :, cols], g_buf.at[j], w_sem.at[0, j]))
        u_copies.append(pltpu.make_async_copy(wu.at[0, :, cols], u_buf.at[j], w_sem.at[1, j]))
        g_copies[j].start()
        u_copies[j].start()
    order = list(range(1, parts)) + [0]
    d_copies = {}
    for t in order:
        d_copies[t] = pltpu.make_async_copy(wd.at[0, :, span(t)], d_buf.at[t], d_sem.at[t])
        d_copies[t].start()
    for copy in x_copies:
        copy.wait()
    x = x_all[...]
    logits = lax.dot_general(
        x, router_t[...], (((1,), (1,)), ((), ())), preferred_element_type=jnp.float32
    )
    names = lax.broadcasted_iota(jnp.int32, logits.shape, 1)
    score = jnp.sum(jnp.where(names == expert, logits, 0.0), axis=1, keepdims=True)
    scale = 1.0 / (1.0 + jnp.exp(-score))
    for j in range(steps):
        g_copies[j].wait()
        u_copies[j].wait()
        gate = scale * jnp.dot(x_all[...], g_buf[j], preferred_element_type=jnp.float32)
        up = scale * jnp.dot(x_all[...], u_buf[j], preferred_element_type=jnp.float32)
        h_all[:, j * hid_step : (j + 1) * hid_step] = (
            gate / (1.0 + jnp.exp(-gate)) * up
        ).astype(jnp.bfloat16)
    o_copies = []
    for t in order:
        d_copies[t].wait()
        for c in range(0, width, out_step):
            o_buf[t, :, c : c + out_step] = jnp.dot(
                h_all[...], d_buf[t, :, c : c + out_step], preferred_element_type=jnp.float32
            ).astype(jnp.bfloat16)
        for r in (1, 0):
            copy = pltpu.make_async_copy(
                o_buf.at[t, pl.ds(r * half, half), :], outs[r * parts + t], o_sem.at[r * parts + t]
            )
            copy.start()
            o_copies.append(copy)
    for copy in o_copies:
        copy.wait()


def expert_chunk(info, xs, router_t, gate_weight, up_weight, down_weight):
    parts = len(xs) // 2
    half, width = xs[0].shape
    rows, model = 2 * half, parts * width
    hidden = gate_weight.shape[2]
    hid_step = min(256, hidden)
    out_step = 1280 if width % 1280 == 0 else width
    bf16 = jnp.bfloat16
    return pl.pallas_call(
        functools.partial(expert_kernel, parts, hid_step, out_step),
        in_specs=[SMEM] + [HBM] * (2 * parts) + [pl.BlockSpec(memory_space=pltpu.VMEM)] + [HBM] * 3,
        out_specs=[HBM] * (2 * parts),
        out_shape=[jax.ShapeDtypeStruct((half, width), bf16)] * (2 * parts),
        scratch_shapes=[
            pltpu.VMEM((rows, model), bf16),
            pltpu.VMEM((hidden // hid_step, model, hid_step), bf16),
            pltpu.VMEM((hidden // hid_step, model, hid_step), bf16),
            pltpu.VMEM((parts, hidden, width), bf16),
            pltpu.VMEM((rows, hidden), bf16),
            pltpu.VMEM((parts, rows, width), bf16),
            pltpu.SemaphoreType.DMA((2 * parts,)),
            pltpu.SemaphoreType.DMA((2, hidden // hid_step)),
            pltpu.SemaphoreType.DMA((parts,)),
            pltpu.SemaphoreType.DMA((2 * parts,)),
        ],
        compiler_params=pltpu.CompilerParams(vmem_limit_bytes=48 * MIB),
        cost_estimate=pl.CostEstimate(
            flops=6 * rows * hidden * model,
            bytes_accessed=6 * hidden * model + 4 * rows * model,
            transcendentals=rows * hidden,
        ),
        name="expert_rows",
    )(info, *xs, router_t, gate_weight, up_weight, down_weight)


def f32(value):
    return value.astype(jnp.float32)


def on_device(tokens, router, gate_weight, up_weight, down_weight, routes):
    experts = router.shape[1]
    slots = 2 * tokens.shape[0] // experts
    parts = lax.axis_size("tensor")
    expert = lax.axis_index("expert") // 2
    place = jnp.stack([lax.axis_index("tensor"), expert]).astype(jnp.int32)
    router_t = router.T
    blocks, column = pack(expert.astype(jnp.int32).reshape(1), routes, tokens, experts, slots)
    per = experts // CHUNKS
    arrived = [to_expert(blocks[m], m) for m in range(experts)]
    returned = [None] * experts
    for c in range(CHUNKS):
        masks = range(c * per, (c + 1) * per)
        own = jnp.concatenate([arrived[m] for m in masks], axis=0)
        mine = [own] + [None] * (parts - 1)
        for t in range(1, parts):
            mine[(parts - t) % parts] = to_tensor(own, t)
        theirs = [to_pair(v) for v in mine]
        outs = expert_chunk(place, mine + theirs, router_t, gate_weight, up_weight, down_weight)
        kept, given = outs[:parts], outs[parts:]
        given = [to_pair(v) for v in given]
        gathered = []
        for t in range(1, parts):
            total = (f32(kept[t]) + f32(given[t])).astype(jnp.bfloat16)
            gathered.append(to_tensor(total, t))
        for n, m in enumerate(masks):
            rows = slice(n * slots, (n + 1) * slots)
            total = f32(kept[0][rows]) + f32(given[0][rows])
            for part in gathered:
                total = total + f32(part[rows])
            returned[m] = to_expert(total.astype(jnp.bfloat16), m)
    return unpack(column, returned)


def solution(mesh):
    return jax.shard_map(
        on_device,
        mesh=mesh,
        in_specs=(
            P("expert", "tensor"),
            P(),
            P("expert", None, "tensor"),
            P("expert", None, "tensor"),
            P("expert", "tensor", None),
            P("expert", None),
        ),
        out_specs=P("expert", "tensor"),
        check_vma=False,
    )
```

```python
import functools

import jax
import jax.numpy as jnp
from jax import lax
from jax.experimental import pallas as pl
from jax.experimental.pallas import tpu as pltpu
from jax.sharding import PartitionSpec as P

CHUNKS = 4
MIB = 1 << 20
HBM = pl.BlockSpec(memory_space=pl.ANY)
VMEM = pl.BlockSpec(memory_space=pltpu.VMEM)
SMEM = pl.BlockSpec(memory_space=pltpu.SMEM)


def to_expert(value, mask):
    if mask == 0:
        return value
    pairs = [(i, i ^ (2 * mask)) for i in range(lax.axis_size("expert"))]
    return lax.ppermute(value, "expert", pairs)


def to_pair(value):
    return lax.ppermute(value, "expert", [(i, i ^ 1) for i in range(lax.axis_size("expert"))])


def to_tensor(value, shift):
    size = lax.axis_size("tensor")
    return lax.ppermute(value, "tensor", [(i, (i + shift) % size) for i in range(size)])


def placing_of(column, total):
    places = lax.broadcasted_iota(jnp.int32, (column.shape[0], total), 1)
    return (column == places).astype(jnp.float32).astype(jnp.bfloat16)


def pack_kernel(experts, slots, info, routes, tokens, *outs):
    blocks, column = outs[:experts], outs[experts]
    chosen = routes[...]
    rows = chosen.shape[0]
    names = lax.broadcasted_iota(jnp.int32, (rows, experts), 1)
    onehot = (chosen == names).astype(jnp.float32)
    earlier = lax.broadcasted_iota(jnp.int32, (rows, rows), 1) < lax.broadcasted_iota(
        jnp.int32, (rows, rows), 0
    )
    counts = jnp.dot(
        earlier.astype(jnp.float32).astype(jnp.bfloat16),
        onehot.astype(jnp.bfloat16),
        preferred_element_type=jnp.float32,
    )
    ranking = jnp.sum(counts * onehot, axis=1, keepdims=True).astype(jnp.int32)
    place = (chosen ^ info[0]) * slots + ranking
    column[...] = place
    packed = lax.dot_general(
        placing_of(place, experts * slots),
        tokens[...],
        (((0,), (0,)), ((), ())),
        preferred_element_type=jnp.float32,
    ).astype(jnp.bfloat16)
    for m in range(experts):
        blocks[m][...] = packed[m * slots : (m + 1) * slots]


def pack(info, routes, tokens, experts, slots):
    rows, width = tokens.shape
    steps = 2 if width % 256 == 0 else 1
    band = width // steps
    outs = pl.pallas_call(
        functools.partial(pack_kernel, experts, slots),
        grid=(steps,),
        in_specs=[
            SMEM,
            pl.BlockSpec((rows, 1), lambda i: (0, 0)),
            pl.BlockSpec((rows, band), lambda i: (0, i)),
        ],
        out_specs=[pl.BlockSpec((slots, band), lambda i: (0, i))] * experts
        + [pl.BlockSpec((rows, 1), lambda i: (0, 0))],
        out_shape=[jax.ShapeDtypeStruct((slots, width), jnp.bfloat16)] * experts
        + [jax.ShapeDtypeStruct((rows, 1), jnp.int32)],
        compiler_params=pltpu.CompilerParams(vmem_limit_bytes=24 * MIB),
        cost_estimate=pl.CostEstimate(
            flops=2 * rows * experts * slots * width, bytes_accessed=6 * rows * width, transcendentals=0
        ),
        name="pack",
    )(info, routes, tokens)
    return outs[:experts], outs[experts]


def unpack_kernel(experts, slots, column, *refs):
    blocks, mixed = refs[:experts], refs[experts]
    ordered = jnp.concatenate([b[...] for b in blocks], axis=0)
    mixed[...] = jnp.dot(
        placing_of(column[...], experts * slots), ordered, preferred_element_type=jnp.float32
    ).astype(jnp.bfloat16)


def unpack(column, blocks):
    experts = len(blocks)
    slots, width = blocks[0].shape
    rows = column.shape[0]
    steps = 2 if width % 256 == 0 else 1
    band = width // steps
    return pl.pallas_call(
        functools.partial(unpack_kernel, experts, slots),
        grid=(steps,),
        in_specs=[pl.BlockSpec((rows, 1), lambda i: (0, 0))]
        + [pl.BlockSpec((slots, band), lambda i: (0, i))] * experts,
        out_specs=pl.BlockSpec((rows, band), lambda i: (0, i)),
        out_shape=jax.ShapeDtypeStruct((rows, width), jnp.bfloat16),
        compiler_params=pltpu.CompilerParams(vmem_limit_bytes=24 * MIB),
        cost_estimate=pl.CostEstimate(
            flops=2 * rows * experts * slots * width, bytes_accessed=6 * rows * width, transcendentals=0
        ),
        name="unpack",
    )(column, *blocks)


def expert_kernel(parts, hid_step, out_step, info, *refs):
    mine, theirs, (router_t, wg, wu, wd) = refs[:parts], refs[parts : 2 * parts], refs[2 * parts : 2 * parts + 4]
    kept, given = refs[2 * parts + 4 : 3 * parts + 4], refs[3 * parts + 4]
    x_all, h_all, o_buf, x_sem, o_sem = refs[3 * parts + 5 :]
    half, width = mine[0].shape
    hidden = wg.shape[2]
    index, expert = info[0], info[1]

    def owner(t):
        return lax.rem(index + t, parts)

    x_copies = []
    for t in range(parts):
        span = pl.ds(pl.multiple_of(owner(t) * width, 128), width)
        own_rows, pair_rows = pl.ds(0, half), pl.ds(half, half)
        x_copies += [
            pltpu.make_async_copy(mine[t], x_all.at[own_rows, span], x_sem.at[0, t]),
            pltpu.make_async_copy(theirs[t], x_all.at[pair_rows, span], x_sem.at[1, t]),
        ]
    for copy in x_copies:
        copy.start()
    for copy in x_copies:
        copy.wait()
    logits = lax.dot_general(
        x_all[...], router_t[...], (((1,), (1,)), ((), ())), preferred_element_type=jnp.float32
    )
    names = lax.broadcasted_iota(jnp.int32, logits.shape, 1)
    score = jnp.sum(jnp.where(names == expert, logits, 0.0), axis=1, keepdims=True)
    scale = 1.0 / (1.0 + jnp.exp(-score))
    for j in range(0, hidden, hid_step):
        cols = slice(j, j + hid_step)
        gate = scale * jnp.dot(x_all[...], wg[0, :, cols], preferred_element_type=jnp.float32)
        up = scale * jnp.dot(x_all[...], wu[0, :, cols], preferred_element_type=jnp.float32)
        h_all[:, cols] = (gate / (1.0 + jnp.exp(-gate)) * up).astype(jnp.bfloat16)
    o_copies = []
    for t in list(range(1, parts)) + [0]:
        for c in range(0, width, out_step):
            cols = pl.ds(pl.multiple_of(owner(t) * width + c, 128), out_step)
            o_buf[t, :, c : c + out_step] = jnp.dot(
                h_all[...], wd[0, :, cols], preferred_element_type=jnp.float32
            ).astype(jnp.bfloat16)
        o_copies += [
            pltpu.make_async_copy(
                o_buf.at[t, pl.ds(half, half)], given.at[:, pl.ds(t * width, width)], o_sem.at[1, t]
            ),
            pltpu.make_async_copy(o_buf.at[t, pl.ds(0, half)], kept[t], o_sem.at[0, t]),
        ]
        o_copies[-2].start()
        o_copies[-1].start()
    for copy in o_copies:
        copy.wait()


def expert_chunk(info, mine, theirs, router_t, weights):
    parts = len(mine)
    half, width = mine[0].shape
    rows, model = 2 * half, parts * width
    hidden = weights[0].shape[2]
    hid_step = min(256, hidden)
    out_step = 1280 if width % 1280 == 0 else width
    bf16 = jnp.bfloat16
    weights = [pltpu.with_memory_space_constraint(w, pltpu.VMEM) for w in weights]
    outs = pl.pallas_call(
        functools.partial(expert_kernel, parts, hid_step, out_step),
        in_specs=[SMEM] + [HBM] * (2 * parts) + [VMEM] * 4,
        out_specs=[HBM] * (parts + 1),
        out_shape=[jax.ShapeDtypeStruct((half, width), bf16)] * parts
        + [jax.ShapeDtypeStruct((half, model), bf16)],
        scratch_shapes=[
            pltpu.VMEM((rows, model), bf16),
            pltpu.VMEM((rows, hidden), bf16),
            pltpu.VMEM((parts, rows, width), bf16),
            pltpu.SemaphoreType.DMA((2, parts)),
            pltpu.SemaphoreType.DMA((2, parts)),
        ],
        compiler_params=pltpu.CompilerParams(vmem_limit_bytes=16 * MIB),
        cost_estimate=pl.CostEstimate(
            flops=6 * rows * hidden * model,
            bytes_accessed=4 * rows * model,
            transcendentals=rows * hidden,
        ),
        name="expert_rows",
    )(info, *mine, *theirs, router_t, *weights)
    return outs[:parts], outs[parts]


def load_kernel(pieces, *refs):
    count = len(refs) // 2
    sources, targets, sems = refs[:count], refs[count : 2 * count], refs[2 * count]
    copies = []
    for n in range(count):
        step = sources[n].shape[1] // pieces
        for p in range(pieces):
            rows = pl.ds(p * step, step)
            copies.append(
                pltpu.make_async_copy(sources[n].at[:, rows], targets[n].at[:, rows], sems.at[n, p])
            )
            copies[-1].start()
    for copy in copies:
        copy.wait()


def load(weights):
    pieces = 4
    return pl.pallas_call(
        functools.partial(load_kernel, pieces),
        in_specs=[HBM] * len(weights),
        out_specs=[VMEM] * len(weights),
        out_shape=[pltpu.VMEM(w.shape, w.dtype) for w in weights],
        scratch_shapes=[pltpu.SemaphoreType.DMA((len(weights), pieces))],
        compiler_params=pltpu.CompilerParams(vmem_limit_bytes=4 * MIB),
        cost_estimate=pl.CostEstimate(
            flops=0, bytes_accessed=2 * sum(w.size * 2 for w in weights), transcendentals=0
        ),
        name="load_weights",
    )(*weights)


def settled(live):
    leaves, shape = jax.tree.flatten(live)
    return jax.tree.unflatten(shape, lax.optimization_barrier(leaves))


def after(value, *earlier):
    return lax.optimization_barrier((value, *earlier))[0]


def f32(value):
    return value.astype(jnp.float32)


def on_device(tokens, router, gate_weight, up_weight, down_weight, routes):
    experts = router.shape[1]
    slots = 2 * tokens.shape[0] // experts
    part_cols = tokens.shape[1]
    parts = lax.axis_size("tensor")
    expert = lax.axis_index("expert") // 2
    place = jnp.stack([lax.axis_index("tensor"), expert]).astype(jnp.int32)
    router_t = router.T
    blocks, column = pack(expert.astype(jnp.int32).reshape(1), routes, tokens, experts, slots)
    masks = [list(range(c, experts, CHUNKS)) for c in range(CHUNKS)]
    live = dict(blocks=dict(enumerate(blocks)), arrived={}, returned={}, column=column)
    live["chunk"] = {}
    live = settled(live)
    weights_at = load([after(w, live["column"]) for w in (gate_weight, up_weight, down_weight)])
    live["weights"] = list(weights_at)
    for unit in range(CHUNKS + 4):
        before = live["chunk"]
        after_unit = {}
        c = unit
        if c < CHUNKS:
            for m in sorted(set(masks[c]) | set(range(CHUNKS if c == 0 else 0)), reverse=True):
                if m in live["blocks"]:
                    with jax.named_scope(f"dispatch_{m}"):
                        live["arrived"][m] = to_expert(live["blocks"].pop(m), m)
        c = unit - 1
        if 0 <= c < CHUNKS:
            own = jnp.concatenate([live["arrived"].pop(m) for m in masks[c]], axis=0)
            mine = [own] + [None] * (parts - 1)
            for t in range(1, parts):
                with jax.named_scope(f"features_{c}"):
                    mine[parts - t] = to_tensor(own, t)
            with jax.named_scope(f"pair_{c}"):
                after_unit[c] = dict(mine=mine, pair=to_pair(own))
        c = unit - 2
        if 0 <= c < CHUNKS:
            chunk = before[c]
            with jax.named_scope(f"pair_{c}"):
                theirs = [chunk["pair"]] + [to_pair(v) for v in chunk["mine"][1:]]
            with jax.named_scope(f"rows_{c}"):
                kept, given = expert_chunk(place, chunk["mine"], theirs, router_t, live["weights"])
            after_unit[c] = dict(kept=kept, given=given)
        c = unit - 3
        if 0 <= c < CHUNKS:
            kept = before[c]["kept"]
            with jax.named_scope(f"partial_{c}"):
                given = to_pair(before[c]["given"])
            gathered = []
            for t in range(1, parts):
                with jax.named_scope(f"reduce_{c}"):
                    total = f32(kept[t]) + f32(given[:, t * part_cols : (t + 1) * part_cols])
                    gathered.append(to_tensor(total.astype(jnp.bfloat16), t))
            after_unit[c] = dict(kept=kept[0], given=given, gathered=gathered)
        c = unit - 4
        if 0 <= c < CHUNKS:
            chunk = before[c]
            for n, m in enumerate(masks[c]):
                rows = slice(n * slots, (n + 1) * slots)
                with jax.named_scope(f"home_{m}"):
                    total = f32(chunk["kept"][rows]) + f32(chunk["given"][rows, :part_cols])
                    for part in chunk["gathered"]:
                        total = total + f32(part[rows])
                    live["returned"][m] = to_expert(total.astype(jnp.bfloat16), m)
        live["chunk"] = after_unit
        if unit == CHUNKS + 1:
            live.pop("weights")
        if unit < CHUNKS + 3:
            live = settled(live)
    return unpack(live["column"], [live["returned"][m] for m in range(experts)])


def solution(mesh):
    return jax.shard_map(
        on_device,
        mesh=mesh,
        in_specs=(
            P("expert", "tensor"),
            P(),
            P("expert", None, "tensor"),
            P("expert", None, "tensor"),
            P("expert", "tensor", None),
            P("expert", None),
        ),
        out_specs=P("expert", "tensor"),
        check_vma=False,
    )
```

```python
import functools

import jax
import jax.numpy as jnp
from jax import lax
from jax.experimental import pallas as pl
from jax.experimental.pallas import tpu as pltpu
from jax.sharding import PartitionSpec as P

CHUNKS = 4
MIB = 1 << 20
HBM = pl.BlockSpec(memory_space=pl.ANY)
VMEM = pl.BlockSpec(memory_space=pltpu.VMEM)
SMEM = pl.BlockSpec(memory_space=pltpu.SMEM)


def to_expert(value, mask):
    if mask == 0:
        return value
    pairs = [(i, i ^ (2 * mask)) for i in range(lax.axis_size("expert"))]
    return lax.ppermute(value, "expert", pairs)


def to_pair(value):
    return lax.ppermute(value, "expert", [(i, i ^ 1) for i in range(lax.axis_size("expert"))])


def to_tensor(value, shift):
    size = lax.axis_size("tensor")
    return lax.ppermute(value, "tensor", [(i, (i + shift) % size) for i in range(size)])


def placing_of(column, total):
    places = lax.broadcasted_iota(jnp.int32, (column.shape[0], total), 1)
    return (column == places).astype(jnp.float32).astype(jnp.bfloat16)


def pack_kernel(experts, slots, info, routes, tokens, *outs):
    blocks, column = outs[:experts], outs[experts]
    chosen = routes[...]
    rows = chosen.shape[0]
    names = lax.broadcasted_iota(jnp.int32, (rows, experts), 1)
    onehot = (chosen == names).astype(jnp.float32)
    earlier = lax.broadcasted_iota(jnp.int32, (rows, rows), 1) < lax.broadcasted_iota(
        jnp.int32, (rows, rows), 0
    )
    counts = jnp.dot(
        earlier.astype(jnp.float32).astype(jnp.bfloat16),
        onehot.astype(jnp.bfloat16),
        preferred_element_type=jnp.float32,
    )
    ranking = jnp.sum(counts * onehot, axis=1, keepdims=True).astype(jnp.int32)
    place = (chosen ^ info[0]) * slots + ranking
    column[...] = place
    packed = lax.dot_general(
        placing_of(place, experts * slots),
        tokens[...],
        (((0,), (0,)), ((), ())),
        preferred_element_type=jnp.float32,
    ).astype(jnp.bfloat16)
    for m in range(experts):
        blocks[m][...] = packed[m * slots : (m + 1) * slots]


def pack(info, routes, tokens, experts, slots):
    rows, width = tokens.shape
    steps = 2 if width % 256 == 0 else 1
    band = width // steps
    outs = pl.pallas_call(
        functools.partial(pack_kernel, experts, slots),
        grid=(steps,),
        in_specs=[
            SMEM,
            pl.BlockSpec((rows, 1), lambda i: (0, 0)),
            pl.BlockSpec((rows, band), lambda i: (0, i)),
        ],
        out_specs=[pl.BlockSpec((slots, band), lambda i: (0, i))] * experts
        + [pl.BlockSpec((rows, 1), lambda i: (0, 0))],
        out_shape=[jax.ShapeDtypeStruct((slots, width), jnp.bfloat16)] * experts
        + [jax.ShapeDtypeStruct((rows, 1), jnp.int32)],
        compiler_params=pltpu.CompilerParams(vmem_limit_bytes=24 * MIB),
        cost_estimate=pl.CostEstimate(
            flops=2 * rows * experts * slots * width, bytes_accessed=6 * rows * width, transcendentals=0
        ),
        name="pack",
    )(info, routes, tokens)
    return outs[:experts], outs[experts]


def unpack_kernel(experts, slots, column, *refs):
    blocks, mixed = refs[:experts], refs[experts]
    ordered = jnp.concatenate([b[...] for b in blocks], axis=0)
    mixed[...] = jnp.dot(
        placing_of(column[...], experts * slots), ordered, preferred_element_type=jnp.float32
    ).astype(jnp.bfloat16)


def unpack(column, blocks):
    experts = len(blocks)
    slots, width = blocks[0].shape
    rows = column.shape[0]
    steps = 2 if width % 256 == 0 else 1
    band = width // steps
    return pl.pallas_call(
        functools.partial(unpack_kernel, experts, slots),
        grid=(steps,),
        in_specs=[pl.BlockSpec((rows, 1), lambda i: (0, 0))]
        + [pl.BlockSpec((slots, band), lambda i: (0, i))] * experts,
        out_specs=pl.BlockSpec((rows, band), lambda i: (0, i)),
        out_shape=jax.ShapeDtypeStruct((rows, width), jnp.bfloat16),
        compiler_params=pltpu.CompilerParams(vmem_limit_bytes=24 * MIB),
        cost_estimate=pl.CostEstimate(
            flops=2 * rows * experts * slots * width, bytes_accessed=6 * rows * width, transcendentals=0
        ),
        name="unpack",
    )(column, *blocks)


def expert_kernel(parts, hid_step, out_step, loading, info, *refs):
    mine, theirs, (router_t, *weights) = refs[:parts], refs[parts : 2 * parts], refs[2 * parts : 2 * parts + 4]
    kept, given = refs[2 * parts + 4 : 3 * parts + 4], refs[3 * parts + 4]
    rest = refs[3 * parts + 5 :]
    if loading:
        sources, weights, rest = weights, rest[:3], rest[3:]
    wg, wu, wd = weights
    x_all, h_all, o_buf, x_sem, o_sem, g_sem, u_sem, d_sem = rest
    half, width = mine[0].shape
    hidden = wg.shape[2]
    index, expert = info[0], info[1]
    order = list(range(1, parts)) + [0]
    steps = range(0, hidden, hid_step)

    def span(t):
        return pl.ds(pl.multiple_of(lax.rem(index + t, parts) * width, 128), width)

    x_copies, g_copies, u_copies, d_copies, o_copies = [], [], [], [], []
    for t in range(parts):
        own_rows, pair_rows = pl.ds(0, half), pl.ds(half, half)
        x_copies += [
            pltpu.make_async_copy(mine[t], x_all.at[own_rows, span(t)], x_sem.at[0, t]),
            pltpu.make_async_copy(theirs[t], x_all.at[pair_rows, span(t)], x_sem.at[1, t]),
        ]
    if loading:
        for n, j in enumerate(steps):
            cols = (0, slice(None), pl.ds(j, hid_step))
            g_copies.append(pltpu.make_async_copy(sources[0].at[cols], wg.at[cols], g_sem.at[n]))
            u_copies.append(pltpu.make_async_copy(sources[1].at[cols], wu.at[cols], u_sem.at[n]))
        for n, t in enumerate(order):
            cols = (0, slice(None), span(t))
            d_copies.append(pltpu.make_async_copy(sources[2].at[cols], wd.at[cols], d_sem.at[n]))
    loads = [copy for pair in zip(g_copies, u_copies) for copy in pair] + d_copies
    for copy in x_copies + loads:
        copy.start()
    for copy in x_copies:
        copy.wait()
    logits = lax.dot_general(
        x_all[...], router_t[...], (((1,), (1,)), ((), ())), preferred_element_type=jnp.float32
    )
    names = lax.broadcasted_iota(jnp.int32, logits.shape, 1)
    score = jnp.sum(jnp.where(names == expert, logits, 0.0), axis=1, keepdims=True)
    scale = 1.0 / (1.0 + jnp.exp(-score))
    for n, j in enumerate(steps):
        cols = slice(j, j + hid_step)
        if loading:
            g_copies[n].wait()
        gate = scale * jnp.dot(x_all[...], wg[0, :, cols], preferred_element_type=jnp.float32)
        if loading:
            u_copies[n].wait()
        up = scale * jnp.dot(x_all[...], wu[0, :, cols], preferred_element_type=jnp.float32)
        h_all[:, cols] = (gate / (1.0 + jnp.exp(-gate)) * up).astype(jnp.bfloat16)
    for n, t in enumerate(order):
        if loading:
            d_copies[n].wait()
        for c in range(0, width, out_step):
            cols = pl.ds(pl.multiple_of(lax.rem(index + t, parts) * width + c, 128), out_step)
            o_buf[t, :, c : c + out_step] = jnp.dot(
                h_all[...], wd[0, :, cols], preferred_element_type=jnp.float32
            ).astype(jnp.bfloat16)
        o_copies += [
            pltpu.make_async_copy(
                o_buf.at[t, pl.ds(half, half)], given.at[:, pl.ds(t * width, width)], o_sem.at[1, t]
            ),
            pltpu.make_async_copy(o_buf.at[t, pl.ds(0, half)], kept[t], o_sem.at[0, t]),
        ]
        o_copies[-2].start()
        o_copies[-1].start()
    for copy in o_copies:
        copy.wait()


def expert_chunk(info, mine, theirs, router_t, weights, loading):
    parts = len(mine)
    half, width = mine[0].shape
    rows, model = 2 * half, parts * width
    hidden = weights[0].shape[2]
    hid_step = min(256, hidden)
    out_step = 1280 if width % 1280 == 0 else width
    bf16 = jnp.bfloat16
    held_in, held_out = ([HBM] * 3, [VMEM] * 3) if loading else ([VMEM] * 3, [])
    place = pltpu.HBM if loading else pltpu.VMEM
    outs = pl.pallas_call(
        functools.partial(expert_kernel, parts, hid_step, out_step, loading),
        in_specs=[SMEM] + [HBM] * (2 * parts) + [VMEM] + held_in,
        out_specs=[HBM] * (parts + 1) + held_out,
        out_shape=[jax.ShapeDtypeStruct((half, width), bf16)] * parts
        + [jax.ShapeDtypeStruct((half, model), bf16)]
        + [pltpu.VMEM(w.shape, w.dtype) for w in weights if loading],
        scratch_shapes=[
            pltpu.VMEM((rows, model), bf16),
            pltpu.VMEM((rows, hidden), bf16),
            pltpu.VMEM((parts, rows, width), bf16),
            pltpu.SemaphoreType.DMA((2, parts)),
            pltpu.SemaphoreType.DMA((2, parts)),
            pltpu.SemaphoreType.DMA((hidden // hid_step,)),
            pltpu.SemaphoreType.DMA((hidden // hid_step,)),
            pltpu.SemaphoreType.DMA((parts,)),
        ],
        compiler_params=pltpu.CompilerParams(vmem_limit_bytes=16 * MIB),
        cost_estimate=pl.CostEstimate(
            flops=6 * rows * hidden * model,
            bytes_accessed=4 * rows * model,
            transcendentals=rows * hidden,
        ),
        name="expert_rows",
    )(info, *mine, *theirs, router_t, *[pltpu.with_memory_space_constraint(w, place) for w in weights])
    return outs[:parts], outs[parts], list(outs[parts + 1 :]) or weights


def settled(live):
    leaves, shape = jax.tree.flatten(live)
    return jax.tree.unflatten(shape, lax.optimization_barrier(leaves))


def f32(value):
    return value.astype(jnp.float32)


def on_device(tokens, router, gate_weight, up_weight, down_weight, routes):
    experts = router.shape[1]
    slots = 2 * tokens.shape[0] // experts
    part_cols = tokens.shape[1]
    parts = lax.axis_size("tensor")
    expert = lax.axis_index("expert") // 2
    place = jnp.stack([lax.axis_index("tensor"), expert]).astype(jnp.int32)
    router_t = router.T
    blocks, column = pack(expert.astype(jnp.int32).reshape(1), routes, tokens, experts, slots)
    masks = [list(range(c, experts, CHUNKS)) for c in range(CHUNKS)]
    live = dict(blocks=dict(enumerate(blocks)), arrived={}, returned={}, column=column)
    live["chunk"] = {}
    live = settled(live)
    weights = [gate_weight, up_weight, down_weight]
    for unit in range(CHUNKS + 4):
        before = live["chunk"]
        after_unit = {}
        c = unit
        if c < CHUNKS:
            for m in sorted(set(masks[c]) | set(range(CHUNKS if c == 0 else 0)), reverse=True):
                if m in live["blocks"]:
                    with jax.named_scope(f"dispatch_{m}"):
                        live["arrived"][m] = to_expert(live["blocks"].pop(m), m)
        c = unit - 1
        if 0 <= c < CHUNKS:
            own = jnp.concatenate([live["arrived"].pop(m) for m in masks[c]], axis=0)
            mine = [own] + [None] * (parts - 1)
            for t in range(1, parts):
                with jax.named_scope(f"features_{c}"):
                    mine[parts - t] = to_tensor(own, t)
            with jax.named_scope(f"pair_{c}"):
                after_unit[c] = dict(mine=mine, pair=to_pair(own))
        c = unit - 2
        if 0 <= c < CHUNKS:
            chunk = before[c]
            with jax.named_scope(f"pair_{c}"):
                theirs = [chunk["pair"]] + [to_pair(v) for v in chunk["mine"][1:]]
            with jax.named_scope(f"rows_{c}"):
                kept, given, weights = expert_chunk(
                    place, chunk["mine"], theirs, router_t, weights, loading=c == 0
                )
            after_unit[c] = dict(kept=kept, given=given)
        c = unit - 3
        if 0 <= c < CHUNKS:
            kept = before[c]["kept"]
            with jax.named_scope(f"partial_{c}"):
                given = to_pair(before[c]["given"])
            gathered = []
            for t in range(1, parts):
                with jax.named_scope(f"reduce_{c}"):
                    total = f32(kept[t]) + f32(given[:, t * part_cols : (t + 1) * part_cols])
                    gathered.append(to_tensor(total.astype(jnp.bfloat16), t))
            after_unit[c] = dict(kept=kept[0], given=given, gathered=gathered)
        c = unit - 4
        if 0 <= c < CHUNKS:
            chunk = before[c]
            for n, m in enumerate(masks[c]):
                rows = slice(n * slots, (n + 1) * slots)
                with jax.named_scope(f"home_{m}"):
                    total = f32(chunk["kept"][rows]) + f32(chunk["given"][rows, :part_cols])
                    for part in chunk["gathered"]:
                        total = total + f32(part[rows])
                    live["returned"][m] = to_expert(total.astype(jnp.bfloat16), m)
        live["chunk"] = after_unit
        if unit < CHUNKS + 3:
            live = settled(live)
    return unpack(live["column"], [live["returned"][m] for m in range(experts)])


def solution(mesh):
    return jax.shard_map(
        on_device,
        mesh=mesh,
        in_specs=(
            P("expert", "tensor"),
            P(),
            P("expert", None, "tensor"),
            P("expert", None, "tensor"),
            P("expert", "tensor", None),
            P("expert", None),
        ),
        out_specs=P("expert", "tensor"),
        check_vma=False,
    )
```

```python
import functools

import jax
import jax.numpy as jnp
from jax import lax
from jax.experimental import pallas as pl
from jax.experimental.pallas import tpu as pltpu
from jax.sharding import PartitionSpec as P

CHUNKS = 4
LOADS = 4
MIB = 1 << 20
HBM = pl.BlockSpec(memory_space=pl.ANY)
VMEM = pl.BlockSpec(memory_space=pltpu.VMEM)
SMEM = pl.BlockSpec(memory_space=pltpu.SMEM)


def to_expert(value, mask):
    if mask == 0:
        return value
    pairs = [(i, i ^ (2 * mask)) for i in range(lax.axis_size("expert"))]
    return lax.ppermute(value, "expert", pairs)


def to_pair(value):
    return lax.ppermute(value, "expert", [(i, i ^ 1) for i in range(lax.axis_size("expert"))])


def to_tensor(value, shift):
    size = lax.axis_size("tensor")
    return lax.ppermute(value, "tensor", [(i, (i + shift) % size) for i in range(size)])


def placing_of(column, total):
    places = lax.broadcasted_iota(jnp.int32, (column.shape[0], total), 1)
    return (column == places).astype(jnp.float32).astype(jnp.bfloat16)


def pack_kernel(experts, slots, info, routes, tokens, *outs):
    blocks, column = outs[:experts], outs[experts]
    chosen = routes[...]
    rows = chosen.shape[0]
    names = lax.broadcasted_iota(jnp.int32, (rows, experts), 1)
    onehot = (chosen == names).astype(jnp.float32)
    earlier = lax.broadcasted_iota(jnp.int32, (rows, rows), 1) < lax.broadcasted_iota(
        jnp.int32, (rows, rows), 0
    )
    counts = jnp.dot(
        earlier.astype(jnp.float32).astype(jnp.bfloat16),
        onehot.astype(jnp.bfloat16),
        preferred_element_type=jnp.float32,
    )
    ranking = jnp.sum(counts * onehot, axis=1, keepdims=True).astype(jnp.int32)
    place = (chosen ^ info[0]) * slots + ranking
    column[...] = place
    packed = lax.dot_general(
        placing_of(place, experts * slots),
        tokens[...],
        (((0,), (0,)), ((), ())),
        preferred_element_type=jnp.float32,
    ).astype(jnp.bfloat16)
    for m in range(experts):
        blocks[m][...] = packed[m * slots : (m + 1) * slots]


def pack(info, routes, tokens, experts, slots):
    rows, width = tokens.shape
    steps = 2 if width % 256 == 0 else 1
    band = width // steps
    outs = pl.pallas_call(
        functools.partial(pack_kernel, experts, slots),
        grid=(steps,),
        in_specs=[
            SMEM,
            pl.BlockSpec((rows, 1), lambda i: (0, 0)),
            pl.BlockSpec((rows, band), lambda i: (0, i)),
        ],
        out_specs=[pl.BlockSpec((slots, band), lambda i: (0, i))] * experts
        + [pl.BlockSpec((rows, 1), lambda i: (0, 0))],
        out_shape=[jax.ShapeDtypeStruct((slots, width), jnp.bfloat16)] * experts
        + [jax.ShapeDtypeStruct((rows, 1), jnp.int32)],
        compiler_params=pltpu.CompilerParams(vmem_limit_bytes=24 * MIB),
        cost_estimate=pl.CostEstimate(
            flops=2 * rows * experts * slots * width, bytes_accessed=6 * rows * width, transcendentals=0
        ),
        name="pack",
    )(info, routes, tokens)
    return outs[:experts], outs[experts]


def unpack_kernel(experts, slots, column, *refs):
    blocks, mixed = refs[:experts], refs[experts]
    ordered = jnp.concatenate([b[...] for b in blocks], axis=0)
    mixed[...] = jnp.dot(
        placing_of(column[...], experts * slots), ordered, preferred_element_type=jnp.float32
    ).astype(jnp.bfloat16)


def unpack(column, blocks):
    experts = len(blocks)
    slots, width = blocks[0].shape
    rows = column.shape[0]
    steps = 2 if width % 256 == 0 else 1
    band = width // steps
    return pl.pallas_call(
        functools.partial(unpack_kernel, experts, slots),
        grid=(steps,),
        in_specs=[pl.BlockSpec((rows, 1), lambda i: (0, 0))]
        + [pl.BlockSpec((slots, band), lambda i: (0, i))] * experts,
        out_specs=pl.BlockSpec((rows, band), lambda i: (0, i)),
        out_shape=jax.ShapeDtypeStruct((rows, width), jnp.bfloat16),
        compiler_params=pltpu.CompilerParams(vmem_limit_bytes=24 * MIB),
        cost_estimate=pl.CostEstimate(
            flops=2 * rows * experts * slots * width, bytes_accessed=6 * rows * width, transcendentals=0
        ),
        name="unpack",
    )(column, *blocks)


def expert_kernel(parts, hid_step, out_step, loading, info, *refs):
    mine, theirs, (router_t, *weights) = refs[:parts], refs[parts : 2 * parts], refs[2 * parts : 2 * parts + 4]
    kept, given = refs[2 * parts + 4 : 3 * parts + 4], refs[3 * parts + 4]
    rest = refs[3 * parts + 5 :]
    if loading:
        sources, weights, rest = weights, rest[:3], rest[3:]
    wg, wu, wd = weights
    x_all, h_all, o_buf, x_sem, o_sem, *rest = rest
    if loading:
        proj, g_sem, u_sem, d_sem = rest
    half, width = mine[0].shape
    hidden = wg.shape[2]
    index, expert = info[0], info[1]
    order = list(range(1, parts)) + [0]
    steps = range(0, hidden, hid_step)

    def span(t):
        return pl.ds(pl.multiple_of(lax.rem(index + t, parts) * width, 128), width)

    x_copies, g_copies, u_copies, d_copies, o_copies = [], [], [], [], []
    for t in range(parts):
        own_rows, pair_rows = pl.ds(0, half), pl.ds(half, half)
        x_copies += [
            pltpu.make_async_copy(mine[t], x_all.at[own_rows, span(t)], x_sem.at[0, t]),
            pltpu.make_async_copy(theirs[t], x_all.at[pair_rows, span(t)], x_sem.at[1, t]),
        ]
    if loading:
        band = wg.shape[1] // LOADS
        for n in range(LOADS):
            part = (0, pl.ds(n * band, band))
            g_copies.append(pltpu.make_async_copy(sources[0].at[part], wg.at[part], g_sem.at[n]))
            u_copies.append(pltpu.make_async_copy(sources[1].at[part], wu.at[part], u_sem.at[n]))
            part = (0, pl.ds(n * (hidden // LOADS), hidden // LOADS))
            d_copies.append(pltpu.make_async_copy(sources[2].at[part], wd.at[part], d_sem.at[n]))
    loads = [copy for pair in zip(g_copies, u_copies) for copy in pair] + d_copies
    for copy in x_copies + loads:
        copy.start()
    for copy in x_copies:
        copy.wait()
    logits = lax.dot_general(
        x_all[...], router_t[...], (((1,), (1,)), ((), ())), preferred_element_type=jnp.float32
    )
    names = lax.broadcasted_iota(jnp.int32, logits.shape, 1)
    score = jnp.sum(jnp.where(names == expert, logits, 0.0), axis=1, keepdims=True)
    scale = 1.0 / (1.0 + jnp.exp(-score))
    if loading:
        for n in range(LOADS):
            part = slice(n * band, (n + 1) * band)
            for i, (copies, w) in enumerate(((g_copies, wg), (u_copies, wu))):
                copies[n].wait()
                term = jnp.dot(x_all[:, part], w[0, part, :], preferred_element_type=jnp.float32)
                proj[i] = term if n == 0 else proj[i] + term
    for j in steps:
        cols = slice(j, j + hid_step)
        if loading:
            gate, up = proj[0, :, cols], proj[1, :, cols]
        else:
            gate = jnp.dot(x_all[...], wg[0, :, cols], preferred_element_type=jnp.float32)
            up = jnp.dot(x_all[...], wu[0, :, cols], preferred_element_type=jnp.float32)
        gate, up = scale * gate, scale * up
        h_all[:, cols] = (gate / (1.0 + jnp.exp(-gate)) * up).astype(jnp.bfloat16)
    for copy in d_copies:
        copy.wait()
    for t in order:
        for c in range(0, width, out_step):
            cols = pl.ds(pl.multiple_of(lax.rem(index + t, parts) * width + c, 128), out_step)
            o_buf[t, :, c : c + out_step] = jnp.dot(
                h_all[...], wd[0, :, cols], preferred_element_type=jnp.float32
            ).astype(jnp.bfloat16)
        o_copies += [
            pltpu.make_async_copy(
                o_buf.at[t, pl.ds(half, half)], given.at[:, pl.ds(t * width, width)], o_sem.at[1, t]
            ),
            pltpu.make_async_copy(o_buf.at[t, pl.ds(0, half)], kept[t], o_sem.at[0, t]),
        ]
        o_copies[-2].start()
        o_copies[-1].start()
    for copy in o_copies:
        copy.wait()


def expert_chunk(info, mine, theirs, router_t, weights, loading):
    parts = len(mine)
    half, width = mine[0].shape
    rows, model = 2 * half, parts * width
    hidden = weights[0].shape[2]
    hid_step = min(256, hidden)
    out_step = 1280 if width % 1280 == 0 else width
    bf16 = jnp.bfloat16
    held_in, held_out = ([HBM] * 3, [VMEM] * 3) if loading else ([VMEM] * 3, [])
    load_scratch = [pltpu.VMEM((2, rows, hidden), jnp.float32)] + [pltpu.SemaphoreType.DMA((LOADS,))] * 3
    load_scratch = load_scratch if loading else []
    place = pltpu.HBM if loading else pltpu.VMEM
    outs = pl.pallas_call(
        functools.partial(expert_kernel, parts, hid_step, out_step, loading),
        in_specs=[SMEM] + [HBM] * (2 * parts) + [VMEM] + held_in,
        out_specs=[HBM] * (parts + 1) + held_out,
        out_shape=[jax.ShapeDtypeStruct((half, width), bf16)] * parts
        + [jax.ShapeDtypeStruct((half, model), bf16)]
        + [pltpu.VMEM(w.shape, w.dtype) for w in weights if loading],
        scratch_shapes=[
            pltpu.VMEM((rows, model), bf16),
            pltpu.VMEM((rows, hidden), bf16),
            pltpu.VMEM((parts, rows, width), bf16),
            pltpu.SemaphoreType.DMA((2, parts)),
            pltpu.SemaphoreType.DMA((2, parts)),
        ]
        + load_scratch,
        compiler_params=pltpu.CompilerParams(vmem_limit_bytes=16 * MIB),
        cost_estimate=pl.CostEstimate(
            flops=6 * rows * hidden * model,
            bytes_accessed=4 * rows * model,
            transcendentals=rows * hidden,
        ),
        name="expert_rows",
    )(info, *mine, *theirs, router_t, *[pltpu.with_memory_space_constraint(w, place) for w in weights])
    return outs[:parts], outs[parts], list(outs[parts + 1 :]) or weights


def settled(live):
    leaves, shape = jax.tree.flatten(live)
    return jax.tree.unflatten(shape, lax.optimization_barrier(leaves))


def f32(value):
    return value.astype(jnp.float32)


def on_device(tokens, router, gate_weight, up_weight, down_weight, routes):
    experts = router.shape[1]
    slots = 2 * tokens.shape[0] // experts
    part_cols = tokens.shape[1]
    parts = lax.axis_size("tensor")
    expert = lax.axis_index("expert") // 2
    place = jnp.stack([lax.axis_index("tensor"), expert]).astype(jnp.int32)
    router_t = router.T
    blocks, column = pack(expert.astype(jnp.int32).reshape(1), routes, tokens, experts, slots)
    masks = [list(range(c, experts, CHUNKS)) for c in range(CHUNKS)]
    live = dict(blocks=dict(enumerate(blocks)), arrived={}, returned={}, column=column)
    live["chunk"] = {}
    live = settled(live)
    weights = [gate_weight, up_weight, down_weight]
    for unit in range(CHUNKS + 4):
        before = live["chunk"]
        after_unit = {}
        c = unit
        if c < CHUNKS:
            for m in masks[c][1:] + masks[min(c + 1, CHUNKS - 1)][:1] + ([0] if c == 0 else []):
                if m in live["blocks"]:
                    with jax.named_scope(f"dispatch_{m}"):
                        live["arrived"][m] = to_expert(live["blocks"].pop(m), m)
        c = unit - 1
        if 0 <= c < CHUNKS:
            own = jnp.concatenate([live["arrived"].pop(m) for m in masks[c]], axis=0)
            mine = [own] + [None] * (parts - 1)
            for t in range(1, parts):
                with jax.named_scope(f"features_{c}"):
                    mine[parts - t] = to_tensor(own, t)
            with jax.named_scope(f"pair_{c}"):
                after_unit[c] = dict(mine=mine, pair=to_pair(own))
        c = unit - 2
        if 0 <= c < CHUNKS:
            chunk = before[c]
            with jax.named_scope(f"pair_{c}"):
                theirs = [chunk["pair"]] + [to_pair(v) for v in chunk["mine"][1:]]
            with jax.named_scope(f"rows_{c}"):
                kept, given, weights = expert_chunk(
                    place, chunk["mine"], theirs, router_t, weights, loading=c == 0
                )
            after_unit[c] = dict(kept=kept, given=given)
        c = unit - 3
        if 0 <= c < CHUNKS:
            kept = before[c]["kept"]
            with jax.named_scope(f"partial_{c}"):
                given = to_pair(before[c]["given"])
            gathered = []
            for t in range(1, parts):
                with jax.named_scope(f"reduce_{c}"):
                    total = f32(kept[t]) + f32(given[:, t * part_cols : (t + 1) * part_cols])
                    gathered.append(to_tensor(total.astype(jnp.bfloat16), t))
            after_unit[c] = dict(kept=kept[0], given=given, gathered=gathered)
        c = unit - 4
        if 0 <= c < CHUNKS:
            chunk = before[c]
            for n, m in enumerate(masks[c]):
                rows = slice(n * slots, (n + 1) * slots)
                with jax.named_scope(f"home_{m}"):
                    total = f32(chunk["kept"][rows]) + f32(chunk["given"][rows, :part_cols])
                    for part in chunk["gathered"]:
                        total = total + f32(part[rows])
                    live["returned"][m] = to_expert(total.astype(jnp.bfloat16), m)
        live["chunk"] = after_unit
        if unit < CHUNKS + 3:
            live = settled(live)
    return unpack(live["column"], [live["returned"][m] for m in range(experts)])


def solution(mesh):
    return jax.shard_map(
        on_device,
        mesh=mesh,
        in_specs=(
            P("expert", "tensor"),
            P(),
            P("expert", None, "tensor"),
            P("expert", None, "tensor"),
            P("expert", "tensor", None),
            P("expert", None),
        ),
        out_specs=P("expert", "tensor"),
        check_vma=False,
    )
```

```python
import functools

import jax
import jax.numpy as jnp
from jax import lax
from jax.experimental import pallas as pl
from jax.experimental.pallas import tpu as pltpu
from jax.sharding import PartitionSpec as P

CHUNKS = 4
LOADS = 4
PIECES = 2
MIB = 1 << 20
HBM = pl.BlockSpec(memory_space=pl.ANY)
VMEM = pl.BlockSpec(memory_space=pltpu.VMEM)
SMEM = pl.BlockSpec(memory_space=pltpu.SMEM)


def to_expert(value, mask):
    if mask == 0:
        return value
    pairs = [(i, i ^ (2 * mask)) for i in range(lax.axis_size("expert"))]
    return lax.ppermute(value, "expert", pairs)


def to_pair(value):
    return lax.ppermute(value, "expert", [(i, i ^ 1) for i in range(lax.axis_size("expert"))])


def to_tensor(value, shift):
    size = lax.axis_size("tensor")
    return lax.ppermute(value, "tensor", [(i, (i + shift) % size) for i in range(size)])


def placing_of(column, total):
    places = lax.broadcasted_iota(jnp.int32, (column.shape[0], total), 1)
    return (column == places).astype(jnp.float32).astype(jnp.bfloat16)


def pack_kernel(experts, slots, info, routes, tokens, *outs):
    blocks, column = outs[:experts], outs[experts]
    chosen = routes[...]
    rows = chosen.shape[0]
    names = lax.broadcasted_iota(jnp.int32, (rows, experts), 1)
    onehot = (chosen == names).astype(jnp.float32)
    earlier = lax.broadcasted_iota(jnp.int32, (rows, rows), 1) < lax.broadcasted_iota(
        jnp.int32, (rows, rows), 0
    )
    counts = jnp.dot(
        earlier.astype(jnp.float32).astype(jnp.bfloat16),
        onehot.astype(jnp.bfloat16),
        preferred_element_type=jnp.float32,
    )
    ranking = jnp.sum(counts * onehot, axis=1, keepdims=True).astype(jnp.int32)
    place = (chosen ^ info[0]) * slots + ranking
    column[...] = place
    packed = lax.dot_general(
        placing_of(place, experts * slots),
        tokens[...],
        (((0,), (0,)), ((), ())),
        preferred_element_type=jnp.float32,
    ).astype(jnp.bfloat16)
    for m in range(experts):
        blocks[m][...] = packed[m * slots : (m + 1) * slots]


def pack(info, routes, tokens, experts, slots):
    rows, width = tokens.shape
    steps = 2 if width % 256 == 0 else 1
    band = width // steps
    outs = pl.pallas_call(
        functools.partial(pack_kernel, experts, slots),
        grid=(steps,),
        in_specs=[
            SMEM,
            pl.BlockSpec((rows, 1), lambda i: (0, 0)),
            pl.BlockSpec((rows, band), lambda i: (0, i)),
        ],
        out_specs=[pl.BlockSpec((slots, band), lambda i: (0, i))] * experts
        + [pl.BlockSpec((rows, 1), lambda i: (0, 0))],
        out_shape=[jax.ShapeDtypeStruct((slots, width), jnp.bfloat16)] * experts
        + [jax.ShapeDtypeStruct((rows, 1), jnp.int32)],
        compiler_params=pltpu.CompilerParams(vmem_limit_bytes=24 * MIB),
        cost_estimate=pl.CostEstimate(
            flops=2 * rows * experts * slots * width, bytes_accessed=6 * rows * width, transcendentals=0
        ),
        name="pack",
    )(info, routes, tokens)
    return outs[:experts], outs[experts]


def unpack_kernel(experts, slots, column, *refs):
    blocks, mixed = refs[:experts], refs[experts]
    ordered = jnp.concatenate([b[...] for b in blocks], axis=0)
    mixed[...] = jnp.dot(
        placing_of(column[...], experts * slots), ordered, preferred_element_type=jnp.float32
    ).astype(jnp.bfloat16)


def unpack(column, blocks):
    experts = len(blocks)
    slots, width = blocks[0].shape
    rows = column.shape[0]
    steps = 2 if width % 256 == 0 else 1
    band = width // steps
    return pl.pallas_call(
        functools.partial(unpack_kernel, experts, slots),
        grid=(steps,),
        in_specs=[pl.BlockSpec((rows, 1), lambda i: (0, 0))]
        + [pl.BlockSpec((slots, band), lambda i: (0, i))] * experts,
        out_specs=pl.BlockSpec((rows, band), lambda i: (0, i)),
        out_shape=jax.ShapeDtypeStruct((rows, width), jnp.bfloat16),
        compiler_params=pltpu.CompilerParams(vmem_limit_bytes=24 * MIB),
        cost_estimate=pl.CostEstimate(
            flops=2 * rows * experts * slots * width, bytes_accessed=6 * rows * width, transcendentals=0
        ),
        name="unpack",
    )(column, *blocks)


def expert_kernel(parts, hid_step, out_step, loading, info, *refs):
    mine, theirs, (router_t, *weights) = refs[:parts], refs[parts : 2 * parts], refs[2 * parts : 2 * parts + 4]
    kept, rest = refs[2 * parts + 4 : 3 * parts + 4], refs[3 * parts + 4 :]
    given, rest = rest[: 1 + PIECES * (parts - 1)], rest[1 + PIECES * (parts - 1) :]
    if loading:
        sources, weights, rest = weights, rest[:3], rest[3:]
    wg, wu, wd = weights
    x_all, h_all, o_buf, x_sem, o_sem, *rest = rest
    if loading:
        proj, g_sem, u_sem, d_sem = rest
    half, width = mine[0].shape
    hidden = wg.shape[2]
    index, expert = info[0], info[1]
    order = list(range(1, parts)) + [0]
    steps = range(0, hidden, hid_step)

    def span(t):
        return pl.ds(pl.multiple_of(lax.rem(index + t, parts) * width, 128), width)

    x_copies, g_copies, u_copies, d_copies, o_copies = [], [], [], [], []
    for t in range(parts):
        own_rows, pair_rows = pl.ds(0, half), pl.ds(half, half)
        x_copies += [
            pltpu.make_async_copy(mine[t], x_all.at[own_rows, span(t)], x_sem.at[0, t]),
            pltpu.make_async_copy(theirs[t], x_all.at[pair_rows, span(t)], x_sem.at[1, t]),
        ]
    if loading:
        band = wg.shape[1] // LOADS
        for n in range(LOADS):
            part = (0, pl.ds(n * band, band))
            g_copies.append(pltpu.make_async_copy(sources[0].at[part], wg.at[part], g_sem.at[n]))
            u_copies.append(pltpu.make_async_copy(sources[1].at[part], wu.at[part], u_sem.at[n]))
            part = (0, pl.ds(n * (hidden // LOADS), hidden // LOADS))
            d_copies.append(pltpu.make_async_copy(sources[2].at[part], wd.at[part], d_sem.at[n]))
    loads = [copy for pair in zip(g_copies, u_copies) for copy in pair] + d_copies
    for copy in x_copies + loads:
        copy.start()
    for copy in x_copies:
        copy.wait()
    logits = lax.dot_general(
        x_all[...], router_t[...], (((1,), (1,)), ((), ())), preferred_element_type=jnp.float32
    )
    names = lax.broadcasted_iota(jnp.int32, logits.shape, 1)
    score = jnp.sum(jnp.where(names == expert, logits, 0.0), axis=1, keepdims=True)
    scale = 1.0 / (1.0 + jnp.exp(-score))
    if loading:
        for n in range(LOADS):
            part = slice(n * band, (n + 1) * band)
            for i, (copies, w) in enumerate(((g_copies, wg), (u_copies, wu))):
                copies[n].wait()
                term = jnp.dot(x_all[:, part], w[0, part, :], preferred_element_type=jnp.float32)
                proj[i] = term if n == 0 else proj[i] + term
    for j in steps:
        cols = slice(j, j + hid_step)
        if loading:
            gate, up = proj[0, :, cols], proj[1, :, cols]
        else:
            gate = jnp.dot(x_all[...], wg[0, :, cols], preferred_element_type=jnp.float32)
            up = jnp.dot(x_all[...], wu[0, :, cols], preferred_element_type=jnp.float32)
        gate, up = scale * gate, scale * up
        h_all[:, cols] = (gate / (1.0 + jnp.exp(-gate)) * up).astype(jnp.bfloat16)
    for copy in d_copies:
        copy.wait()
    for t in order:
        for c in range(0, width, out_step):
            cols = pl.ds(pl.multiple_of(lax.rem(index + t, parts) * width + c, 128), out_step)
            o_buf[t, :, c : c + out_step] = jnp.dot(
                h_all[...], wd[0, :, cols], preferred_element_type=jnp.float32
            ).astype(jnp.bfloat16)
        pieces = given[:1] if t == 0 else given[1 + PIECES * (t - 1) :][:PIECES]
        extent = half // len(pieces)
        targets = [(half + n * extent, extent, piece) for n, piece in enumerate(pieces)]
        for n, (start, extent, target) in enumerate([(0, half, kept[t]), *targets]):
            source = o_buf.at[t, pl.ds(start, extent)]
            o_copies.append(pltpu.make_async_copy(source, target, o_sem.at[n, t]))
            o_copies[-1].start()
    for copy in o_copies:
        copy.wait()


def expert_chunk(info, mine, theirs, router_t, weights, loading):
    parts = len(mine)
    half, width = mine[0].shape
    rows, model = 2 * half, parts * width
    hidden = weights[0].shape[2]
    hid_step = min(256, hidden)
    out_step = 1280 if width % 1280 == 0 else width
    bf16 = jnp.bfloat16
    held_in, held_out = ([HBM] * 3, [VMEM] * 3) if loading else ([VMEM] * 3, [])
    load_scratch = [pltpu.VMEM((2, rows, hidden), jnp.float32)] + [pltpu.SemaphoreType.DMA((LOADS,))] * 3
    load_scratch = load_scratch if loading else []
    place = pltpu.HBM if loading else pltpu.VMEM
    outs = pl.pallas_call(
        functools.partial(expert_kernel, parts, hid_step, out_step, loading),
        in_specs=[SMEM] + [HBM] * (2 * parts) + [VMEM] + held_in,
        out_specs=[HBM] * (parts + 1 + PIECES * (parts - 1)) + held_out,
        out_shape=[jax.ShapeDtypeStruct((half, width), bf16)] * (parts + 1)
        + [jax.ShapeDtypeStruct((half // PIECES, width), bf16)] * (PIECES * (parts - 1))
        + [pltpu.VMEM(w.shape, w.dtype) for w in weights if loading],
        scratch_shapes=[
            pltpu.VMEM((rows, model), bf16),
            pltpu.VMEM((rows, hidden), bf16),
            pltpu.VMEM((parts, rows, width), bf16),
            pltpu.SemaphoreType.DMA((2, parts)),
            pltpu.SemaphoreType.DMA((1 + PIECES, parts)),
        ]
        + load_scratch,
        compiler_params=pltpu.CompilerParams(vmem_limit_bytes=16 * MIB),
        cost_estimate=pl.CostEstimate(
            flops=6 * rows * hidden * model,
            bytes_accessed=4 * rows * model,
            transcendentals=rows * hidden,
        ),
        name="expert_rows",
    )(info, *mine, *theirs, router_t, *[pltpu.with_memory_space_constraint(w, place) for w in weights])
    kept, stay, rest = outs[:parts], outs[parts], outs[parts + 1 :]
    given = [stay] + [rest[PIECES * t : PIECES * (t + 1)] for t in range(parts - 1)]
    return kept, given, list(rest[PIECES * (parts - 1) :]) or weights


def settled(live):
    leaves, shape = jax.tree.flatten(live)
    return jax.tree.unflatten(shape, lax.optimization_barrier(leaves))


def after(value, *earlier):
    return lax.optimization_barrier((value, *earlier))[0]


def f32(value):
    return value.astype(jnp.float32)


def piece_rows(pieces, rows):
    extent = pieces[0].shape[0]
    n = rows.start // extent
    return pieces[n][rows.start - n * extent : rows.stop - n * extent]


def on_device(tokens, router, gate_weight, up_weight, down_weight, routes):
    experts = router.shape[1]
    slots = 2 * tokens.shape[0] // experts
    part_cols = tokens.shape[1]
    parts = lax.axis_size("tensor")
    expert = lax.axis_index("expert") // 2
    place = jnp.stack([lax.axis_index("tensor"), expert]).astype(jnp.int32)
    router_t = router.T
    blocks, column = pack(expert.astype(jnp.int32).reshape(1), routes, tokens, experts, slots)
    masks = [list(range(c, experts, CHUNKS)) for c in range(CHUNKS)]
    live = dict(blocks=dict(enumerate(blocks)), arrived={}, returned={}, column=column)
    live["chunk"] = {}
    live = settled(live)
    weights = [gate_weight, up_weight, down_weight]
    for unit in range(CHUNKS + 4):
        before, chunks = live["chunk"], {}
        landed, crossed = [], []
        c = unit
        if c < CHUNKS:
            for m in masks[c][1:] + masks[min(c + 1, CHUNKS - 1)][:1] + ([0] if c == 0 else []):
                if m in live["blocks"]:
                    with jax.named_scope(f"dispatch_{m}"):
                        live["arrived"][m] = to_expert(live["blocks"].pop(m), m)
                        landed.append(live["arrived"][m])
        c = unit - 4
        if 0 <= c < CHUNKS:
            chunk = before[c]
            for n, m in reversed(list(enumerate(masks[c]))):
                rows = slice(n * slots, (n + 1) * slots)
                with jax.named_scope(f"home_{m}"):
                    total = f32(chunk["kept"][rows]) + f32(chunk["given"][rows])
                    for pieces in chunk["gathered"]:
                        total = total + f32(piece_rows(pieces, rows))
                    live["returned"][m] = to_expert(total.astype(jnp.bfloat16), m)
                    landed.append(live["returned"][m])
        c = unit - 1
        if 0 <= c < CHUNKS:
            own = jnp.concatenate([live["arrived"].pop(m) for m in masks[c]], axis=0)
            mine = [own] + [None] * (parts - 1)
            with jax.named_scope(f"features_{c}"):
                for t in range(1, parts):
                    mine[parts - t] = to_tensor(own, t)
            with jax.named_scope(f"pair_{c}"):
                chunks[c] = dict(mine=mine, pair=to_pair(own))
            crossed += mine[1:]
        c = unit - 3
        if 0 <= c < CHUNKS:
            chunk = before[c]
            gathered = []
            with jax.named_scope(f"reduce_{c}"):
                for t, v in enumerate(chunk["sums"], start=1):
                    if c < CHUNKS - 1:
                        gathered.append([to_tensor(v, t)])
                    else:
                        half = v.shape[0] // 2
                        tail = to_tensor(v[half:], t)
                        gathered.append([to_tensor(after(v[:half], tail), t), tail])
            crossed += [pieces[0] for pieces in gathered]
            with jax.named_scope(f"partial_{c}"):
                given = to_pair(chunk["given"])
            chunks[c] = dict(kept=chunk["kept"], given=given, gathered=gathered)
        c = unit - 2
        if 0 <= c < CHUNKS:
            chunk = before[c]
            with jax.named_scope(f"pair_{c}"):
                theirs = [chunk["pair"]] + [to_pair(v) for v in chunk["mine"][1:]]
            with jax.named_scope(f"rows_{c}"):
                kept, given, weights = expert_chunk(
                    place, chunk["mine"], theirs, router_t, weights, loading=c == 0
                )
            with jax.named_scope(f"partial_{c}"):
                sums = []
                for t in range(1, parts):
                    other = [after(to_pair(after(v, *landed)), *crossed) for v in given[t]]
                    total = f32(kept[t]) + f32(jnp.concatenate(other))
                    sums.append(total.astype(jnp.bfloat16))
            chunks[c] = dict(kept=kept[0], given=given[0], sums=sums)
        live["chunk"] = chunks
        if unit < CHUNKS + 2:
            live = settled(live)
    return unpack(live["column"], [live["returned"][m] for m in range(experts)])


def solution(mesh):
    return jax.shard_map(
        on_device,
        mesh=mesh,
        in_specs=(
            P("expert", "tensor"),
            P(),
            P("expert", None, "tensor"),
            P("expert", None, "tensor"),
            P("expert", "tensor", None),
            P("expert", None),
        ),
        out_specs=P("expert", "tensor"),
        check_vma=False,
    )
```

```python
import functools

import jax
import jax.numpy as jnp
from jax import lax
from jax.experimental import pallas as pl
from jax.experimental.pallas import tpu as pltpu
from jax.sharding import PartitionSpec as P

CHUNKS = 4
LOADS = 4
PIECES = 2
MIB = 1 << 20
HBM = pl.BlockSpec(memory_space=pl.ANY)
VMEM = pl.BlockSpec(memory_space=pltpu.VMEM)
SMEM = pl.BlockSpec(memory_space=pltpu.SMEM)


def to_expert(value, mask):
    if mask == 0:
        return value
    pairs = [(i, i ^ (2 * mask)) for i in range(lax.axis_size("expert"))]
    return lax.ppermute(value, "expert", pairs)


def to_pair(value):
    return lax.ppermute(value, "expert", [(i, i ^ 1) for i in range(lax.axis_size("expert"))])


def to_tensor(value, shift):
    size = lax.axis_size("tensor")
    return lax.ppermute(value, "tensor", [(i, (i + shift) % size) for i in range(size)])


def placing_of(column, total):
    places = lax.broadcasted_iota(jnp.int32, (column.shape[0], total), 1)
    return (column == places).astype(jnp.float32).astype(jnp.bfloat16)


def pack_kernel(experts, slots, info, routes, tokens, *outs):
    blocks, column = outs[:experts], outs[experts]
    chosen = routes[...]
    rows = chosen.shape[0]
    names = lax.broadcasted_iota(jnp.int32, (rows, experts), 1)
    onehot = (chosen == names).astype(jnp.float32)
    earlier = lax.broadcasted_iota(jnp.int32, (rows, rows), 1) < lax.broadcasted_iota(
        jnp.int32, (rows, rows), 0
    )
    counts = jnp.dot(
        earlier.astype(jnp.float32).astype(jnp.bfloat16),
        onehot.astype(jnp.bfloat16),
        preferred_element_type=jnp.float32,
    )
    ranking = jnp.sum(counts * onehot, axis=1, keepdims=True).astype(jnp.int32)
    place = (chosen ^ info[0]) * slots + ranking
    column[...] = place
    packed = lax.dot_general(
        placing_of(place, experts * slots),
        tokens[...],
        (((0,), (0,)), ((), ())),
        preferred_element_type=jnp.float32,
    ).astype(jnp.bfloat16)
    for m in range(experts):
        blocks[m][...] = packed[m * slots : (m + 1) * slots]


def pack(info, routes, tokens, experts, slots):
    rows, width = tokens.shape
    steps = 2 if width % 256 == 0 else 1
    band = width // steps
    outs = pl.pallas_call(
        functools.partial(pack_kernel, experts, slots),
        grid=(steps,),
        in_specs=[
            SMEM,
            pl.BlockSpec((rows, 1), lambda i: (0, 0)),
            pl.BlockSpec((rows, band), lambda i: (0, i)),
        ],
        out_specs=[pl.BlockSpec((slots, band), lambda i: (0, i))] * experts
        + [pl.BlockSpec((rows, 1), lambda i: (0, 0))],
        out_shape=[jax.ShapeDtypeStruct((slots, width), jnp.bfloat16)] * experts
        + [jax.ShapeDtypeStruct((rows, 1), jnp.int32)],
        compiler_params=pltpu.CompilerParams(vmem_limit_bytes=24 * MIB),
        cost_estimate=pl.CostEstimate(
            flops=2 * rows * experts * slots * width, bytes_accessed=6 * rows * width, transcendentals=0
        ),
        name="pack",
    )(info, routes, tokens)
    return outs[:experts], outs[experts]


def unpack_kernel(experts, slots, column, *refs):
    blocks, mixed = refs[:experts], refs[experts]
    ordered = jnp.concatenate([b[...] for b in blocks], axis=0)
    mixed[...] = jnp.dot(
        placing_of(column[...], experts * slots), ordered, preferred_element_type=jnp.float32
    ).astype(jnp.bfloat16)


def unpack(column, blocks):
    experts = len(blocks)
    slots, width = blocks[0].shape
    rows = column.shape[0]
    steps = 2 if width % 256 == 0 else 1
    band = width // steps
    return pl.pallas_call(
        functools.partial(unpack_kernel, experts, slots),
        grid=(steps,),
        in_specs=[pl.BlockSpec((rows, 1), lambda i: (0, 0))]
        + [pl.BlockSpec((slots, band), lambda i: (0, i))] * experts,
        out_specs=pl.BlockSpec((rows, band), lambda i: (0, i)),
        out_shape=jax.ShapeDtypeStruct((rows, width), jnp.bfloat16),
        compiler_params=pltpu.CompilerParams(vmem_limit_bytes=24 * MIB),
        cost_estimate=pl.CostEstimate(
            flops=2 * rows * experts * slots * width, bytes_accessed=6 * rows * width, transcendentals=0
        ),
        name="unpack",
    )(column, *blocks)


def expert_kernel(parts, hid_step, out_step, loading, info, *refs):
    mine, theirs, (router_t, *weights) = refs[:parts], refs[parts : 2 * parts], refs[2 * parts : 2 * parts + 4]
    kept, rest = refs[2 * parts + 4 : 3 * parts + 4], refs[3 * parts + 4 :]
    given, rest = rest[: 1 + PIECES * (parts - 1)], rest[1 + PIECES * (parts - 1) :]
    if loading:
        sources, weights, rest = weights, rest[:3], rest[3:]
    wg, wu, wd = weights
    x_all, h_all, o_buf, x_sem, o_sem, *rest = rest
    if loading:
        proj, g_sem, u_sem, d_sem = rest
    half, width = mine[0].shape
    hidden = wg.shape[2]
    index, expert = info[0], info[1]
    order = list(range(1, parts)) + [0]
    steps = range(0, hidden, hid_step)

    def span(t):
        return pl.ds(pl.multiple_of(lax.rem(index + t, parts) * width, 128), width)

    x_copies, g_copies, u_copies, d_copies, o_copies = [], [], [], [], []
    for t in range(parts):
        own_rows, pair_rows = pl.ds(0, half), pl.ds(half, half)
        x_copies += [
            pltpu.make_async_copy(mine[t], x_all.at[own_rows, span(t)], x_sem.at[0, t]),
            pltpu.make_async_copy(theirs[t], x_all.at[pair_rows, span(t)], x_sem.at[1, t]),
        ]
    if loading:
        band = wg.shape[1] // LOADS
        for n in range(LOADS):
            part = (0, pl.ds(n * band, band))
            g_copies.append(pltpu.make_async_copy(sources[0].at[part], wg.at[part], g_sem.at[n]))
            u_copies.append(pltpu.make_async_copy(sources[1].at[part], wu.at[part], u_sem.at[n]))
            part = (0, pl.ds(n * (hidden // LOADS), hidden // LOADS))
            d_copies.append(pltpu.make_async_copy(sources[2].at[part], wd.at[part], d_sem.at[n]))
    loads = [copy for pair in zip(g_copies, u_copies) for copy in pair] + d_copies
    for copy in x_copies + loads:
        copy.start()
    for copy in x_copies:
        copy.wait()
    logits = lax.dot_general(
        x_all[...], router_t[...], (((1,), (1,)), ((), ())), preferred_element_type=jnp.float32
    )
    names = lax.broadcasted_iota(jnp.int32, logits.shape, 1)
    score = jnp.sum(jnp.where(names == expert, logits, 0.0), axis=1, keepdims=True)
    scale = 1.0 / (1.0 + jnp.exp(-score))
    if loading:
        for n in range(LOADS):
            part = slice(n * band, (n + 1) * band)
            for i, (copies, w) in enumerate(((g_copies, wg), (u_copies, wu))):
                copies[n].wait()
                term = jnp.dot(x_all[:, part], w[0, part, :], preferred_element_type=jnp.float32)
                proj[i] = term if n == 0 else proj[i] + term
    for j in steps:
        cols = slice(j, j + hid_step)
        if loading:
            gate, up = proj[0, :, cols], proj[1, :, cols]
        else:
            gate = jnp.dot(x_all[...], wg[0, :, cols], preferred_element_type=jnp.float32)
            up = jnp.dot(x_all[...], wu[0, :, cols], preferred_element_type=jnp.float32)
        gate, up = scale * gate, scale * up
        h_all[:, cols] = (gate / (1.0 + jnp.exp(-gate)) * up).astype(jnp.bfloat16)
    for copy in d_copies:
        copy.wait()
    for t in order:
        for c in range(0, width, out_step):
            cols = pl.ds(pl.multiple_of(lax.rem(index + t, parts) * width + c, 128), out_step)
            o_buf[t, :, c : c + out_step] = jnp.dot(
                h_all[...], wd[0, :, cols], preferred_element_type=jnp.float32
            ).astype(jnp.bfloat16)
        pieces = given[:1] if t == 0 else given[1 + PIECES * (t - 1) :][:PIECES]
        extent = half // len(pieces)
        targets = [(half + n * extent, extent, piece) for n, piece in enumerate(pieces)]
        for n, (start, extent, target) in enumerate([(0, half, kept[t]), *targets]):
            source = o_buf.at[t, pl.ds(start, extent)]
            o_copies.append(pltpu.make_async_copy(source, target, o_sem.at[n, t]))
            o_copies[-1].start()
    for copy in o_copies:
        copy.wait()


def expert_chunk(info, mine, theirs, router_t, weights, loading):
    parts = len(mine)
    half, width = mine[0].shape
    rows, model = 2 * half, parts * width
    hidden = weights[0].shape[2]
    hid_step = min(256, hidden)
    out_step = 1280 if width % 1280 == 0 else width
    bf16 = jnp.bfloat16
    held_in, held_out = ([HBM] * 3, [VMEM] * 3) if loading else ([VMEM] * 3, [])
    load_scratch = [pltpu.VMEM((2, rows, hidden), jnp.float32)] + [pltpu.SemaphoreType.DMA((LOADS,))] * 3
    load_scratch = load_scratch if loading else []
    place = pltpu.HBM if loading else pltpu.VMEM
    outs = pl.pallas_call(
        functools.partial(expert_kernel, parts, hid_step, out_step, loading),
        in_specs=[SMEM] + [HBM] * (2 * parts) + [VMEM] + held_in,
        out_specs=[HBM] * (parts + 1 + PIECES * (parts - 1)) + held_out,
        out_shape=[jax.ShapeDtypeStruct((half, width), bf16)] * (parts + 1)
        + [jax.ShapeDtypeStruct((half // PIECES, width), bf16)] * (PIECES * (parts - 1))
        + [pltpu.VMEM(w.shape, w.dtype) for w in weights if loading],
        scratch_shapes=[
            pltpu.VMEM((rows, model), bf16),
            pltpu.VMEM((rows, hidden), bf16),
            pltpu.VMEM((parts, rows, width), bf16),
            pltpu.SemaphoreType.DMA((2, parts)),
            pltpu.SemaphoreType.DMA((1 + PIECES, parts)),
        ]
        + load_scratch,
        compiler_params=pltpu.CompilerParams(vmem_limit_bytes=16 * MIB),
        cost_estimate=pl.CostEstimate(
            flops=rows, bytes_accessed=rows, transcendentals=0
        ),
        name="expert_rows",
    )(info, *mine, *theirs, router_t, *[pltpu.with_memory_space_constraint(w, place) for w in weights])
    kept, stay, rest = outs[:parts], outs[parts], outs[parts + 1 :]
    given = [stay] + [rest[PIECES * t : PIECES * (t + 1)] for t in range(parts - 1)]
    return kept, given, list(rest[PIECES * (parts - 1) :]) or weights


def after(value, *earlier):
    return lax.optimization_barrier((value, *earlier))[0]


def f32(value):
    return value.astype(jnp.float32)


def piece_rows(pieces, rows):
    extent = pieces[0].shape[0]
    n = rows.start // extent
    return pieces[n][rows.start - n * extent : rows.stop - n * extent]


def on_device(tokens, router, gate_weight, up_weight, down_weight, routes):
    experts = router.shape[1]
    slots = 2 * tokens.shape[0] // experts
    part_cols = tokens.shape[1]
    parts = lax.axis_size("tensor")
    expert = lax.axis_index("expert") // 2
    place = jnp.stack([lax.axis_index("tensor"), expert]).astype(jnp.int32)
    router_t = router.T
    blocks, column = pack(expert.astype(jnp.int32).reshape(1), routes, tokens, experts, slots)
    per = experts // CHUNKS
    light, heavy = list(range(per, experts // 2)), list(range(experts // 2, experts))
    masks = [list(range(per))]
    for c in range(1, CHUNKS):
        some = light[: per // 2]
        masks.append(some + heavy[: per - len(some)])
        light, heavy = light[len(some) :], heavy[per - len(some) :]
    arrived, returned, mine, theirs, kept, stay, given, sums, gathered = ({} for _ in range(9))
    weights = [gate_weight, up_weight, down_weight]

    def dispatch(some, *earlier):
        for m in some:
            with jax.named_scope(f"dispatch_{m}"):
                arrived[m] = to_expert(after(blocks[m], *earlier), m)

    def landed(c):
        return [arrived[m] for m in masks[c]]

    def features(c, *earlier):
        own = jnp.concatenate(landed(c), axis=0)
        mine[c] = [own] + [None] * (parts - 1)
        with jax.named_scope(f"features_{c}"):
            for t in range(1, parts):
                mine[c][parts - t] = to_tensor(own, t)
        with jax.named_scope(f"pair_{c}"):
            theirs[c] = [to_pair(after(own, *earlier))]

    def rows(c, *earlier):
        nonlocal weights
        with jax.named_scope(f"pair_{c}"):
            theirs[c] += [to_pair(after(v, *earlier)) for v in mine[c][1:]]
        with jax.named_scope(f"rows_{c}"):
            kept[c], (stay[c], *given[c]), weights = expert_chunk(
                place, mine[c], theirs[c], router_t, weights, loading=c == 0
            )

    def pair_sum(c, *earlier):
        with jax.named_scope(f"partial_{c}"):
            sums[c] = []
            for t in range(1, parts):
                other = [to_pair(after(v, *earlier)) for v in given[c][t - 1]]
                total = f32(kept[c][t]) + f32(jnp.concatenate(other))
                sums[c].append(total.astype(jnp.bfloat16))
        with jax.named_scope(f"stay_{c}"):
            stay[c] = to_pair(after(stay[c], *sums[c]))

    def reduce(c):
        with jax.named_scope(f"reduce_{c}"):
            pieces = PIECES if c == CHUNKS - 1 else 1
            extent = sums[c][0].shape[0] // pieces
            gathered[c] = [
                [to_tensor(v[n * extent : (n + 1) * extent], t) for n in range(pieces)]
                for t, v in enumerate(sums[c], start=1)
            ]

    def finished(c):
        outs = []
        for n in range(per):
            span = slice(n * slots, (n + 1) * slots)
            total = f32(kept[c][0][span]) + f32(stay[c][span])
            for pieces in gathered[c]:
                total = total + f32(piece_rows(pieces, span))
            outs.append(total.astype(jnp.bfloat16))
        return outs

    def home(c, outs):
        for m, value in reversed(list(zip(masks[c], outs))):
            with jax.named_scope(f"home_{m}"):
                returned[m] = to_expert(value, m)

    def flat(pieces):
        return [v for some in pieces for v in some]

    dispatch(masks[0])
    dispatch(masks[1][per // 2 :])
    dispatch(masks[1][: per // 2], *landed(0))
    features(0)
    rows_0 = landed(1)
    dispatch(masks[2], *landed(1))
    rows(0, *rows_0)
    features(1, *theirs[0])
    pair_sum(0, *landed(2), *mine[1][1:], theirs[1][0])
    dispatch(masks[3], *landed(2), *mine[1][1:])
    reduce(0)
    rows(1, *sums[0])
    features(2, *theirs[1])
    pair_sum(1, *mine[2][1:], theirs[2][0], *flat(gathered[0]), *landed(3))
    reduce(1)
    rows(2, *sums[1], *landed(3))
    features(3, *theirs[2])
    first = finished(0)
    pair_sum(2, *mine[3][1:], theirs[3][0], *first)
    reduce(2)
    home(0, first)
    second = finished(1)
    rows(3, *sums[2], *second)
    home(1, second)
    pair_sum(3, *[returned[m] for c in (0, 1) for m in masks[c]], *flat(gathered[2]))
    reduce(3)
    home(2, finished(2))
    home(3, finished(3))
    return unpack(column, [returned[m] for m in range(experts)])


def solution(mesh):
    return jax.shard_map(
        on_device,
        mesh=mesh,
        in_specs=(
            P("expert", "tensor"),
            P(),
            P("expert", None, "tensor"),
            P("expert", None, "tensor"),
            P("expert", "tensor", None),
            P("expert", None),
        ),
        out_specs=P("expert", "tensor"),
        check_vma=False,
    )
```

```python
import functools

import jax
import jax.numpy as jnp
from jax import lax
from jax.experimental import pallas as pl
from jax.experimental.pallas import tpu as pltpu
from jax.sharding import PartitionSpec as P

CHUNKS = 4
LOADS = 4
PIECES = 2
MIB = 1 << 20
HBM = pl.BlockSpec(memory_space=pl.ANY)
VMEM = pl.BlockSpec(memory_space=pltpu.VMEM)
SMEM = pl.BlockSpec(memory_space=pltpu.SMEM)


def to_expert(value, mask):
    if mask == 0:
        return value
    pairs = [(i, i ^ (2 * mask)) for i in range(lax.axis_size("expert"))]
    return lax.ppermute(value, "expert", pairs)


def to_pair(value):
    return lax.ppermute(value, "expert", [(i, i ^ 1) for i in range(lax.axis_size("expert"))])


def to_tensor(value, shift):
    size = lax.axis_size("tensor")
    return lax.ppermute(value, "tensor", [(i, (i + shift) % size) for i in range(size)])


def placing_of(place, total):
    slot = lax.broadcasted_iota(jnp.int32, (total, place.shape[1]), 0)
    return (place == slot).astype(jnp.float32).astype(jnp.bfloat16)


def pack_kernel(experts, slots, info, routes, tokens, *outs):
    blocks, column = outs[:experts], outs[experts]
    chosen = routes[...]
    rows = chosen.shape[1]
    onehot = (chosen == lax.broadcasted_iota(jnp.int32, (experts, rows), 0)).astype(jnp.float32)
    earlier = lax.broadcasted_iota(jnp.int32, (rows, rows), 0) < lax.broadcasted_iota(
        jnp.int32, (rows, rows), 1
    )
    counts = jnp.dot(
        onehot.astype(jnp.bfloat16),
        earlier.astype(jnp.float32).astype(jnp.bfloat16),
        preferred_element_type=jnp.float32,
    )
    ranking = jnp.sum(counts * onehot, axis=0, keepdims=True).astype(jnp.int32)
    place = (chosen ^ info[0]) * slots + ranking
    column[...] = place
    packed = jnp.dot(
        placing_of(place, experts * slots), tokens[...], preferred_element_type=jnp.float32
    ).astype(jnp.bfloat16)
    for m in range(experts):
        blocks[m][...] = packed[m * slots : (m + 1) * slots]


def pack(info, routes, tokens, experts, slots):
    rows, width = tokens.shape
    steps = 2 if width % 256 == 0 else 1
    band = width // steps
    outs = pl.pallas_call(
        functools.partial(pack_kernel, experts, slots),
        grid=(steps,),
        in_specs=[
            SMEM,
            pl.BlockSpec((1, rows), lambda i: (0, 0)),
            pl.BlockSpec((rows, band), lambda i: (0, i)),
        ],
        out_specs=[pl.BlockSpec((slots, band), lambda i: (0, i))] * experts
        + [pl.BlockSpec((1, rows), lambda i: (0, 0))],
        out_shape=[jax.ShapeDtypeStruct((slots, width), jnp.bfloat16)] * experts
        + [jax.ShapeDtypeStruct((1, rows), jnp.int32)],
        compiler_params=pltpu.CompilerParams(vmem_limit_bytes=24 * MIB),
        cost_estimate=pl.CostEstimate(
            flops=2 * rows * experts * slots * width, bytes_accessed=6 * rows * width, transcendentals=0
        ),
        name="pack",
    )(info, routes.reshape(1, rows), pltpu.with_memory_space_constraint(tokens, pltpu.HBM))
    return outs[:experts], outs[experts]


def unpack_kernel(experts, slots, column, *refs):
    blocks, mixed = refs[:experts], refs[experts]
    ordered = jnp.concatenate([b[...] for b in blocks], axis=0)
    mixed[...] = lax.dot_general(
        placing_of(column[...], experts * slots),
        ordered,
        (((0,), (0,)), ((), ())),
        preferred_element_type=jnp.float32,
    ).astype(jnp.bfloat16)


def unpack(column, blocks):
    experts = len(blocks)
    slots, width = blocks[0].shape
    rows = column.shape[1]
    steps = 2 if width % 256 == 0 else 1
    band = width // steps
    return pl.pallas_call(
        functools.partial(unpack_kernel, experts, slots),
        grid=(steps,),
        in_specs=[pl.BlockSpec((1, rows), lambda i: (0, 0))]
        + [pl.BlockSpec((slots, band), lambda i: (0, i))] * experts,
        out_specs=pl.BlockSpec((rows, band), lambda i: (0, i)),
        out_shape=jax.ShapeDtypeStruct((rows, width), jnp.bfloat16),
        compiler_params=pltpu.CompilerParams(vmem_limit_bytes=24 * MIB),
        cost_estimate=pl.CostEstimate(
            flops=2 * rows * experts * slots * width, bytes_accessed=6 * rows * width, transcendentals=0
        ),
        name="unpack",
    )(column, *blocks)


def expert_kernel(parts, hid_step, out_step, loading, info, *refs):
    mine, theirs, (router_t, *weights) = refs[:parts], refs[parts : 2 * parts], refs[2 * parts : 2 * parts + 4]
    kept, rest = refs[2 * parts + 4 : 3 * parts + 4], refs[3 * parts + 4 :]
    given, rest = rest[: 1 + PIECES * (parts - 1)], rest[1 + PIECES * (parts - 1) :]
    if loading:
        sources, weights, rest = weights, rest[:3], rest[3:]
    wg, wu, wd = weights
    x_all, h_all, o_buf, x_sem, o_sem, *rest = rest
    if loading:
        proj, g_sem, u_sem, d_sem = rest
    half, width = mine[0].shape
    hidden = wg.shape[2]
    index, expert = info[0], info[1]
    order = list(range(1, parts)) + [0]
    steps = range(0, hidden, hid_step)

    def span(t):
        return pl.ds(pl.multiple_of(lax.rem(index + t, parts) * width, 128), width)

    x_copies, g_copies, u_copies, d_copies, o_copies = [], [], [], [], []
    for t in range(parts):
        own_rows, pair_rows = pl.ds(0, half), pl.ds(half, half)
        x_copies += [
            pltpu.make_async_copy(mine[t], x_all.at[own_rows, span(t)], x_sem.at[0, t]),
            pltpu.make_async_copy(theirs[t], x_all.at[pair_rows, span(t)], x_sem.at[1, t]),
        ]
    if loading:
        band = wg.shape[1] // LOADS
        for n in range(LOADS):
            part = (0, pl.ds(n * band, band))
            g_copies.append(pltpu.make_async_copy(sources[0].at[part], wg.at[part], g_sem.at[n]))
            u_copies.append(pltpu.make_async_copy(sources[1].at[part], wu.at[part], u_sem.at[n]))
            part = (0, pl.ds(n * (hidden // LOADS), hidden // LOADS))
            d_copies.append(pltpu.make_async_copy(sources[2].at[part], wd.at[part], d_sem.at[n]))
    loads = [copy for pair in zip(g_copies, u_copies) for copy in pair] + d_copies
    for copy in x_copies + loads:
        copy.start()
    for copy in x_copies:
        copy.wait()
    logits = lax.dot_general(
        x_all[...], router_t[...], (((1,), (1,)), ((), ())), preferred_element_type=jnp.float32
    )
    names = lax.broadcasted_iota(jnp.int32, logits.shape, 1)
    score = jnp.sum(jnp.where(names == expert, logits, 0.0), axis=1, keepdims=True)
    scale = 1.0 / (1.0 + jnp.exp(-score))
    if loading:
        for n in range(LOADS):
            part = slice(n * band, (n + 1) * band)
            for i, (copies, w) in enumerate(((g_copies, wg), (u_copies, wu))):
                copies[n].wait()
                term = jnp.dot(x_all[:, part], w[0, part, :], preferred_element_type=jnp.float32)
                proj[i] = term if n == 0 else proj[i] + term
    for j in steps:
        cols = slice(j, j + hid_step)
        if loading:
            gate, up = proj[0, :, cols], proj[1, :, cols]
        else:
            gate = jnp.dot(x_all[...], wg[0, :, cols], preferred_element_type=jnp.float32)
            up = jnp.dot(x_all[...], wu[0, :, cols], preferred_element_type=jnp.float32)
        gate, up = scale * gate, scale * up
        h_all[:, cols] = (gate / (1.0 + jnp.exp(-gate)) * up).astype(jnp.bfloat16)
    for copy in d_copies:
        copy.wait()
    for t in order:
        for c in range(0, width, out_step):
            cols = pl.ds(pl.multiple_of(lax.rem(index + t, parts) * width + c, 128), out_step)
            o_buf[t, :, c : c + out_step] = jnp.dot(
                h_all[...], wd[0, :, cols], preferred_element_type=jnp.float32
            ).astype(jnp.bfloat16)
        pieces = given[:1] if t == 0 else given[1 + PIECES * (t - 1) :][:PIECES]
        extent = half // len(pieces)
        targets = [(half + n * extent, extent, piece) for n, piece in enumerate(pieces)]
        for n, (start, extent, target) in enumerate([(0, half, kept[t]), *targets]):
            source = o_buf.at[t, pl.ds(start, extent)]
            o_copies.append(pltpu.make_async_copy(source, target, o_sem.at[n, t]))
            o_copies[-1].start()
    for copy in o_copies:
        copy.wait()


def expert_chunk(info, mine, theirs, router_t, weights, loading):
    parts = len(mine)
    half, width = mine[0].shape
    rows, model = 2 * half, parts * width
    hidden = weights[0].shape[2]
    hid_step = min(256, hidden)
    out_step = 1280 if width % 1280 == 0 else width
    bf16 = jnp.bfloat16
    held_in, held_out = ([HBM] * 3, [VMEM] * 3) if loading else ([VMEM] * 3, [])
    load_scratch = [pltpu.VMEM((2, rows, hidden), jnp.float32)] + [pltpu.SemaphoreType.DMA((LOADS,))] * 3
    load_scratch = load_scratch if loading else []
    place = pltpu.HBM if loading else pltpu.VMEM
    outs = pl.pallas_call(
        functools.partial(expert_kernel, parts, hid_step, out_step, loading),
        in_specs=[SMEM] + [HBM] * (2 * parts) + [VMEM] + held_in,
        out_specs=[HBM] * (parts + 1 + PIECES * (parts - 1)) + held_out,
        out_shape=[jax.ShapeDtypeStruct((half, width), bf16)] * (parts + 1)
        + [jax.ShapeDtypeStruct((half // PIECES, width), bf16)] * (PIECES * (parts - 1))
        + [pltpu.VMEM(w.shape, w.dtype) for w in weights if loading],
        scratch_shapes=[
            pltpu.VMEM((rows, model), bf16),
            pltpu.VMEM((rows, hidden), bf16),
            pltpu.VMEM((parts, rows, width), bf16),
            pltpu.SemaphoreType.DMA((2, parts)),
            pltpu.SemaphoreType.DMA((1 + PIECES, parts)),
        ]
        + load_scratch,
        compiler_params=pltpu.CompilerParams(vmem_limit_bytes=16 * MIB),
        cost_estimate=pl.CostEstimate(
            flops=6 * rows * hidden * model,
            bytes_accessed=4 * rows * model,
            transcendentals=rows * hidden,
        ),
        name="expert_rows",
    )(info, *mine, *theirs, router_t, *[pltpu.with_memory_space_constraint(w, place) for w in weights])
    kept, stay, rest = outs[:parts], outs[parts], outs[parts + 1 :]
    given = [stay] + [rest[PIECES * t : PIECES * (t + 1)] for t in range(parts - 1)]
    return kept, given, list(rest[PIECES * (parts - 1) :]) or weights


def settled(live):
    leaves, shape = jax.tree.flatten(live)
    return jax.tree.unflatten(shape, lax.optimization_barrier(leaves))


def after(value, *earlier):
    return lax.optimization_barrier((value, *earlier))[0]


def f32(value):
    return value.astype(jnp.float32)


def piece_rows(pieces, rows):
    extent = pieces[0].shape[0]
    n = rows.start // extent
    return pieces[n][rows.start - n * extent : rows.stop - n * extent]


def on_device(tokens, router, gate_weight, up_weight, down_weight, routes):
    experts = router.shape[1]
    slots = 2 * tokens.shape[0] // experts
    part_cols = tokens.shape[1]
    parts = lax.axis_size("tensor")
    expert = lax.axis_index("expert") // 2
    place = jnp.stack([lax.axis_index("tensor"), expert]).astype(jnp.int32)
    router_t = router.T
    blocks, column = pack(expert.astype(jnp.int32).reshape(1), routes, tokens, experts, slots)
    masks = [list(range(c, experts, CHUNKS)) for c in range(CHUNKS)]
    weights = [gate_weight, up_weight, down_weight]
    returned = {}

    def dispatch(m, value):
        with jax.named_scope(f"dispatch_{m}"):
            return to_expert(value, m)

    def features(c, some):
        own = jnp.concatenate(some, axis=0)
        mine = [own] + [None] * (parts - 1)
        with jax.named_scope(f"features_{c}"):
            for t in range(1, parts):
                mine[parts - t] = to_tensor(own, t)
        with jax.named_scope(f"pair_{c}"):
            return dict(mine=mine, pair=to_pair(own))

    def rows(c, chunk, *earlier):
        nonlocal weights
        with jax.named_scope(f"pair_{c}"):
            theirs = [chunk["pair"]] + [to_pair(after(v, *earlier)) for v in chunk["mine"][1:]]
        with jax.named_scope(f"rows_{c}"):
            kept, given, weights = expert_chunk(
                place, chunk["mine"], theirs, router_t, weights, loading=c == 0
            )
        return dict(kept=kept, given=given)

    def pair_sum(c, chunk, *earlier, swap=True):
        kept, (stay, *given) = chunk["kept"], chunk["given"]
        with jax.named_scope(f"partial_{c}"):
            sums = []
            for t in range(1, parts):
                other = [to_pair(after(v, *earlier)) for v in given[t - 1]]
                sums.append((f32(kept[t]) + f32(jnp.concatenate(other))).astype(jnp.bfloat16))
        stay = swapped(c, stay, *sums) if swap else stay
        return dict(kept=kept[0], stay=stay, sums=sums)

    def swapped(c, stay, *earlier):
        with jax.named_scope(f"stay_{c}"):
            return to_pair(after(stay, *earlier))

    def reduce(c, chunk, pieces):
        extent = chunk["sums"][0].shape[0] // pieces
        with jax.named_scope(f"reduce_{c}"):
            gathered = [
                [to_tensor(v[n * extent : (n + 1) * extent], t) for n in range(pieces)]
                for t, v in enumerate(chunk["sums"], start=1)
            ]
        return dict(kept=chunk["kept"], stay=chunk["stay"], gathered=gathered)

    def home(c, chunk, earlier={}):
        for n, m in reversed(list(enumerate(masks[c]))):
            span = slice(n * slots, (n + 1) * slots)
            with jax.named_scope(f"home_{m}"):
                total = f32(chunk["kept"][span]) + f32(chunk["stay"][span])
                for pieces in chunk["gathered"]:
                    total = total + f32(piece_rows(pieces, span))
                value = after(total.astype(jnp.bfloat16), *earlier.get(m, []))
                returned[m] = to_expert(value, m)
        return [returned[m] for m in masks[c]]

    blocks = dict(enumerate(blocks))
    arrived = {}

    def landing(some):
        for m in some:
            arrived[m] = dispatch(m, blocks.pop(m))

    half = len(masks[0]) // 2
    landing(reversed(masks[0]))
    arrived, blocks = settled((arrived, blocks))
    x0 = features(0, [arrived[m] for m in masks[0]])
    landing(reversed(masks[1]))
    arrived, blocks, x0 = settled((arrived, blocks, x0))
    x1 = features(1, [arrived[m] for m in masks[1]])
    landing(masks[2][half:] + masks[2][:half] + masks[3][:half])
    y0 = rows(0, x0)
    arrived, blocks, x1, y0 = settled((arrived, blocks, x1, y0))
    x2 = features(2, [arrived[m] for m in masks[2]])
    landing(masks[3][half:])
    z0 = reduce(0, pair_sum(0, y0), 1)
    y1 = rows(1, x1)
    arrived, x2, y1, z0 = settled((arrived, x2, y1, z0))
    x3 = features(3, [arrived[m] for m in masks[3]])
    back = home(0, z0)
    s1 = pair_sum(1, y1)
    z1 = reduce(1, s1, 1)
    y2 = rows(2, x2, *s1["sums"])
    s2 = pair_sum(2, y2, *back, *x3["mine"][1:], x3["pair"], s1["stay"])
    z2 = reduce(2, s2, PIECES)
    y3 = rows(3, x3, *s2["sums"])
    crossed = [pieces[0] for pieces in z1["gathered"] + z2["gathered"]]
    s3 = pair_sum(3, y3, *crossed, s2["stay"], swap=False)
    z3 = reduce(3, s3, PIECES)
    low, high = slice(0, half), slice(half, 2 * half)
    z1["kept"] = after(z1["kept"], y3["given"][0])
    home(1, z1)
    z2["kept"] = after(z2["kept"], *s3["sums"])
    near, far = ([returned[m] for m in masks[1][part]] for part in (low, high))
    home(2, z2, {m: far for m in masks[2][low]} | {m: near for m in masks[2][high]})
    z3["stay"] = swapped(3, s3["stay"], *[pieces[-1] for pieces in z3["gathered"]])
    home(3, z3, {m: [returned[n] for n in masks[2][low]] for m in masks[3][low]})
    return unpack(column, [returned[m] for m in range(experts)])


def solution(mesh):
    return jax.shard_map(
        on_device,
        mesh=mesh,
        in_specs=(
            P("expert", "tensor"),
            P(),
            P("expert", None, "tensor"),
            P("expert", None, "tensor"),
            P("expert", "tensor", None),
            P("expert", None),
        ),
        out_specs=P("expert", "tensor"),
        check_vma=False,
    )
```

```python
import functools

import jax
import jax.numpy as jnp
from jax import lax
from jax.experimental import pallas as pl
from jax.experimental.pallas import tpu as pltpu
from jax.sharding import PartitionSpec as P

CHUNKS = 4
LOADS = 4
PIECES = 2
MIB = 1 << 20
HBM = pl.BlockSpec(memory_space=pl.ANY)
VMEM = pl.BlockSpec(memory_space=pltpu.VMEM)
SMEM = pl.BlockSpec(memory_space=pltpu.SMEM)


def to_expert(value, mask):
    if mask == 0:
        return value
    pairs = [(i, i ^ (2 * mask)) for i in range(lax.axis_size("expert"))]
    return lax.ppermute(value, "expert", pairs)


def to_pair(value):
    return lax.ppermute(value, "expert", [(i, i ^ 1) for i in range(lax.axis_size("expert"))])


def to_tensor(value, shift):
    size = lax.axis_size("tensor")
    return lax.ppermute(value, "tensor", [(i, (i + shift) % size) for i in range(size)])


def placing_of(place, total):
    slot = lax.broadcasted_iota(jnp.int32, (total, place.shape[1]), 0)
    return (place == slot).astype(jnp.float32).astype(jnp.bfloat16)


def pack_kernel(experts, slots, info, routes, tokens, *outs):
    blocks, column = outs[:experts], outs[experts]
    chosen = routes[...]
    rows = chosen.shape[1]
    onehot = (chosen == lax.broadcasted_iota(jnp.int32, (experts, rows), 0)).astype(jnp.float32)
    earlier = lax.broadcasted_iota(jnp.int32, (rows, rows), 0) < lax.broadcasted_iota(
        jnp.int32, (rows, rows), 1
    )
    counts = jnp.dot(
        onehot.astype(jnp.bfloat16),
        earlier.astype(jnp.float32).astype(jnp.bfloat16),
        preferred_element_type=jnp.float32,
    )
    ranking = jnp.sum(counts * onehot, axis=0, keepdims=True).astype(jnp.int32)
    place = (chosen ^ info[0]) * slots + ranking
    column[...] = place
    packed = jnp.dot(
        placing_of(place, experts * slots), tokens[...], preferred_element_type=jnp.float32
    ).astype(jnp.bfloat16)
    for m in range(experts):
        blocks[m][...] = packed[m * slots : (m + 1) * slots]


def pack(info, routes, tokens, experts, slots):
    rows, width = tokens.shape
    steps = 2 if width % 256 == 0 else 1
    band = width // steps
    outs = pl.pallas_call(
        functools.partial(pack_kernel, experts, slots),
        grid=(steps,),
        in_specs=[
            SMEM,
            pl.BlockSpec((1, rows), lambda i: (0, 0)),
            pl.BlockSpec((rows, band), lambda i: (0, i)),
        ],
        out_specs=[pl.BlockSpec((slots, band), lambda i: (0, i))] * experts
        + [pl.BlockSpec((1, rows), lambda i: (0, 0))],
        out_shape=[jax.ShapeDtypeStruct((slots, width), jnp.bfloat16)] * experts
        + [jax.ShapeDtypeStruct((1, rows), jnp.int32)],
        compiler_params=pltpu.CompilerParams(vmem_limit_bytes=24 * MIB),
        cost_estimate=pl.CostEstimate(
            flops=2 * rows * experts * slots * width, bytes_accessed=6 * rows * width, transcendentals=0
        ),
        name="pack",
    )(info, routes.reshape(1, rows), pltpu.with_memory_space_constraint(tokens, pltpu.HBM))
    return outs[:experts], outs[experts]


def unpack_kernel(experts, slots, column, *refs):
    blocks, mixed = refs[:experts], refs[experts]
    ordered = jnp.concatenate([b[...] for b in blocks], axis=0)
    mixed[...] = lax.dot_general(
        placing_of(column[...], experts * slots),
        ordered,
        (((0,), (0,)), ((), ())),
        preferred_element_type=jnp.float32,
    ).astype(jnp.bfloat16)


def unpack(column, blocks):
    experts = len(blocks)
    slots, width = blocks[0].shape
    rows = column.shape[1]
    steps = 2 if width % 256 == 0 else 1
    band = width // steps
    return pl.pallas_call(
        functools.partial(unpack_kernel, experts, slots),
        grid=(steps,),
        in_specs=[pl.BlockSpec((1, rows), lambda i: (0, 0))]
        + [pl.BlockSpec((slots, band), lambda i: (0, i))] * experts,
        out_specs=pl.BlockSpec((rows, band), lambda i: (0, i)),
        out_shape=jax.ShapeDtypeStruct((rows, width), jnp.bfloat16),
        compiler_params=pltpu.CompilerParams(vmem_limit_bytes=24 * MIB),
        cost_estimate=pl.CostEstimate(
            flops=2 * rows * experts * slots * width, bytes_accessed=6 * rows * width, transcendentals=0
        ),
        name="unpack",
    )(column, *blocks)


def expert_kernel(parts, hid_step, out_step, loading, info, *refs):
    mine, theirs, (router_t, *weights) = refs[:parts], refs[parts : 2 * parts], refs[2 * parts : 2 * parts + 4]
    kept, rest = refs[2 * parts + 4 : 3 * parts + 4], refs[3 * parts + 4 :]
    given, rest = rest[: 1 + PIECES * (parts - 1)], rest[1 + PIECES * (parts - 1) :]
    if loading:
        sources, weights, rest = weights, rest[:3], rest[3:]
    wg, wu, wd = weights
    x_all, h_all, o_buf, x_sem, o_sem, *rest = rest
    if loading:
        proj, g_sem, u_sem, d_sem = rest
    half, width = mine[0].shape
    hidden = wg.shape[2]
    index, expert = info[0], info[1]
    order = list(range(1, parts)) + [0]
    steps = range(0, hidden, hid_step)

    def span(t):
        return pl.ds(pl.multiple_of(lax.rem(index + t, parts) * width, 128), width)

    x_copies, g_copies, u_copies, d_copies, o_copies = [], [], [], [], []
    for t in range(parts):
        own_rows, pair_rows = pl.ds(0, half), pl.ds(half, half)
        x_copies += [
            pltpu.make_async_copy(mine[t], x_all.at[own_rows, span(t)], x_sem.at[0, t]),
            pltpu.make_async_copy(theirs[t], x_all.at[pair_rows, span(t)], x_sem.at[1, t]),
        ]
    if loading:
        band = wg.shape[1] // LOADS
        for n in range(LOADS):
            part = (0, pl.ds(n * band, band))
            g_copies.append(pltpu.make_async_copy(sources[0].at[part], wg.at[part], g_sem.at[n]))
            u_copies.append(pltpu.make_async_copy(sources[1].at[part], wu.at[part], u_sem.at[n]))
            part = (0, pl.ds(n * (hidden // LOADS), hidden // LOADS))
            d_copies.append(pltpu.make_async_copy(sources[2].at[part], wd.at[part], d_sem.at[n]))
    loads = [copy for pair in zip(g_copies, u_copies) for copy in pair] + d_copies
    for copy in x_copies + loads:
        copy.start()
    for copy in x_copies:
        copy.wait()
    logits = lax.dot_general(
        x_all[...], router_t[...], (((1,), (1,)), ((), ())), preferred_element_type=jnp.float32
    )
    names = lax.broadcasted_iota(jnp.int32, logits.shape, 1)
    score = jnp.sum(jnp.where(names == expert, logits, 0.0), axis=1, keepdims=True)
    scale = 1.0 / (1.0 + jnp.exp(-score))
    if loading:
        for n in range(LOADS):
            part = slice(n * band, (n + 1) * band)
            for i, (copies, w) in enumerate(((g_copies, wg), (u_copies, wu))):
                copies[n].wait()
                term = jnp.dot(x_all[:, part], w[0, part, :], preferred_element_type=jnp.float32)
                proj[i] = term if n == 0 else proj[i] + term
    for j in steps:
        cols = slice(j, j + hid_step)
        if loading:
            gate, up = proj[0, :, cols], proj[1, :, cols]
        else:
            gate = jnp.dot(x_all[...], wg[0, :, cols], preferred_element_type=jnp.float32)
            up = jnp.dot(x_all[...], wu[0, :, cols], preferred_element_type=jnp.float32)
        gate, up = scale * gate, scale * up
        h_all[:, cols] = (gate / (1.0 + jnp.exp(-gate)) * up).astype(jnp.bfloat16)
    for copy in d_copies:
        copy.wait()
    for t in order:
        for c in range(0, width, out_step):
            cols = pl.ds(pl.multiple_of(lax.rem(index + t, parts) * width + c, 128), out_step)
            o_buf[t, :, c : c + out_step] = jnp.dot(
                h_all[...], wd[0, :, cols], preferred_element_type=jnp.float32
            ).astype(jnp.bfloat16)
        pieces = given[:1] if t == 0 else given[1 + PIECES * (t - 1) :][:PIECES]
        extent = half // len(pieces)
        targets = [(half + n * extent, extent, piece) for n, piece in enumerate(pieces)]
        for n, (start, extent, target) in enumerate([(0, half, kept[t]), *targets]):
            source = o_buf.at[t, pl.ds(start, extent)]
            o_copies.append(pltpu.make_async_copy(source, target, o_sem.at[n, t]))
            o_copies[-1].start()
    for copy in o_copies:
        copy.wait()


def expert_chunk(info, mine, theirs, router_t, weights, loading):
    parts = len(mine)
    half, width = mine[0].shape
    rows, model = 2 * half, parts * width
    hidden = weights[0].shape[2]
    hid_step = min(256, hidden)
    out_step = 1280 if width % 1280 == 0 else width
    bf16 = jnp.bfloat16
    held_in, held_out = ([HBM] * 3, [VMEM] * 3) if loading else ([VMEM] * 3, [])
    load_scratch = [pltpu.VMEM((2, rows, hidden), jnp.float32)] + [pltpu.SemaphoreType.DMA((LOADS,))] * 3
    load_scratch = load_scratch if loading else []
    place = pltpu.HBM if loading else pltpu.VMEM
    outs = pl.pallas_call(
        functools.partial(expert_kernel, parts, hid_step, out_step, loading),
        in_specs=[SMEM] + [HBM] * (2 * parts) + [VMEM] + held_in,
        out_specs=[HBM] * (parts + 1 + PIECES * (parts - 1)) + held_out,
        out_shape=[jax.ShapeDtypeStruct((half, width), bf16)] * (parts + 1)
        + [jax.ShapeDtypeStruct((half // PIECES, width), bf16)] * (PIECES * (parts - 1))
        + [pltpu.VMEM(w.shape, w.dtype) for w in weights if loading],
        scratch_shapes=[
            pltpu.VMEM((rows, model), bf16),
            pltpu.VMEM((rows, hidden), bf16),
            pltpu.VMEM((parts, rows, width), bf16),
            pltpu.SemaphoreType.DMA((2, parts)),
            pltpu.SemaphoreType.DMA((1 + PIECES, parts)),
        ]
        + load_scratch,
        compiler_params=pltpu.CompilerParams(vmem_limit_bytes=16 * MIB),
        cost_estimate=pl.CostEstimate(
            flops=6 * rows * hidden * model,
            bytes_accessed=4 * rows * model,
            transcendentals=rows * hidden,
        ),
        name="expert_rows",
    )(info, *mine, *theirs, router_t, *[pltpu.with_memory_space_constraint(w, place) for w in weights])
    kept, stay, rest = outs[:parts], outs[parts], outs[parts + 1 :]
    given = [stay] + [rest[PIECES * t : PIECES * (t + 1)] for t in range(parts - 1)]
    return kept, given, list(rest[PIECES * (parts - 1) :]) or weights


def settled(live):
    leaves, shape = jax.tree.flatten(live)
    return jax.tree.unflatten(shape, lax.optimization_barrier(leaves))


def after(value, *earlier):
    return lax.optimization_barrier((value, *earlier))[0]


def f32(value):
    return value.astype(jnp.float32)


def piece_rows(pieces, rows):
    extent = pieces[0].shape[0]
    n = rows.start // extent
    return pieces[n][rows.start - n * extent : rows.stop - n * extent]


def on_device(tokens, router, gate_weight, up_weight, down_weight, routes):
    experts = router.shape[1]
    slots = 2 * tokens.shape[0] // experts
    part_cols = tokens.shape[1]
    parts = lax.axis_size("tensor")
    expert = lax.axis_index("expert") // 2
    place = jnp.stack([lax.axis_index("tensor"), expert]).astype(jnp.int32)
    router_t = router.T
    blocks, column = pack(expert.astype(jnp.int32).reshape(1), routes, tokens, experts, slots)
    masks = [list(range(c, experts, CHUNKS)) for c in range(CHUNKS)]
    weights = [gate_weight, up_weight, down_weight]
    returned = {}

    def dispatch(m, value):
        with jax.named_scope(f"dispatch_{m}"):
            return to_expert(value, m)

    def features(c, some):
        own = jnp.concatenate(some, axis=0)
        mine = [own] + [None] * (parts - 1)
        with jax.named_scope(f"features_{c}"):
            for t in range(1, parts):
                mine[parts - t] = to_tensor(own, t)
        with jax.named_scope(f"pair_{c}"):
            return dict(mine=mine, pair=to_pair(own))

    def rows(c, chunk, *earlier):
        nonlocal weights
        with jax.named_scope(f"pair_{c}"):
            theirs = [chunk["pair"]] + [to_pair(after(v, *earlier)) for v in chunk["mine"][1:]]
        with jax.named_scope(f"rows_{c}"):
            kept, given, weights = expert_chunk(
                place, chunk["mine"], theirs, router_t, weights, loading=c == 0
            )
        return dict(kept=kept, given=given)

    def pair_sum(c, chunk, *earlier):
        kept, (stay, *given) = chunk["kept"], chunk["given"]
        with jax.named_scope(f"partial_{c}"):
            sums = []
            for t in range(1, parts):
                other = [to_pair(after(v, *earlier)) for v in given[t - 1]]
                sums.append((f32(kept[t]) + f32(jnp.concatenate(other))).astype(jnp.bfloat16))
        with jax.named_scope(f"stay_{c}"):
            return dict(kept=kept[0], stay=to_pair(after(stay, *sums)), sums=sums)

    def reduce(c, chunk, pieces):
        extent = chunk["sums"][0].shape[0] // pieces
        with jax.named_scope(f"reduce_{c}"):
            gathered = [
                [to_tensor(v[n * extent : (n + 1) * extent], t) for n in range(pieces)]
                for t, v in enumerate(chunk["sums"], start=1)
            ]
        return dict(kept=chunk["kept"], stay=chunk["stay"], gathered=gathered)

    def finished(c, chunk, n, *earlier):
        span = slice(n * slots, (n + 1) * slots)
        total = f32(after(chunk["kept"], *earlier)[span]) + f32(chunk["stay"][span])
        for pieces in chunk["gathered"]:
            total = total + f32(piece_rows(pieces, span))
        return total.astype(jnp.bfloat16)

    def home(c, outs):
        for m, value in reversed(list(zip(masks[c], outs))):
            with jax.named_scope(f"home_{m}"):
                returned[m] = to_expert(value, m)
        return [returned[m] for m in masks[c]]

    blocks = dict(enumerate(blocks))
    arrived = {}

    def landing(some):
        for m in some:
            arrived[m] = dispatch(m, blocks.pop(m))

    half = len(masks[0]) // 2
    landing(reversed(masks[0]))
    arrived, blocks = settled((arrived, blocks))
    x0 = features(0, [arrived[m] for m in masks[0]])
    landing(reversed(masks[1]))
    arrived, blocks, x0 = settled((arrived, blocks, x0))
    x1 = features(1, [arrived[m] for m in masks[1]])
    landing(masks[2][half:] + masks[2][:half] + masks[3][:half])
    y0 = rows(0, x0)
    arrived, blocks, x1, y0 = settled((arrived, blocks, x1, y0))
    x2 = features(2, [arrived[m] for m in masks[2]])
    landing(masks[3][half:])
    z0 = reduce(0, pair_sum(0, y0), 1)
    y1 = rows(1, x1)
    arrived, x2, y1, z0 = settled((arrived, x2, y1, z0))
    x3 = features(3, [arrived[m] for m in masks[3]])
    each = range(2 * half)
    back = home(0, [finished(0, z0, n) for n in each])
    s1 = pair_sum(1, y1)
    z1 = reduce(1, s1, PIECES)
    y2 = rows(2, x2, *s1["sums"])
    crossed = x3["mine"][1:] + [pieces[0] for pieces in z1["gathered"]]
    s2 = pair_sum(2, y2, *back, *crossed, x3["pair"], s1["stay"])
    z2 = reduce(2, s2, 1)
    outs = [finished(1, z1, n, *s2["sums"]) for n in each]
    y3 = rows(3, x3, *s2["sums"], *outs)
    back = home(1, outs)
    s3 = pair_sum(3, y3, *back, *[pieces[0] for pieces in z2["gathered"]], s2["stay"])
    z3 = reduce(3, s3, PIECES)
    back = home(2, [finished(2, z2, n, *s3["sums"]) for n in each])
    late = [finished(3, z3, n) for n in each[half:]]
    home(3, [finished(3, z3, n, *late, *back) for n in each[:half]] + late)
    return unpack(column, [returned[m] for m in range(experts)])


def solution(mesh):
    return jax.shard_map(
        on_device,
        mesh=mesh,
        in_specs=(
            P("expert", "tensor"),
            P(),
            P("expert", None, "tensor"),
            P("expert", None, "tensor"),
            P("expert", "tensor", None),
            P("expert", None),
        ),
        out_specs=P("expert", "tensor"),
        check_vma=False,
    )
```

```python
import functools

import jax
import jax.numpy as jnp
from jax import lax
from jax.experimental import pallas as pl
from jax.experimental.pallas import tpu as pltpu
from jax.sharding import PartitionSpec as P

CHUNKS = 4
LOADS = 4
PIECES = 2
MIB = 1 << 20
HBM = pl.BlockSpec(memory_space=pl.ANY)
VMEM = pl.BlockSpec(memory_space=pltpu.VMEM)
SMEM = pl.BlockSpec(memory_space=pltpu.SMEM)


def to_expert(value, mask):
    if mask == 0:
        return value
    pairs = [(i, i ^ (2 * mask)) for i in range(lax.axis_size("expert"))]
    return lax.ppermute(value, "expert", pairs)


def to_pair(value):
    return lax.ppermute(value, "expert", [(i, i ^ 1) for i in range(lax.axis_size("expert"))])


def to_tensor(value, shift):
    size = lax.axis_size("tensor")
    return lax.ppermute(value, "tensor", [(i, (i + shift) % size) for i in range(size)])


def placing_of(place, total):
    slot = lax.broadcasted_iota(jnp.int32, (total, place.shape[1]), 0)
    return (place == slot).astype(jnp.float32).astype(jnp.bfloat16)


def pack_kernel(experts, slots, info, routes, tokens, *outs):
    blocks, column = outs[:experts], outs[experts]
    chosen = routes[...]
    rows = chosen.shape[1]
    onehot = (chosen == lax.broadcasted_iota(jnp.int32, (experts, rows), 0)).astype(jnp.float32)
    earlier = lax.broadcasted_iota(jnp.int32, (rows, rows), 0) < lax.broadcasted_iota(
        jnp.int32, (rows, rows), 1
    )
    counts = jnp.dot(
        onehot.astype(jnp.bfloat16),
        earlier.astype(jnp.float32).astype(jnp.bfloat16),
        preferred_element_type=jnp.float32,
    )
    ranking = jnp.sum(counts * onehot, axis=0, keepdims=True).astype(jnp.int32)
    place = (chosen ^ info[0]) * slots + ranking
    column[...] = place
    packed = jnp.dot(
        placing_of(place, experts * slots), tokens[...], preferred_element_type=jnp.float32
    ).astype(jnp.bfloat16)
    for m in range(experts):
        blocks[m][...] = packed[m * slots : (m + 1) * slots]


def pack(info, routes, tokens, experts, slots):
    rows, width = tokens.shape
    steps = 2 if width % 256 == 0 else 1
    band = width // steps
    outs = pl.pallas_call(
        functools.partial(pack_kernel, experts, slots),
        grid=(steps,),
        in_specs=[
            SMEM,
            pl.BlockSpec((1, rows), lambda i: (0, 0)),
            pl.BlockSpec((rows, band), lambda i: (0, i)),
        ],
        out_specs=[pl.BlockSpec((slots, band), lambda i: (0, i))] * experts
        + [pl.BlockSpec((1, rows), lambda i: (0, 0))],
        out_shape=[jax.ShapeDtypeStruct((slots, width), jnp.bfloat16)] * experts
        + [jax.ShapeDtypeStruct((1, rows), jnp.int32)],
        compiler_params=pltpu.CompilerParams(vmem_limit_bytes=24 * MIB),
        cost_estimate=pl.CostEstimate(
            flops=2 * rows * experts * slots * width, bytes_accessed=6 * rows * width, transcendentals=0
        ),
        name="pack",
    )(info, routes.reshape(1, rows), pltpu.with_memory_space_constraint(tokens, pltpu.HBM))
    return outs[:experts], outs[experts]


def unpack_kernel(masks, slots, column, *refs):
    blocks, earlier, mixed = refs[: len(masks)], refs[len(masks) : -1], refs[-1]
    ordered = jnp.concatenate([b[...] for b in blocks], axis=0)
    place = column[...]
    placing = jnp.concatenate([placing_of(place - m * slots, slots) for m in masks], axis=0)
    total = lax.dot_general(
        placing, ordered, (((0,), (0,)), ((), ())), preferred_element_type=jnp.float32
    )
    for part in earlier:
        total = total + part[...].astype(jnp.float32)
    mixed[...] = total.astype(jnp.bfloat16)


def unpack(column, blocks, earlier):
    masks = sorted(blocks)
    slots, width = blocks[masks[0]].shape
    rows = column.shape[1]
    steps = 2 if width % 256 == 0 else 1
    band = width // steps
    whole = pl.BlockSpec((rows, band), lambda i: (0, i))
    before = [] if earlier is None else [earlier]
    return pl.pallas_call(
        functools.partial(unpack_kernel, masks, slots),
        grid=(steps,),
        in_specs=[pl.BlockSpec((1, rows), lambda i: (0, 0))]
        + [pl.BlockSpec((slots, band), lambda i: (0, i))] * len(masks)
        + [whole] * len(before),
        out_specs=whole,
        out_shape=jax.ShapeDtypeStruct((rows, width), jnp.bfloat16),
        compiler_params=pltpu.CompilerParams(vmem_limit_bytes=24 * MIB),
        cost_estimate=pl.CostEstimate(
            flops=16 * len(masks) * rows * slots * width, bytes_accessed=6 * rows * width, transcendentals=0
        ),
        name="unpack",
    )(column, *[blocks[m] for m in masks], *before)


def expert_kernel(parts, hid_step, out_step, loading, info, *refs):
    mine, theirs, (router_t, *weights) = refs[:parts], refs[parts : 2 * parts], refs[2 * parts : 2 * parts + 4]
    kept, rest = refs[2 * parts + 4 : 3 * parts + 4], refs[3 * parts + 4 :]
    given, rest = rest[: 1 + PIECES * (parts - 1)], rest[1 + PIECES * (parts - 1) :]
    if loading:
        sources, weights, rest = weights, rest[:3], rest[3:]
    wg, wu, wd = weights
    x_all, h_all, o_buf, x_sem, o_sem, *rest = rest
    if loading:
        proj, g_sem, u_sem, d_sem = rest
    half, width = mine[0].shape
    hidden = wg.shape[2]
    index, expert = info[0], info[1]
    order = list(range(1, parts)) + [0]
    steps = range(0, hidden, hid_step)

    def span(t):
        return pl.ds(pl.multiple_of(lax.rem(index + t, parts) * width, 128), width)

    x_copies, g_copies, u_copies, d_copies, o_copies = [], [], [], [], []
    for t in range(parts):
        own_rows, pair_rows = pl.ds(0, half), pl.ds(half, half)
        x_copies += [
            pltpu.make_async_copy(mine[t], x_all.at[own_rows, span(t)], x_sem.at[0, t]),
            pltpu.make_async_copy(theirs[t], x_all.at[pair_rows, span(t)], x_sem.at[1, t]),
        ]
    if loading:
        band = wg.shape[1] // LOADS
        for n in range(LOADS):
            part = (0, pl.ds(n * band, band))
            g_copies.append(pltpu.make_async_copy(sources[0].at[part], wg.at[part], g_sem.at[n]))
            u_copies.append(pltpu.make_async_copy(sources[1].at[part], wu.at[part], u_sem.at[n]))
            part = (0, pl.ds(n * (hidden // LOADS), hidden // LOADS))
            d_copies.append(pltpu.make_async_copy(sources[2].at[part], wd.at[part], d_sem.at[n]))
    loads = [copy for pair in zip(g_copies, u_copies) for copy in pair] + d_copies
    for copy in x_copies + loads:
        copy.start()
    for copy in x_copies:
        copy.wait()
    logits = lax.dot_general(
        x_all[...], router_t[...], (((1,), (1,)), ((), ())), preferred_element_type=jnp.float32
    )
    names = lax.broadcasted_iota(jnp.int32, logits.shape, 1)
    score = jnp.sum(jnp.where(names == expert, logits, 0.0), axis=1, keepdims=True)
    scale = 1.0 / (1.0 + jnp.exp(-score))
    if loading:
        for n in range(LOADS):
            part = slice(n * band, (n + 1) * band)
            for i, (copies, w) in enumerate(((g_copies, wg), (u_copies, wu))):
                copies[n].wait()
                term = jnp.dot(x_all[:, part], w[0, part, :], preferred_element_type=jnp.float32)
                proj[i] = term if n == 0 else proj[i] + term
    for j in steps:
        cols = slice(j, j + hid_step)
        if loading:
            gate, up = proj[0, :, cols], proj[1, :, cols]
        else:
            gate = jnp.dot(x_all[...], wg[0, :, cols], preferred_element_type=jnp.float32)
            up = jnp.dot(x_all[...], wu[0, :, cols], preferred_element_type=jnp.float32)
        gate, up = scale * gate, scale * up
        h_all[:, cols] = (gate / (1.0 + jnp.exp(-gate)) * up).astype(jnp.bfloat16)
    for copy in d_copies:
        copy.wait()
    for t in order:
        for c in range(0, width, out_step):
            cols = pl.ds(pl.multiple_of(lax.rem(index + t, parts) * width + c, 128), out_step)
            o_buf[t, :, c : c + out_step] = jnp.dot(
                h_all[...], wd[0, :, cols], preferred_element_type=jnp.float32
            ).astype(jnp.bfloat16)
        pieces = given[:1] if t == 0 else given[1 + PIECES * (t - 1) :][:PIECES]
        extent = half // len(pieces)
        targets = [(half + n * extent, extent, piece) for n, piece in enumerate(pieces)]
        for n, (start, extent, target) in enumerate([(0, half, kept[t]), *targets]):
            source = o_buf.at[t, pl.ds(start, extent)]
            o_copies.append(pltpu.make_async_copy(source, target, o_sem.at[n, t]))
            o_copies[-1].start()
    for copy in o_copies:
        copy.wait()


def expert_chunk(info, mine, theirs, router_t, weights, loading):
    parts = len(mine)
    half, width = mine[0].shape
    rows, model = 2 * half, parts * width
    hidden = weights[0].shape[2]
    hid_step = min(256, hidden)
    out_step = 1280 if width % 1280 == 0 else width
    bf16 = jnp.bfloat16
    held_in, held_out = ([HBM] * 3, [VMEM] * 3) if loading else ([VMEM] * 3, [])
    load_scratch = [pltpu.VMEM((2, rows, hidden), jnp.float32)] + [pltpu.SemaphoreType.DMA((LOADS,))] * 3
    load_scratch = load_scratch if loading else []
    place = pltpu.HBM if loading else pltpu.VMEM
    outs = pl.pallas_call(
        functools.partial(expert_kernel, parts, hid_step, out_step, loading),
        in_specs=[SMEM] + [HBM] * (2 * parts) + [VMEM] + held_in,
        out_specs=[HBM] * (parts + 1 + PIECES * (parts - 1)) + held_out,
        out_shape=[jax.ShapeDtypeStruct((half, width), bf16)] * (parts + 1)
        + [jax.ShapeDtypeStruct((half // PIECES, width), bf16)] * (PIECES * (parts - 1))
        + [pltpu.VMEM(w.shape, w.dtype) for w in weights if loading],
        scratch_shapes=[
            pltpu.VMEM((rows, model), bf16),
            pltpu.VMEM((rows, hidden), bf16),
            pltpu.VMEM((parts, rows, width), bf16),
            pltpu.SemaphoreType.DMA((2, parts)),
            pltpu.SemaphoreType.DMA((1 + PIECES, parts)),
        ]
        + load_scratch,
        compiler_params=pltpu.CompilerParams(vmem_limit_bytes=16 * MIB),
        cost_estimate=pl.CostEstimate(
            flops=6 * rows * hidden * model,
            bytes_accessed=4 * rows * model,
            transcendentals=rows * hidden,
        ),
        name="expert_rows",
    )(info, *mine, *theirs, router_t, *[pltpu.with_memory_space_constraint(w, place) for w in weights])
    kept, stay, rest = outs[:parts], outs[parts], outs[parts + 1 :]
    given = [stay] + [rest[PIECES * t : PIECES * (t + 1)] for t in range(parts - 1)]
    return kept, given, list(rest[PIECES * (parts - 1) :]) or weights


def settled(live):
    leaves, shape = jax.tree.flatten(live)
    return jax.tree.unflatten(shape, lax.optimization_barrier(leaves))


def after(value, *earlier):
    return lax.optimization_barrier((value, *earlier))[0]


def f32(value):
    return value.astype(jnp.float32)


def piece_rows(pieces, rows):
    extent = pieces[0].shape[0]
    n = rows.start // extent
    return pieces[n][rows.start - n * extent : rows.stop - n * extent]


def on_device(tokens, router, gate_weight, up_weight, down_weight, routes):
    experts = router.shape[1]
    slots = 2 * tokens.shape[0] // experts
    part_cols = tokens.shape[1]
    parts = lax.axis_size("tensor")
    expert = lax.axis_index("expert") // 2
    place = jnp.stack([lax.axis_index("tensor"), expert]).astype(jnp.int32)
    router_t = router.T
    blocks, column = pack(expert.astype(jnp.int32).reshape(1), routes, tokens, experts, slots)
    masks = [list(range(c, experts, CHUNKS)) for c in range(CHUNKS)]
    weights = [gate_weight, up_weight, down_weight]
    returned = {}

    def dispatch(m, value):
        with jax.named_scope(f"dispatch_{m}"):
            return to_expert(value, m)

    def features(c, some):
        own = jnp.concatenate(some, axis=0)
        mine = [own] + [None] * (parts - 1)
        with jax.named_scope(f"features_{c}"):
            for t in range(1, parts):
                mine[parts - t] = to_tensor(own, t)
        with jax.named_scope(f"pair_{c}"):
            return dict(mine=mine, pair=to_pair(own))

    def rows(c, chunk, *earlier):
        nonlocal weights
        with jax.named_scope(f"pair_{c}"):
            theirs = [chunk["pair"]] + [to_pair(after(v, *earlier)) for v in chunk["mine"][1:]]
        with jax.named_scope(f"rows_{c}"):
            kept, given, weights = expert_chunk(
                place, chunk["mine"], theirs, router_t, weights, loading=c == 0
            )
        return dict(kept=kept, given=given)

    def pair_sum(c, chunk, *earlier):
        kept, (stay, *given) = chunk["kept"], chunk["given"]
        with jax.named_scope(f"partial_{c}"):
            sums = []
            for t in range(1, parts):
                other = [to_pair(after(v, *earlier)) for v in given[t - 1]]
                sums.append((f32(kept[t]) + f32(jnp.concatenate(other))).astype(jnp.bfloat16))
        with jax.named_scope(f"stay_{c}"):
            return dict(kept=kept[0], stay=to_pair(after(stay, *sums)), sums=sums)

    def reduce(c, chunk, pieces):
        extent = chunk["sums"][0].shape[0] // pieces
        with jax.named_scope(f"reduce_{c}"):
            gathered = [
                [to_tensor(v[n * extent : (n + 1) * extent], t) for n in range(pieces)]
                for t, v in enumerate(chunk["sums"], start=1)
            ]
        return dict(kept=chunk["kept"], stay=chunk["stay"], gathered=gathered)

    def finished(c, chunk, n, *earlier):
        span = slice(n * slots, (n + 1) * slots)
        total = f32(after(chunk["kept"], *earlier)[span]) + f32(chunk["stay"][span])
        for pieces in chunk["gathered"]:
            total = total + f32(piece_rows(pieces, span))
        return total.astype(jnp.bfloat16)

    def home(c, outs):
        for m, value in reversed(list(zip(masks[c], outs))):
            with jax.named_scope(f"home_{m}"):
                returned[m] = to_expert(value, m)
        return [returned[m] for m in masks[c]]

    blocks = dict(enumerate(blocks))
    arrived = {}

    def landing(some):
        for m in some:
            arrived[m] = dispatch(m, blocks.pop(m))

    half = len(masks[0]) // 2
    landing(reversed(masks[0]))
    arrived, blocks = settled((arrived, blocks))
    x0 = features(0, [arrived[m] for m in masks[0]])
    landing(reversed(masks[1]))
    arrived, blocks, x0 = settled((arrived, blocks, x0))
    x1 = features(1, [arrived[m] for m in masks[1]])
    landing(masks[2][half:] + masks[2][:half] + masks[3][:half])
    y0 = rows(0, x0)
    arrived, blocks, x1, y0 = settled((arrived, blocks, x1, y0))
    each = range(2 * half)
    x2 = features(2, [arrived[m] for m in masks[2]])
    landing(masks[3][half:])
    s0 = pair_sum(0, y0)
    z0 = reduce(0, s0, PIECES)
    y1 = rows(1, x1, *s0["sums"])
    due = [*x2["mine"][1:], x2["pair"], s0["stay"], *[arrived[m] for m in masks[3]]]
    s1 = pair_sum(1, y1, *due, *[pieces[0] for pieces in z0["gathered"]])
    z1 = reduce(1, s1, 1)
    x3 = features(3, [arrived[m] for m in masks[3]])
    outs = [finished(0, z0, n, *s1["sums"]) for n in each]
    y2 = rows(2, x2, *s1["sums"], *outs)
    due = [*home(0, outs), x3["pair"], s1["stay"]]
    s2 = pair_sum(2, y2, *due, *[pieces[0] for pieces in z1["gathered"]])
    z2 = reduce(2, s2, 1)
    outs = [finished(1, z1, n, *s2["sums"]) for n in each]
    y3 = rows(3, x3, *s2["sums"], *outs)
    due = [*home(1, outs), s2["stay"]]
    s3 = pair_sum(3, y3, *due, *[pieces[0] for pieces in z2["gathered"]])
    z3 = reduce(3, s3, PIECES)
    home(2, [finished(2, z2, n, *s3["sums"]) for n in each])
    late = [finished(3, z3, n) for n in each[half:]]
    home(3, [finished(3, z3, n, *late) for n in each[:half]] + late)
    last = masks[3][:half]
    mixed = unpack(column, {m: v for m, v in returned.items() if m not in last}, None)
    return unpack(column, {m: returned[m] for m in last}, mixed)


def solution(mesh):
    return jax.shard_map(
        on_device,
        mesh=mesh,
        in_specs=(
            P("expert", "tensor"),
            P(),
            P("expert", None, "tensor"),
            P("expert", None, "tensor"),
            P("expert", "tensor", None),
            P("expert", None),
        ),
        out_specs=P("expert", "tensor"),
        check_vma=False,
    )
```

```python
import functools

import jax
import jax.numpy as jnp
from jax import lax
from jax.experimental import pallas as pl
from jax.experimental.pallas import tpu as pltpu
from jax.sharding import PartitionSpec as P

CHUNKS = 4
LOADS = 2
PIECES = 2
MIB = 1 << 20
HBM = pl.BlockSpec(memory_space=pl.ANY)
VMEM = pl.BlockSpec(memory_space=pltpu.VMEM)
SMEM = pl.BlockSpec(memory_space=pltpu.SMEM)


def to_expert(value, mask):
    if mask == 0:
        return value
    pairs = [(i, i ^ (2 * mask)) for i in range(lax.axis_size("expert"))]
    return lax.ppermute(value, "expert", pairs)


def to_pair(value):
    return lax.ppermute(value, "expert", [(i, i ^ 1) for i in range(lax.axis_size("expert"))])


def to_tensor(value, shift):
    size = lax.axis_size("tensor")
    return lax.ppermute(value, "tensor", [(i, (i + shift) % size) for i in range(size)])


def placing_of(place, total):
    slot = lax.broadcasted_iota(jnp.int32, (total, place.shape[1]), 0)
    return (place == slot).astype(jnp.float32).astype(jnp.bfloat16)


def pack_kernel(experts, slots, info, routes, tokens, *outs):
    blocks, column = outs[:experts], outs[experts]
    chosen = routes[...]
    rows = chosen.shape[1]
    onehot = (chosen == lax.broadcasted_iota(jnp.int32, (experts, rows), 0)).astype(jnp.float32)
    earlier = lax.broadcasted_iota(jnp.int32, (rows, rows), 0) < lax.broadcasted_iota(
        jnp.int32, (rows, rows), 1
    )
    counts = jnp.dot(
        onehot.astype(jnp.bfloat16),
        earlier.astype(jnp.float32).astype(jnp.bfloat16),
        preferred_element_type=jnp.float32,
    )
    ranking = jnp.sum(counts * onehot, axis=0, keepdims=True).astype(jnp.int32)
    place = (chosen ^ info[0]) * slots + ranking
    column[...] = place
    packed = jnp.dot(
        placing_of(place, experts * slots), tokens[...], preferred_element_type=jnp.float32
    ).astype(jnp.bfloat16)
    for m in range(experts):
        blocks[m][...] = packed[m * slots : (m + 1) * slots]


def pack(info, routes, tokens, experts, slots):
    rows, width = tokens.shape
    steps = 2 if width % 256 == 0 else 1
    band = width // steps
    outs = pl.pallas_call(
        functools.partial(pack_kernel, experts, slots),
        grid=(steps,),
        in_specs=[
            SMEM,
            pl.BlockSpec((1, rows), lambda i: (0, 0)),
            pl.BlockSpec((rows, band), lambda i: (0, i)),
        ],
        out_specs=[pl.BlockSpec((slots, band), lambda i: (0, i))] * experts
        + [pl.BlockSpec((1, rows), lambda i: (0, 0))],
        out_shape=[jax.ShapeDtypeStruct((slots, width), jnp.bfloat16)] * experts
        + [jax.ShapeDtypeStruct((1, rows), jnp.int32)],
        compiler_params=pltpu.CompilerParams(vmem_limit_bytes=24 * MIB),
        cost_estimate=pl.CostEstimate(
            flops=2 * rows * experts * slots * width, bytes_accessed=6 * rows * width, transcendentals=0
        ),
        name="pack",
    )(info, routes.reshape(1, rows), pltpu.with_memory_space_constraint(tokens, pltpu.HBM))
    return outs[:experts], outs[experts]


def unpack_kernel(masks, slots, column, *refs):
    blocks, earlier, mixed = refs[: len(masks)], refs[len(masks) : -1], refs[-1]
    ordered = jnp.concatenate([b[...] for b in blocks], axis=0)
    place = column[...]
    placing = jnp.concatenate([placing_of(place - m * slots, slots) for m in masks], axis=0)
    total = lax.dot_general(
        placing, ordered, (((0,), (0,)), ((), ())), preferred_element_type=jnp.float32
    )
    for part in earlier:
        total = total + part[...].astype(jnp.float32)
    mixed[...] = total.astype(jnp.bfloat16)


def unpack(column, blocks, earlier):
    masks = sorted(blocks)
    slots, width = blocks[masks[0]].shape
    rows = column.shape[1]
    steps = 2 if width % 256 == 0 else 1
    band = width // steps
    whole = pl.BlockSpec((rows, band), lambda i: (0, i))
    before = [] if earlier is None else [earlier]
    return pl.pallas_call(
        functools.partial(unpack_kernel, masks, slots),
        grid=(steps,),
        in_specs=[pl.BlockSpec((1, rows), lambda i: (0, 0))]
        + [pl.BlockSpec((slots, band), lambda i: (0, i))] * len(masks)
        + [whole] * len(before),
        out_specs=whole,
        out_shape=jax.ShapeDtypeStruct((rows, width), jnp.bfloat16),
        compiler_params=pltpu.CompilerParams(vmem_limit_bytes=24 * MIB),
        cost_estimate=pl.CostEstimate(
            flops=16 * len(masks) * rows * slots * width, bytes_accessed=6 * rows * width, transcendentals=0
        ),
        name="unpack",
    )(column, *[blocks[m] for m in masks], *before)


def expert_kernel(parts, hid_step, out_step, loading, info, *refs):
    mine, theirs, (router_t, *weights) = refs[:parts], refs[parts : 2 * parts], refs[2 * parts : 2 * parts + 4]
    kept, given = refs[2 * parts + 4 : 3 * parts + 4], refs[3 * parts + 4]
    rest = refs[3 * parts + 5 :]
    if loading:
        sources, weights, rest = weights, rest[:3], rest[3:]
    wg, wu, wd = weights
    x_all, h_all, o_buf, x_sem, o_sem, *rest = rest
    if loading:
        proj, g_sem, u_sem, d_sem = rest
    half, width = mine[0].shape
    hidden = wg.shape[2]
    index, expert = info[0], info[1]
    order = list(range(1, parts)) + [0]
    steps = range(0, hidden, hid_step)

    def span(t):
        return pl.ds(pl.multiple_of(lax.rem(index + t, parts) * width, 128), width)

    x_copies, g_copies, u_copies, d_copies, o_copies = [], [], [], [], []
    for t in range(parts):
        own_rows, pair_rows = pl.ds(0, half), pl.ds(half, half)
        x_copies += [
            pltpu.make_async_copy(mine[t], x_all.at[own_rows, span(t)], x_sem.at[0, t]),
            pltpu.make_async_copy(theirs[t], x_all.at[pair_rows, span(t)], x_sem.at[1, t]),
        ]
    if loading:
        band = wg.shape[1] // LOADS
        for n in range(LOADS):
            part = (0, pl.ds(n * band, band))
            g_copies.append(pltpu.make_async_copy(sources[0].at[part], wg.at[part], g_sem.at[n]))
            u_copies.append(pltpu.make_async_copy(sources[1].at[part], wu.at[part], u_sem.at[n]))
            part = (0, pl.ds(n * (hidden // LOADS), hidden // LOADS))
            d_copies.append(pltpu.make_async_copy(sources[2].at[part], wd.at[part], d_sem.at[n]))
    loads = [copy for pair in zip(g_copies, u_copies) for copy in pair] + d_copies
    for copy in x_copies + loads:
        copy.start()
    for copy in x_copies:
        copy.wait()
    logits = lax.dot_general(
        x_all[...], router_t[...], (((1,), (1,)), ((), ())), preferred_element_type=jnp.float32
    )
    names = lax.broadcasted_iota(jnp.int32, logits.shape, 1)
    score = jnp.sum(jnp.where(names == expert, logits, 0.0), axis=1, keepdims=True)
    scale = 1.0 / (1.0 + jnp.exp(-score))
    if loading:
        for n in range(LOADS):
            part = slice(n * band, (n + 1) * band)
            for i, (copies, w) in enumerate(((g_copies, wg), (u_copies, wu))):
                copies[n].wait()
                term = jnp.dot(x_all[:, part], w[0, part, :], preferred_element_type=jnp.float32)
                proj[i] = term if n == 0 else proj[i] + term
    for j in steps:
        cols = slice(j, j + hid_step)
        if loading:
            gate, up = proj[0, :, cols], proj[1, :, cols]
        else:
            gate = jnp.dot(x_all[...], wg[0, :, cols], preferred_element_type=jnp.float32)
            up = jnp.dot(x_all[...], wu[0, :, cols], preferred_element_type=jnp.float32)
        gate, up = scale * gate, scale * up
        h_all[:, cols] = (gate / (1.0 + jnp.exp(-gate)) * up).astype(jnp.bfloat16)
    for copy in d_copies:
        copy.wait()
    for t in order:
        for c in range(0, width, out_step):
            cols = pl.ds(pl.multiple_of(lax.rem(index + t, parts) * width + c, 128), out_step)
            o_buf[t, :, c : c + out_step] = jnp.dot(
                h_all[...], wd[0, :, cols], preferred_element_type=jnp.float32
            ).astype(jnp.bfloat16)
        o_copies += [
            pltpu.make_async_copy(
                o_buf.at[t, pl.ds(half, half)], given.at[:, pl.ds(t * width, width)], o_sem.at[1, t]
            ),
            pltpu.make_async_copy(o_buf.at[t, pl.ds(0, half)], kept[t], o_sem.at[0, t]),
        ]
        o_copies[-2].start()
        o_copies[-1].start()
    for copy in o_copies:
        copy.wait()


def expert_chunk(info, mine, theirs, router_t, weights, loading):
    parts = len(mine)
    half, width = mine[0].shape
    rows, model = 2 * half, parts * width
    hidden = weights[0].shape[2]
    hid_step = min(256, hidden)
    out_step = 1280 if width % 1280 == 0 else width
    bf16 = jnp.bfloat16
    held_in, held_out = ([HBM] * 3, [VMEM] * 3) if loading else ([VMEM] * 3, [])
    load_scratch = [pltpu.VMEM((2, rows, hidden), jnp.float32)] + [pltpu.SemaphoreType.DMA((LOADS,))] * 3
    load_scratch = load_scratch if loading else []
    place = pltpu.HBM if loading else pltpu.VMEM
    outs = pl.pallas_call(
        functools.partial(expert_kernel, parts, hid_step, out_step, loading),
        in_specs=[SMEM] + [HBM] * (2 * parts) + [VMEM] + held_in,
        out_specs=[HBM] * (parts + 1) + held_out,
        out_shape=[jax.ShapeDtypeStruct((half, width), bf16)] * parts
        + [jax.ShapeDtypeStruct((half, model), bf16)]
        + [pltpu.VMEM(w.shape, w.dtype) for w in weights if loading],
        scratch_shapes=[
            pltpu.VMEM((rows, model), bf16),
            pltpu.VMEM((rows, hidden), bf16),
            pltpu.VMEM((parts, rows, width), bf16),
            pltpu.SemaphoreType.DMA((2, parts)),
            pltpu.SemaphoreType.DMA((2, parts)),
        ]
        + load_scratch,
        compiler_params=pltpu.CompilerParams(vmem_limit_bytes=16 * MIB),
        cost_estimate=pl.CostEstimate(
            flops=6 * rows * hidden * model,
            bytes_accessed=4 * rows * model,
            transcendentals=rows * hidden,
        ),
        name="expert_rows",
    )(info, *mine, *theirs, router_t, *[pltpu.with_memory_space_constraint(w, place) for w in weights])
    return outs[:parts], outs[parts], list(outs[parts + 1 :]) or weights


def settled(live):
    leaves, shape = jax.tree.flatten(live)
    return jax.tree.unflatten(shape, lax.optimization_barrier(leaves))


def after(value, *earlier):
    return lax.optimization_barrier((value, *earlier))[0]


def f32(value):
    return value.astype(jnp.float32)


def piece_rows(pieces, rows):
    extent = pieces[0].shape[0]
    n = rows.start // extent
    return pieces[n][rows.start - n * extent : rows.stop - n * extent]


def on_device(tokens, router, gate_weight, up_weight, down_weight, routes):
    experts = router.shape[1]
    slots = 2 * tokens.shape[0] // experts
    part_cols = tokens.shape[1]
    parts = lax.axis_size("tensor")
    expert = lax.axis_index("expert") // 2
    place = jnp.stack([lax.axis_index("tensor"), expert]).astype(jnp.int32)
    router_t = router.T
    blocks, column = pack(expert.astype(jnp.int32).reshape(1), routes, tokens, experts, slots)
    masks = [list(range(c, experts, CHUNKS)) for c in range(CHUNKS)]
    weights = [gate_weight, up_weight, down_weight]
    returned = {}

    def dispatch(m, value):
        with jax.named_scope(f"dispatch_{m}"):
            return to_expert(value, m)

    def features(c, some):
        own = jnp.concatenate(some, axis=0)
        mine = [own] + [None] * (parts - 1)
        with jax.named_scope(f"features_{c}"):
            for t in range(1, parts):
                mine[parts - t] = to_tensor(own, t)
        with jax.named_scope(f"pair_{c}"):
            return dict(mine=mine, pair=to_pair(own))

    def rows(c, chunk):
        nonlocal weights
        with jax.named_scope(f"pair_{c}"):
            theirs = [chunk["pair"]] + [to_pair(v) for v in chunk["mine"][1:]]
        with jax.named_scope(f"rows_{c}"):
            kept, given, weights = expert_chunk(
                place, chunk["mine"], theirs, router_t, weights, loading=c == 0
            )
        return dict(kept=kept, given=given)

    def pair_sum(c, chunk):
        kept, sums = chunk["kept"], []
        with jax.named_scope(f"partial_{c}"):
            given = to_pair(chunk["given"])
            for t in range(1, parts):
                other = given[:, t * part_cols : (t + 1) * part_cols]
                sums.append((f32(kept[t]) + f32(other)).astype(jnp.bfloat16))
        return dict(kept=kept[0], stay=given[:, :part_cols], sums=sums)

    def reduce(c, chunk, pieces):
        extent = chunk["sums"][0].shape[0] // pieces
        with jax.named_scope(f"reduce_{c}"):
            gathered = [
                [to_tensor(v[n * extent : (n + 1) * extent], t) for n in range(pieces)]
                for t, v in enumerate(chunk["sums"], start=1)
            ]
        return dict(kept=chunk["kept"], stay=chunk["stay"], gathered=gathered)

    def finished(chunk, n, *earlier):
        span = slice(n * slots, (n + 1) * slots)
        total = f32(after(chunk["kept"], *earlier)[span]) + f32(chunk["stay"][span])
        for pieces in chunk["gathered"]:
            total = total + f32(piece_rows(pieces, span))
        return total.astype(jnp.bfloat16)

    def home(c, outs):
        for m, value in reversed(list(zip(masks[c], outs))):
            with jax.named_scope(f"home_{m}"):
                returned[m] = to_expert(value, m)
        return [returned[m] for m in masks[c]]

    blocks = dict(enumerate(blocks))
    arrived = {}

    def landing(some):
        for m in some:
            arrived[m] = dispatch(m, blocks.pop(m))

    half = len(masks[0]) // 2
    landing(reversed(masks[0]))
    arrived, blocks = settled((arrived, blocks))
    x0 = features(0, [arrived[m] for m in masks[0]])
    landing(reversed(masks[1]))
    arrived, blocks, x0 = settled((arrived, blocks, x0))
    x1 = features(1, [arrived[m] for m in masks[1]])
    landing(masks[2][half:] + masks[2][:half] + masks[3][:half])
    y0 = rows(0, x0)
    arrived, blocks, x1, y0 = settled((arrived, blocks, x1, y0))
    each = range(2 * half)
    x2 = features(2, [arrived[m] for m in masks[2]])
    landing(masks[3][half:])
    z0 = reduce(0, pair_sum(0, y0), 1)
    y1 = rows(1, x1)
    arrived, x2, y1, z0 = settled((arrived, x2, y1, z0))
    x3 = features(3, [arrived[m] for m in masks[3]])
    home(0, [finished(z0, n) for n in each])
    z1 = reduce(1, pair_sum(1, y1), 1)
    y2 = rows(2, x2)
    returned, x3, y2, z1 = settled((returned, x3, y2, z1))
    home(1, [finished(z1, n) for n in each])
    z2 = reduce(2, pair_sum(2, y2), 1)
    y3 = rows(3, x3)
    returned, y3, z2 = settled((returned, y3, z2))
    z3 = reduce(3, pair_sum(3, y3), PIECES)
    home(2, [finished(z2, n) for n in each])
    late = [finished(z3, n) for n in each[half:]]
    home(3, [finished(z3, n, *late) for n in each[:half]] + late)
    last = masks[3][:half]
    mixed = unpack(column, {m: v for m, v in returned.items() if m not in last}, None)
    return unpack(column, {m: returned[m] for m in last}, mixed)


def solution(mesh):
    return jax.shard_map(
        on_device,
        mesh=mesh,
        in_specs=(
            P("expert", "tensor"),
            P(),
            P("expert", None, "tensor"),
            P("expert", None, "tensor"),
            P("expert", "tensor", None),
            P("expert", None),
        ),
        out_specs=P("expert", "tensor"),
        check_vma=False,
    )
```

```python
import functools

import jax
import jax.numpy as jnp
from jax import lax
from jax.experimental import pallas as pl
from jax.experimental.pallas import tpu as pltpu
from jax.sharding import PartitionSpec as P

CHUNKS = 4
LOADS = 2
PIECES = 2
MIB = 1 << 20
HBM = pl.BlockSpec(memory_space=pl.ANY)
VMEM = pl.BlockSpec(memory_space=pltpu.VMEM)
SMEM = pl.BlockSpec(memory_space=pltpu.SMEM)


def to_expert(value, mask):
    if mask == 0:
        return value
    pairs = [(i, i ^ (2 * mask)) for i in range(lax.axis_size("expert"))]
    return lax.ppermute(value, "expert", pairs)


def to_pair(value):
    return lax.ppermute(value, "expert", [(i, i ^ 1) for i in range(lax.axis_size("expert"))])


def to_tensor(value, shift):
    size = lax.axis_size("tensor")
    return lax.ppermute(value, "tensor", [(i, (i + shift) % size) for i in range(size)])


def placing_of(place, total):
    slot = lax.broadcasted_iota(jnp.int32, (total, place.shape[1]), 0)
    return (place == slot).astype(jnp.float32).astype(jnp.bfloat16)


def pack_kernel(experts, slots, info, routes, tokens, *outs):
    blocks, column = outs[:experts], outs[experts]
    chosen = routes[...]
    rows = chosen.shape[1]
    onehot = (chosen == lax.broadcasted_iota(jnp.int32, (experts, rows), 0)).astype(jnp.float32)
    earlier = lax.broadcasted_iota(jnp.int32, (rows, rows), 0) < lax.broadcasted_iota(
        jnp.int32, (rows, rows), 1
    )
    counts = jnp.dot(
        onehot.astype(jnp.bfloat16),
        earlier.astype(jnp.float32).astype(jnp.bfloat16),
        preferred_element_type=jnp.float32,
    )
    ranking = jnp.sum(counts * onehot, axis=0, keepdims=True).astype(jnp.int32)
    place = (chosen ^ info[0]) * slots + ranking
    column[...] = place
    packed = jnp.dot(
        placing_of(place, experts * slots), tokens[...], preferred_element_type=jnp.float32
    ).astype(jnp.bfloat16)
    for m in range(experts):
        blocks[m][...] = packed[m * slots : (m + 1) * slots]


def pack(info, routes, tokens, experts, slots):
    rows, width = tokens.shape
    steps = 2 if width % 256 == 0 else 1
    band = width // steps
    outs = pl.pallas_call(
        functools.partial(pack_kernel, experts, slots),
        grid=(steps,),
        in_specs=[
            SMEM,
            pl.BlockSpec((1, rows), lambda i: (0, 0)),
            pl.BlockSpec((rows, band), lambda i: (0, i)),
        ],
        out_specs=[pl.BlockSpec((slots, band), lambda i: (0, i))] * experts
        + [pl.BlockSpec((1, rows), lambda i: (0, 0))],
        out_shape=[jax.ShapeDtypeStruct((slots, width), jnp.bfloat16)] * experts
        + [jax.ShapeDtypeStruct((1, rows), jnp.int32)],
        compiler_params=pltpu.CompilerParams(vmem_limit_bytes=24 * MIB),
        cost_estimate=pl.CostEstimate(
            flops=2 * rows * experts * slots * width, bytes_accessed=6 * rows * width, transcendentals=0
        ),
        name="pack",
    )(info, routes.reshape(1, rows), pltpu.with_memory_space_constraint(tokens, pltpu.HBM))
    return outs[:experts], outs[experts]


def unpack_kernel(masks, slots, column, *refs):
    blocks, earlier, mixed = refs[: len(masks)], refs[len(masks) : -1], refs[-1]
    ordered = jnp.concatenate([b[...] for b in blocks], axis=0)
    place = column[...]
    placing = jnp.concatenate([placing_of(place - m * slots, slots) for m in masks], axis=0)
    total = lax.dot_general(
        placing, ordered, (((0,), (0,)), ((), ())), preferred_element_type=jnp.float32
    )
    for part in earlier:
        total = total + part[...].astype(jnp.float32)
    mixed[...] = total.astype(jnp.bfloat16)


def unpack(column, blocks, earlier):
    masks = sorted(blocks)
    slots, width = blocks[masks[0]].shape
    rows = column.shape[1]
    steps = 2 if width % 256 == 0 else 1
    band = width // steps
    whole = pl.BlockSpec((rows, band), lambda i: (0, i))
    before = [] if earlier is None else [earlier]
    return pl.pallas_call(
        functools.partial(unpack_kernel, masks, slots),
        grid=(steps,),
        in_specs=[pl.BlockSpec((1, rows), lambda i: (0, 0))]
        + [pl.BlockSpec((slots, band), lambda i: (0, i))] * len(masks)
        + [whole] * len(before),
        out_specs=whole,
        out_shape=jax.ShapeDtypeStruct((rows, width), jnp.bfloat16),
        compiler_params=pltpu.CompilerParams(vmem_limit_bytes=24 * MIB),
        cost_estimate=pl.CostEstimate(
            flops=16 * len(masks) * rows * slots * width, bytes_accessed=6 * rows * width, transcendentals=0
        ),
        name="unpack",
    )(column, *[blocks[m] for m in masks], *before)


def expert_kernel(parts, hid_step, out_step, loading, info, *refs):
    mine, theirs, (router_t, *weights) = refs[:parts], refs[parts : 2 * parts], refs[2 * parts : 2 * parts + 4]
    kept, given = refs[2 * parts + 4 : 3 * parts + 4], refs[3 * parts + 4]
    rest = refs[3 * parts + 5 :]
    if loading:
        sources, weights, rest = weights, rest[:3], rest[3:]
    wg, wu, wd = weights
    x_all, h_all, o_buf, x_sem, o_sem, *rest = rest
    if loading:
        proj, g_sem, u_sem, d_sem = rest
    half, width = mine[0].shape
    hidden = wg.shape[2]
    index, expert = info[0], info[1]
    order = list(range(1, parts)) + [0]
    steps = range(0, hidden, hid_step)

    def span(t):
        return pl.ds(pl.multiple_of(lax.rem(index + t, parts) * width, 128), width)

    x_copies, g_copies, u_copies, d_copies, o_copies = [], [], [], [], []
    for t in range(parts):
        own_rows, pair_rows = pl.ds(0, half), pl.ds(half, half)
        x_copies += [
            pltpu.make_async_copy(mine[t], x_all.at[own_rows, span(t)], x_sem.at[0, t]),
            pltpu.make_async_copy(theirs[t], x_all.at[pair_rows, span(t)], x_sem.at[1, t]),
        ]
    if loading:
        band = wg.shape[1] // LOADS
        for n in range(LOADS):
            part = (0, pl.ds(n * band, band))
            g_copies.append(pltpu.make_async_copy(sources[0].at[part], wg.at[part], g_sem.at[n]))
            u_copies.append(pltpu.make_async_copy(sources[1].at[part], wu.at[part], u_sem.at[n]))
            part = (0, pl.ds(n * (hidden // LOADS), hidden // LOADS))
            d_copies.append(pltpu.make_async_copy(sources[2].at[part], wd.at[part], d_sem.at[n]))
    loads = [copy for pair in zip(g_copies, u_copies) for copy in pair] + d_copies
    for copy in x_copies + loads:
        copy.start()
    for copy in x_copies:
        copy.wait()
    logits = lax.dot_general(
        x_all[...], router_t[...], (((1,), (1,)), ((), ())), preferred_element_type=jnp.float32
    )
    names = lax.broadcasted_iota(jnp.int32, logits.shape, 1)
    score = jnp.sum(jnp.where(names == expert, logits, 0.0), axis=1, keepdims=True)
    scale = 1.0 / (1.0 + jnp.exp(-score))
    if loading:
        for n in range(LOADS):
            part = slice(n * band, (n + 1) * band)
            for i, (copies, w) in enumerate(((g_copies, wg), (u_copies, wu))):
                copies[n].wait()
                term = jnp.dot(x_all[:, part], w[0, part, :], preferred_element_type=jnp.float32)
                proj[i] = term if n == 0 else proj[i] + term
    for j in steps:
        cols = slice(j, j + hid_step)
        if loading:
            gate, up = proj[0, :, cols], proj[1, :, cols]
        else:
            gate = jnp.dot(x_all[...], wg[0, :, cols], preferred_element_type=jnp.float32)
            up = jnp.dot(x_all[...], wu[0, :, cols], preferred_element_type=jnp.float32)
        gate, up = scale * gate, scale * up
        h_all[:, cols] = (gate / (1.0 + jnp.exp(-gate)) * up).astype(jnp.bfloat16)
    for copy in d_copies:
        copy.wait()
    for t in order:
        for c in range(0, width, out_step):
            cols = pl.ds(pl.multiple_of(lax.rem(index + t, parts) * width + c, 128), out_step)
            o_buf[t, :, c : c + out_step] = jnp.dot(
                h_all[...], wd[0, :, cols], preferred_element_type=jnp.float32
            ).astype(jnp.bfloat16)
        o_copies += [
            pltpu.make_async_copy(
                o_buf.at[t, pl.ds(half, half)], given.at[:, pl.ds(t * width, width)], o_sem.at[1, t]
            ),
            pltpu.make_async_copy(o_buf.at[t, pl.ds(0, half)], kept[t], o_sem.at[0, t]),
        ]
        o_copies[-2].start()
        o_copies[-1].start()
    for copy in o_copies:
        copy.wait()


def expert_chunk(info, mine, theirs, router_t, weights, loading):
    parts = len(mine)
    half, width = mine[0].shape
    rows, model = 2 * half, parts * width
    hidden = weights[0].shape[2]
    hid_step = min(256, hidden)
    out_step = 1280 if width % 1280 == 0 else width
    bf16 = jnp.bfloat16
    held_in, held_out = ([HBM] * 3, [VMEM] * 3) if loading else ([VMEM] * 3, [])
    load_scratch = [pltpu.VMEM((2, rows, hidden), jnp.float32)] + [pltpu.SemaphoreType.DMA((LOADS,))] * 3
    load_scratch = load_scratch if loading else []
    place = pltpu.HBM if loading else pltpu.VMEM
    outs = pl.pallas_call(
        functools.partial(expert_kernel, parts, hid_step, out_step, loading),
        in_specs=[SMEM] + [HBM] * (2 * parts) + [VMEM] + held_in,
        out_specs=[HBM] * (parts + 1) + held_out,
        out_shape=[jax.ShapeDtypeStruct((half, width), bf16)] * parts
        + [jax.ShapeDtypeStruct((half, model), bf16)]
        + [pltpu.VMEM(w.shape, w.dtype) for w in weights if loading],
        scratch_shapes=[
            pltpu.VMEM((rows, model), bf16),
            pltpu.VMEM((rows, hidden), bf16),
            pltpu.VMEM((parts, rows, width), bf16),
            pltpu.SemaphoreType.DMA((2, parts)),
            pltpu.SemaphoreType.DMA((2, parts)),
        ]
        + load_scratch,
        compiler_params=pltpu.CompilerParams(vmem_limit_bytes=16 * MIB),
        cost_estimate=pl.CostEstimate(
            flops=6 * rows * hidden * model,
            bytes_accessed=4 * rows * model,
            transcendentals=rows * hidden,
        ),
        name="expert_rows",
    )(info, *mine, *theirs, router_t, *[pltpu.with_memory_space_constraint(w, place) for w in weights])
    return outs[:parts], outs[parts], list(outs[parts + 1 :]) or weights


def settled(live):
    leaves, shape = jax.tree.flatten(live)
    return jax.tree.unflatten(shape, lax.optimization_barrier(leaves))


def after(value, *earlier):
    return lax.optimization_barrier((value, *earlier))[0]


def f32(value):
    return value.astype(jnp.float32)


def piece_rows(pieces, rows):
    extent = pieces[0].shape[0]
    n = rows.start // extent
    return pieces[n][rows.start - n * extent : rows.stop - n * extent]


def on_device(tokens, router, gate_weight, up_weight, down_weight, routes):
    experts = router.shape[1]
    slots = 2 * tokens.shape[0] // experts
    part_cols = tokens.shape[1]
    parts = lax.axis_size("tensor")
    expert = lax.axis_index("expert") // 2
    place = jnp.stack([lax.axis_index("tensor"), expert]).astype(jnp.int32)
    router_t = router.T
    blocks, column = pack(expert.astype(jnp.int32).reshape(1), routes, tokens, experts, slots)
    masks = [list(range(c, experts, CHUNKS)) for c in range(CHUNKS)]
    weights = [gate_weight, up_weight, down_weight]
    returned = {}

    def dispatch(m, value):
        with jax.named_scope(f"dispatch_{m}"):
            return to_expert(value, m)

    def features(c, some):
        own = jnp.concatenate(some, axis=0)
        mine = [own] + [None] * (parts - 1)
        with jax.named_scope(f"features_{c}"):
            for t in range(1, parts):
                mine[parts - t] = to_tensor(own, t)
        with jax.named_scope(f"pair_{c}"):
            return dict(mine=mine, pair=to_pair(own))

    def rows(c, chunk, *earlier):
        nonlocal weights
        with jax.named_scope(f"pair_{c}"):
            theirs = [chunk["pair"]] + [to_pair(after(v, *earlier)) for v in chunk["mine"][1:]]
        with jax.named_scope(f"rows_{c}"):
            kept, given, weights = expert_chunk(
                place, chunk["mine"], theirs, router_t, weights, loading=c == 0
            )
        return dict(kept=kept, given=given)

    def pair_sum(c, chunk, *earlier):
        kept, sums = chunk["kept"], []
        with jax.named_scope(f"partial_{c}"):
            given = to_pair(after(chunk["given"], *earlier))
            for t in range(1, parts):
                other = given[:, t * part_cols : (t + 1) * part_cols]
                sums.append((f32(kept[t]) + f32(other)).astype(jnp.bfloat16))
        return dict(kept=kept[0], stay=given[:, :part_cols], sums=sums)

    def reduce(c, chunk, pieces):
        extent = chunk["sums"][0].shape[0] // pieces
        with jax.named_scope(f"reduce_{c}"):
            gathered = [
                [to_tensor(v[n * extent : (n + 1) * extent], t) for n in range(pieces)]
                for t, v in enumerate(chunk["sums"], start=1)
            ]
        return dict(kept=chunk["kept"], stay=chunk["stay"], gathered=gathered)

    def finished(chunk, n, *earlier):
        span = slice(n * slots, (n + 1) * slots)
        total = f32(after(chunk["kept"], *earlier)[span]) + f32(chunk["stay"][span])
        for pieces in chunk["gathered"]:
            total = total + f32(piece_rows(pieces, span))
        return total.astype(jnp.bfloat16)

    def home(c, outs):
        for m, value in reversed(list(zip(masks[c], outs))):
            with jax.named_scope(f"home_{m}"):
                returned[m] = to_expert(value, m)
        return [returned[m] for m in masks[c]]

    blocks = dict(enumerate(blocks))
    arrived = {}

    def landing(some):
        for m in some:
            arrived[m] = dispatch(m, blocks.pop(m))

    half = len(masks[0]) // 2
    each = range(2 * half)
    landing(masks[0][half:] + masks[1][half:] + masks[1][:half] + masks[0][:half])
    arrived, blocks = settled((arrived, blocks))
    x0 = features(0, [arrived[m] for m in masks[0]])
    x1 = features(1, [arrived[m] for m in masks[1]])
    landing(masks[2][half:] + masks[2][:half] + masks[3][half:])
    y0 = rows(0, x0, *[arrived[m] for m in masks[2]])
    arrived, blocks, x1, y0 = settled((arrived, blocks, x1, y0))
    x2 = features(2, [arrived[m] for m in masks[2]])
    landing(masks[3][:half])
    s0 = pair_sum(0, y0)
    z0 = reduce(0, s0, PIECES)
    y1 = rows(1, x1)
    x3 = features(3, [arrived[m] for m in masks[3]])
    ahead = [pieces[0] for pieces in z0["gathered"]]
    s1 = pair_sum(1, y1, *ahead, *x2["mine"][1:], x2["pair"], *[arrived[m] for m in masks[3]])
    z1 = reduce(1, s1, PIECES)
    ahead = [pieces[0] for pieces in z1["gathered"]]
    y2 = rows(2, x2, *s1["sums"])
    s2 = pair_sum(2, y2, *ahead, *x3["mine"][1:], x3["pair"])
    z2 = reduce(2, s2, 1)
    outs = [finished(z0, n, *s2["sums"]) for n in each]
    y3 = rows(3, x3, *s2["sums"], *outs)
    due = home(0, outs)
    ahead = [pieces[0] for pieces in z2["gathered"]] + [pieces[-1] for pieces in z1["gathered"]]
    s3 = pair_sum(3, y3, *due, *ahead)
    z3 = reduce(3, s3, PIECES)
    home(1, [finished(z1, n) for n in each])
    home(2, [finished(z2, n, *s3["sums"]) for n in each])
    late = [finished(z3, n) for n in each[half:]]
    home(3, [finished(z3, n, *late) for n in each[:half]] + late)
    last = masks[3][:half]
    mixed = unpack(column, {m: v for m, v in returned.items() if m not in last}, None)
    return unpack(column, {m: returned[m] for m in last}, mixed)


def solution(mesh):
    return jax.shard_map(
        on_device,
        mesh=mesh,
        in_specs=(
            P("expert", "tensor"),
            P(),
            P("expert", None, "tensor"),
            P("expert", None, "tensor"),
            P("expert", "tensor", None),
            P("expert", None),
        ),
        out_specs=P("expert", "tensor"),
        check_vma=False,
    )
```

```python
import functools

import jax
import jax.numpy as jnp
from jax import lax
from jax.experimental import pallas as pl
from jax.experimental.pallas import tpu as pltpu
from jax.sharding import PartitionSpec as P

CHUNKS = 4
LOADS = 2
PIECES = 2
MIB = 1 << 20
HBM = pl.BlockSpec(memory_space=pl.ANY)
VMEM = pl.BlockSpec(memory_space=pltpu.VMEM)
SMEM = pl.BlockSpec(memory_space=pltpu.SMEM)


def to_expert(value, mask):
    if mask == 0:
        return value
    pairs = [(i, i ^ (2 * mask)) for i in range(lax.axis_size("expert"))]
    return lax.ppermute(value, "expert", pairs)


def to_pair(value):
    return lax.ppermute(value, "expert", [(i, i ^ 1) for i in range(lax.axis_size("expert"))])


def to_tensor(value, shift):
    size = lax.axis_size("tensor")
    return lax.ppermute(value, "tensor", [(i, (i + shift) % size) for i in range(size)])


def placing_of(place, total):
    slot = lax.broadcasted_iota(jnp.int32, (total, place.shape[1]), 0)
    return (place == slot).astype(jnp.float32).astype(jnp.bfloat16)


def pack_kernel(experts, slots, info, routes, tokens, *outs):
    blocks, column = outs[:experts], outs[experts]
    chosen = routes[...]
    rows = chosen.shape[1]
    onehot = (chosen == lax.broadcasted_iota(jnp.int32, (experts, rows), 0)).astype(jnp.float32)
    earlier = lax.broadcasted_iota(jnp.int32, (rows, rows), 0) < lax.broadcasted_iota(
        jnp.int32, (rows, rows), 1
    )
    counts = jnp.dot(
        onehot.astype(jnp.bfloat16),
        earlier.astype(jnp.float32).astype(jnp.bfloat16),
        preferred_element_type=jnp.float32,
    )
    ranking = jnp.sum(counts * onehot, axis=0, keepdims=True).astype(jnp.int32)
    place = (chosen ^ info[0]) * slots + ranking
    column[...] = place
    packed = jnp.dot(
        placing_of(place, experts * slots), tokens[...], preferred_element_type=jnp.float32
    ).astype(jnp.bfloat16)
    for m in range(experts):
        blocks[m][...] = packed[m * slots : (m + 1) * slots]


def pack(info, routes, tokens, experts, slots):
    rows, width = tokens.shape
    steps = 2 if width % 256 == 0 else 1
    band = width // steps
    outs = pl.pallas_call(
        functools.partial(pack_kernel, experts, slots),
        grid=(steps,),
        in_specs=[
            SMEM,
            pl.BlockSpec((1, rows), lambda i: (0, 0)),
            pl.BlockSpec((rows, band), lambda i: (0, i)),
        ],
        out_specs=[pl.BlockSpec((slots, band), lambda i: (0, i))] * experts
        + [pl.BlockSpec((1, rows), lambda i: (0, 0))],
        out_shape=[jax.ShapeDtypeStruct((slots, width), jnp.bfloat16)] * experts
        + [jax.ShapeDtypeStruct((1, rows), jnp.int32)],
        compiler_params=pltpu.CompilerParams(vmem_limit_bytes=24 * MIB),
        cost_estimate=pl.CostEstimate(
            flops=2 * rows * experts * slots * width, bytes_accessed=6 * rows * width, transcendentals=0
        ),
        name="pack",
    )(info, routes.reshape(1, rows), pltpu.with_memory_space_constraint(tokens, pltpu.HBM))
    return outs[:experts], outs[experts]


def unpack_kernel(masks, slots, column, *refs):
    blocks, earlier, mixed = refs[: len(masks)], refs[len(masks) : -1], refs[-1]
    ordered = jnp.concatenate([b[...] for b in blocks], axis=0)
    place = column[...]
    placing = jnp.concatenate([placing_of(place - m * slots, slots) for m in masks], axis=0)
    total = lax.dot_general(
        placing, ordered, (((0,), (0,)), ((), ())), preferred_element_type=jnp.float32
    )
    for part in earlier:
        total = total + part[...].astype(jnp.float32)
    mixed[...] = total.astype(jnp.bfloat16)


def unpack(column, blocks, earlier):
    masks = sorted(blocks)
    slots, width = blocks[masks[0]].shape
    rows = column.shape[1]
    steps = 2 if width % 256 == 0 else 1
    band = width // steps
    whole = pl.BlockSpec((rows, band), lambda i: (0, i))
    before = [] if earlier is None else [earlier]
    return pl.pallas_call(
        functools.partial(unpack_kernel, masks, slots),
        grid=(steps,),
        in_specs=[pl.BlockSpec((1, rows), lambda i: (0, 0))]
        + [pl.BlockSpec((slots, band), lambda i: (0, i))] * len(masks)
        + [whole] * len(before),
        out_specs=whole,
        out_shape=jax.ShapeDtypeStruct((rows, width), jnp.bfloat16),
        compiler_params=pltpu.CompilerParams(vmem_limit_bytes=24 * MIB),
        cost_estimate=pl.CostEstimate(
            flops=16 * len(masks) * rows * slots * width, bytes_accessed=6 * rows * width, transcendentals=0
        ),
        name="unpack",
    )(column, *[blocks[m] for m in masks], *before)


def expert_kernel(parts, hid_step, out_step, loading, info, *refs):
    mine, theirs, (router_t, *weights) = refs[:parts], refs[parts : 2 * parts], refs[2 * parts : 2 * parts + 4]
    kept, given = refs[2 * parts + 4 : 3 * parts + 4], refs[3 * parts + 4]
    rest = refs[3 * parts + 5 :]
    if loading:
        sources, weights, rest = weights, rest[:3], rest[3:]
    wg, wu, wd = weights
    x_all, h_all, o_buf, x_sem, o_sem, *rest = rest
    if loading:
        proj, g_sem, u_sem, d_sem = rest
    half, width = mine[0].shape
    hidden = wg.shape[2]
    index, expert = info[0], info[1]
    order = list(range(1, parts)) + [0]
    steps = range(0, hidden, hid_step)

    def span(t):
        return pl.ds(pl.multiple_of(lax.rem(index + t, parts) * width, 128), width)

    x_copies, g_copies, u_copies, d_copies, o_copies = [], [], [], [], []
    for t in range(parts):
        own_rows, pair_rows = pl.ds(0, half), pl.ds(half, half)
        x_copies += [
            pltpu.make_async_copy(mine[t], x_all.at[own_rows, span(t)], x_sem.at[0, t]),
            pltpu.make_async_copy(theirs[t], x_all.at[pair_rows, span(t)], x_sem.at[1, t]),
        ]
    if loading:
        band = wg.shape[1] // LOADS
        for n in range(LOADS):
            part = (0, pl.ds(n * band, band))
            g_copies.append(pltpu.make_async_copy(sources[0].at[part], wg.at[part], g_sem.at[n]))
            u_copies.append(pltpu.make_async_copy(sources[1].at[part], wu.at[part], u_sem.at[n]))
            part = (0, pl.ds(n * (hidden // LOADS), hidden // LOADS))
            d_copies.append(pltpu.make_async_copy(sources[2].at[part], wd.at[part], d_sem.at[n]))
    loads = [copy for pair in zip(g_copies, u_copies) for copy in pair] + d_copies
    for copy in x_copies + loads:
        copy.start()
    for copy in x_copies:
        copy.wait()
    logits = lax.dot_general(
        x_all[...], router_t[...], (((1,), (1,)), ((), ())), preferred_element_type=jnp.float32
    )
    names = lax.broadcasted_iota(jnp.int32, logits.shape, 1)
    score = jnp.sum(jnp.where(names == expert, logits, 0.0), axis=1, keepdims=True)
    scale = 1.0 / (1.0 + jnp.exp(-score))
    if loading:
        for n in range(LOADS):
            part = slice(n * band, (n + 1) * band)
            for i, (copies, w) in enumerate(((g_copies, wg), (u_copies, wu))):
                copies[n].wait()
                term = jnp.dot(x_all[:, part], w[0, part, :], preferred_element_type=jnp.float32)
                proj[i] = term if n == 0 else proj[i] + term
    for j in steps:
        cols = slice(j, j + hid_step)
        if loading:
            gate, up = proj[0, :, cols], proj[1, :, cols]
        else:
            gate = jnp.dot(x_all[...], wg[0, :, cols], preferred_element_type=jnp.float32)
            up = jnp.dot(x_all[...], wu[0, :, cols], preferred_element_type=jnp.float32)
        gate, up = scale * gate, scale * up
        h_all[:, cols] = (gate / (1.0 + jnp.exp(-gate)) * up).astype(jnp.bfloat16)
    for copy in d_copies:
        copy.wait()
    for t in order:
        for c in range(0, width, out_step):
            cols = pl.ds(pl.multiple_of(lax.rem(index + t, parts) * width + c, 128), out_step)
            o_buf[t, :, c : c + out_step] = jnp.dot(
                h_all[...], wd[0, :, cols], preferred_element_type=jnp.float32
            ).astype(jnp.bfloat16)
        o_copies += [
            pltpu.make_async_copy(
                o_buf.at[t, pl.ds(half, half)], given.at[:, pl.ds(t * width, width)], o_sem.at[1, t]
            ),
            pltpu.make_async_copy(o_buf.at[t, pl.ds(0, half)], kept[t], o_sem.at[0, t]),
        ]
        o_copies[-2].start()
        o_copies[-1].start()
    for copy in o_copies:
        copy.wait()


def expert_chunk(info, mine, theirs, router_t, weights, loading):
    parts = len(mine)
    half, width = mine[0].shape
    rows, model = 2 * half, parts * width
    hidden = weights[0].shape[2]
    hid_step = min(256, hidden)
    out_step = 1280 if width % 1280 == 0 else width
    bf16 = jnp.bfloat16
    held_in, held_out = ([HBM] * 3, [VMEM] * 3) if loading else ([VMEM] * 3, [])
    load_scratch = [pltpu.VMEM((2, rows, hidden), jnp.float32)] + [pltpu.SemaphoreType.DMA((LOADS,))] * 3
    load_scratch = load_scratch if loading else []
    place = pltpu.HBM if loading else pltpu.VMEM
    outs = pl.pallas_call(
        functools.partial(expert_kernel, parts, hid_step, out_step, loading),
        in_specs=[SMEM] + [HBM] * (2 * parts) + [VMEM] + held_in,
        out_specs=[HBM] * (parts + 1) + held_out,
        out_shape=[jax.ShapeDtypeStruct((half, width), bf16)] * parts
        + [jax.ShapeDtypeStruct((half, model), bf16)]
        + [pltpu.VMEM(w.shape, w.dtype) for w in weights if loading],
        scratch_shapes=[
            pltpu.VMEM((rows, model), bf16),
            pltpu.VMEM((rows, hidden), bf16),
            pltpu.VMEM((parts, rows, width), bf16),
            pltpu.SemaphoreType.DMA((2, parts)),
            pltpu.SemaphoreType.DMA((2, parts)),
        ]
        + load_scratch,
        compiler_params=pltpu.CompilerParams(vmem_limit_bytes=16 * MIB),
        cost_estimate=pl.CostEstimate(
            flops=6 * rows * hidden * model,
            bytes_accessed=4 * rows * model,
            transcendentals=rows * hidden,
        ),
        name="expert_rows",
    )(info, *mine, *theirs, router_t, *[pltpu.with_memory_space_constraint(w, place) for w in weights])
    return outs[:parts], outs[parts], list(outs[parts + 1 :]) or weights


def settled(live):
    leaves, shape = jax.tree.flatten(live)
    return jax.tree.unflatten(shape, lax.optimization_barrier(leaves))


def after(value, *earlier):
    return lax.optimization_barrier((value, *earlier))[0]


def f32(value):
    return value.astype(jnp.float32)


def piece_rows(pieces, rows):
    extent = pieces[0].shape[0]
    n = rows.start // extent
    return pieces[n][rows.start - n * extent : rows.stop - n * extent]


def on_device(tokens, router, gate_weight, up_weight, down_weight, routes):
    experts = router.shape[1]
    slots = 2 * tokens.shape[0] // experts
    part_cols = tokens.shape[1]
    parts = lax.axis_size("tensor")
    expert = lax.axis_index("expert") // 2
    place = jnp.stack([lax.axis_index("tensor"), expert]).astype(jnp.int32)
    router_t = router.T
    blocks, column = pack(expert.astype(jnp.int32).reshape(1), routes, tokens, experts, slots)
    half = experts // (2 * CHUNKS)
    light, heavy = list(range(experts // 2))[::-1], list(range(experts // 2, experts))
    masks = [light[c * half : (c + 1) * half] + heavy[c * half : (c + 1) * half] for c in range(CHUNKS)]
    weights = [gate_weight, up_weight, down_weight]
    returned = {}

    def dispatch(m, value):
        with jax.named_scope(f"dispatch_{m}"):
            return to_expert(value, m)

    def features(c, some):
        own = jnp.concatenate(some, axis=0)
        mine = [own] + [None] * (parts - 1)
        with jax.named_scope(f"features_{c}"):
            for t in range(1, parts):
                mine[parts - t] = to_tensor(own, t)
        with jax.named_scope(f"pair_{c}"):
            return dict(mine=mine, pair=to_pair(own))

    def rows(c, chunk):
        nonlocal weights
        with jax.named_scope(f"pair_{c}"):
            theirs = [chunk["pair"]] + [to_pair(v) for v in chunk["mine"][1:]]
        with jax.named_scope(f"rows_{c}"):
            kept, given, weights = expert_chunk(
                place, chunk["mine"], theirs, router_t, weights, loading=c == 0
            )
        return dict(kept=kept, given=given)

    def pair_sum(c, chunk):
        kept, sums = chunk["kept"], []
        with jax.named_scope(f"partial_{c}"):
            given = to_pair(chunk["given"])
            for t in range(1, parts):
                other = given[:, t * part_cols : (t + 1) * part_cols]
                sums.append((f32(kept[t]) + f32(other)).astype(jnp.bfloat16))
        return dict(kept=kept[0], stay=given[:, :part_cols], sums=sums)

    def reduce(c, chunk, pieces):
        extent = chunk["sums"][0].shape[0] // pieces
        with jax.named_scope(f"reduce_{c}"):
            gathered = [
                [to_tensor(v[n * extent : (n + 1) * extent], t) for n in range(pieces)]
                for t, v in enumerate(chunk["sums"], start=1)
            ]
        return dict(kept=chunk["kept"], stay=chunk["stay"], gathered=gathered)

    def finished(chunk, n, *earlier):
        span = slice(n * slots, (n + 1) * slots)
        total = f32(after(chunk["kept"], *earlier)[span]) + f32(chunk["stay"][span])
        for pieces in chunk["gathered"]:
            total = total + f32(piece_rows(pieces, span))
        return total.astype(jnp.bfloat16)

    def home(c, outs):
        for m, value in reversed(list(zip(masks[c], outs))):
            with jax.named_scope(f"home_{m}"):
                returned[m] = to_expert(value, m)
        return [returned[m] for m in masks[c]]

    blocks = dict(enumerate(blocks))
    arrived = {}

    def landing(some):
        for m in some:
            arrived[m] = dispatch(m, blocks.pop(m))

    landing(reversed(masks[0]))
    arrived, blocks = settled((arrived, blocks))
    x0 = features(0, [arrived[m] for m in masks[0]])
    landing(reversed(masks[1]))
    arrived, blocks, x0 = settled((arrived, blocks, x0))
    x1 = features(1, [arrived[m] for m in masks[1]])
    landing(masks[2][half:] + masks[2][:half] + masks[3][:half])
    y0 = rows(0, x0)
    arrived, blocks, x1, y0 = settled((arrived, blocks, x1, y0))
    each = range(2 * half)
    x2 = features(2, [arrived[m] for m in masks[2]])
    landing(masks[3][half:])
    z0 = reduce(0, pair_sum(0, y0), 1)
    y1 = rows(1, x1)
    arrived, x2, y1, z0 = settled((arrived, x2, y1, z0))
    x3 = features(3, [arrived[m] for m in masks[3]])
    home(0, [finished(z0, n) for n in each])
    z1 = reduce(1, pair_sum(1, y1), 1)
    y2 = rows(2, x2)
    returned, x3, y2, z1 = settled((returned, x3, y2, z1))
    home(1, [finished(z1, n) for n in each])
    z2 = reduce(2, pair_sum(2, y2), 1)
    y3 = rows(3, x3)
    returned, y3, z2 = settled((returned, y3, z2))
    z3 = reduce(3, pair_sum(3, y3), PIECES)
    home(2, [finished(z2, n) for n in each])
    late = [finished(z3, n) for n in each[half:]]
    home(3, [finished(z3, n, *late) for n in each[:half]] + late)
    return unpack(column, returned, None)


def solution(mesh):
    return jax.shard_map(
        on_device,
        mesh=mesh,
        in_specs=(
            P("expert", "tensor"),
            P(),
            P("expert", None, "tensor"),
            P("expert", None, "tensor"),
            P("expert", "tensor", None),
            P("expert", None),
        ),
        out_specs=P("expert", "tensor"),
        check_vma=False,
    )
```

```python
import functools

import jax
import jax.numpy as jnp
from jax import lax
from jax.experimental import pallas as pl
from jax.experimental.pallas import tpu as pltpu
from jax.sharding import PartitionSpec as P

CHUNKS = 4
LOADS = 2
PIECES = 2
MIB = 1 << 20
HBM = pl.BlockSpec(memory_space=pl.ANY)
VMEM = pl.BlockSpec(memory_space=pltpu.VMEM)
SMEM = pl.BlockSpec(memory_space=pltpu.SMEM)


def to_expert(value, mask):
    if mask == 0:
        return value
    pairs = [(i, i ^ (2 * mask)) for i in range(lax.axis_size("expert"))]
    return lax.ppermute(value, "expert", pairs)


def to_pair(value):
    return lax.ppermute(value, "expert", [(i, i ^ 1) for i in range(lax.axis_size("expert"))])


def to_tensor(value, shift):
    size = lax.axis_size("tensor")
    return lax.ppermute(value, "tensor", [(i, (i + shift) % size) for i in range(size)])


def placing_of(place, total):
    slot = lax.broadcasted_iota(jnp.int32, (total, place.shape[1]), 0)
    return (place == slot).astype(jnp.float32).astype(jnp.bfloat16)


def pack_kernel(experts, slots, info, routes, tokens, *outs):
    blocks, column = outs[:experts], outs[experts]
    chosen = routes[...]
    rows = chosen.shape[1]
    onehot = (chosen == lax.broadcasted_iota(jnp.int32, (experts, rows), 0)).astype(jnp.float32)
    earlier = lax.broadcasted_iota(jnp.int32, (rows, rows), 0) < lax.broadcasted_iota(
        jnp.int32, (rows, rows), 1
    )
    counts = jnp.dot(
        onehot.astype(jnp.bfloat16),
        earlier.astype(jnp.float32).astype(jnp.bfloat16),
        preferred_element_type=jnp.float32,
    )
    ranking = jnp.sum(counts * onehot, axis=0, keepdims=True).astype(jnp.int32)
    place = (chosen ^ info[0]) * slots + ranking
    column[...] = place
    packed = jnp.dot(
        placing_of(place, experts * slots), tokens[...], preferred_element_type=jnp.float32
    ).astype(jnp.bfloat16)
    for m in range(experts):
        blocks[m][...] = packed[m * slots : (m + 1) * slots]


def pack(info, routes, tokens, experts, slots):
    rows, width = tokens.shape
    steps = 2 if width % 256 == 0 else 1
    band = width // steps
    outs = pl.pallas_call(
        functools.partial(pack_kernel, experts, slots),
        grid=(steps,),
        in_specs=[
            SMEM,
            pl.BlockSpec((1, rows), lambda i: (0, 0)),
            pl.BlockSpec((rows, band), lambda i: (0, i)),
        ],
        out_specs=[pl.BlockSpec((slots, band), lambda i: (0, i))] * experts
        + [pl.BlockSpec((1, rows), lambda i: (0, 0))],
        out_shape=[jax.ShapeDtypeStruct((slots, width), jnp.bfloat16)] * experts
        + [jax.ShapeDtypeStruct((1, rows), jnp.int32)],
        compiler_params=pltpu.CompilerParams(vmem_limit_bytes=24 * MIB),
        cost_estimate=pl.CostEstimate(
            flops=2 * rows * experts * slots * width, bytes_accessed=6 * rows * width, transcendentals=0
        ),
        name="pack",
    )(info, routes.reshape(1, rows), pltpu.with_memory_space_constraint(tokens, pltpu.HBM))
    return outs[:experts], outs[experts]


def unpack_kernel(masks, slots, column, *refs):
    blocks, earlier, mixed = refs[: len(masks)], refs[len(masks) : -1], refs[-1]
    ordered = jnp.concatenate([b[...] for b in blocks], axis=0)
    place = column[...]
    placing = jnp.concatenate([placing_of(place - m * slots, slots) for m in masks], axis=0)
    total = lax.dot_general(
        placing, ordered, (((0,), (0,)), ((), ())), preferred_element_type=jnp.float32
    )
    for part in earlier:
        total = total + part[...].astype(jnp.float32)
    mixed[...] = total.astype(jnp.bfloat16)


def unpack(column, blocks, earlier):
    masks = sorted(blocks)
    slots, width = blocks[masks[0]].shape
    rows = column.shape[1]
    steps = 2 if width % 256 == 0 else 1
    band = width // steps
    whole = pl.BlockSpec((rows, band), lambda i: (0, i))
    before = [] if earlier is None else [earlier]
    return pl.pallas_call(
        functools.partial(unpack_kernel, masks, slots),
        grid=(steps,),
        in_specs=[pl.BlockSpec((1, rows), lambda i: (0, 0))]
        + [pl.BlockSpec((slots, band), lambda i: (0, i))] * len(masks)
        + [whole] * len(before),
        out_specs=whole,
        out_shape=jax.ShapeDtypeStruct((rows, width), jnp.bfloat16),
        compiler_params=pltpu.CompilerParams(vmem_limit_bytes=24 * MIB),
        cost_estimate=pl.CostEstimate(
            flops=16 * len(masks) * rows * slots * width, bytes_accessed=6 * rows * width, transcendentals=0
        ),
        name="unpack",
    )(column, *[blocks[m] for m in masks], *before)


def expert_kernel(parts, hid_step, out_step, loading, info, *refs):
    mine, theirs, (router_t, *weights) = refs[:parts], refs[parts : 2 * parts], refs[2 * parts : 2 * parts + 4]
    kept, given = refs[2 * parts + 4 : 3 * parts + 4], refs[3 * parts + 4]
    rest = refs[3 * parts + 5 :]
    if loading:
        sources, weights, rest = weights, rest[:3], rest[3:]
    wg, wu, wd = weights
    x_all, h_all, o_buf, x_sem, o_sem, *rest = rest
    if loading:
        proj, g_sem, u_sem, d_sem = rest
    half, width = mine[0].shape
    hidden = wg.shape[2]
    index, expert = info[0], info[1]
    order = list(range(1, parts)) + [0]
    steps = range(0, hidden, hid_step)

    def span(t):
        return pl.ds(pl.multiple_of(lax.rem(index + t, parts) * width, 128), width)

    x_copies, g_copies, u_copies, d_copies, o_copies = [], [], [], [], []
    for t in range(parts):
        own_rows, pair_rows = pl.ds(0, half), pl.ds(half, half)
        x_copies += [
            pltpu.make_async_copy(mine[t], x_all.at[own_rows, span(t)], x_sem.at[0, t]),
            pltpu.make_async_copy(theirs[t], x_all.at[pair_rows, span(t)], x_sem.at[1, t]),
        ]
    if loading:
        band = wg.shape[1] // LOADS
        for n in range(LOADS):
            part = (0, pl.ds(n * band, band))
            g_copies.append(pltpu.make_async_copy(sources[0].at[part], wg.at[part], g_sem.at[n]))
            u_copies.append(pltpu.make_async_copy(sources[1].at[part], wu.at[part], u_sem.at[n]))
            part = (0, pl.ds(n * (hidden // LOADS), hidden // LOADS))
            d_copies.append(pltpu.make_async_copy(sources[2].at[part], wd.at[part], d_sem.at[n]))
    loads = [copy for pair in zip(g_copies, u_copies) for copy in pair] + d_copies
    for copy in x_copies + loads:
        copy.start()
    for copy in x_copies:
        copy.wait()
    logits = lax.dot_general(
        x_all[...], router_t[...], (((1,), (1,)), ((), ())), preferred_element_type=jnp.float32
    )
    names = lax.broadcasted_iota(jnp.int32, logits.shape, 1)
    score = jnp.sum(jnp.where(names == expert, logits, 0.0), axis=1, keepdims=True)
    scale = 1.0 / (1.0 + jnp.exp(-score))
    if loading:
        for n in range(LOADS):
            part = slice(n * band, (n + 1) * band)
            for i, (copies, w) in enumerate(((g_copies, wg), (u_copies, wu))):
                copies[n].wait()
                term = jnp.dot(x_all[:, part], w[0, part, :], preferred_element_type=jnp.float32)
                proj[i] = term if n == 0 else proj[i] + term
    for j in steps:
        cols = slice(j, j + hid_step)
        if loading:
            gate, up = proj[0, :, cols], proj[1, :, cols]
        else:
            gate = jnp.dot(x_all[...], wg[0, :, cols], preferred_element_type=jnp.float32)
            up = jnp.dot(x_all[...], wu[0, :, cols], preferred_element_type=jnp.float32)
        gate, up = scale * gate, scale * up
        h_all[:, cols] = (gate / (1.0 + jnp.exp(-gate)) * up).astype(jnp.bfloat16)
    for copy in d_copies:
        copy.wait()
    for t in order:
        for c in range(0, width, out_step):
            cols = pl.ds(pl.multiple_of(lax.rem(index + t, parts) * width + c, 128), out_step)
            o_buf[t, :, c : c + out_step] = jnp.dot(
                h_all[...], wd[0, :, cols], preferred_element_type=jnp.float32
            ).astype(jnp.bfloat16)
        o_copies += [
            pltpu.make_async_copy(
                o_buf.at[t, pl.ds(half, half)], given.at[:, pl.ds(t * width, width)], o_sem.at[1, t]
            ),
            pltpu.make_async_copy(o_buf.at[t, pl.ds(0, half)], kept[t], o_sem.at[0, t]),
        ]
        o_copies[-2].start()
        o_copies[-1].start()
    for copy in o_copies:
        copy.wait()


def expert_chunk(info, mine, theirs, router_t, weights, loading):
    parts = len(mine)
    half, width = mine[0].shape
    rows, model = 2 * half, parts * width
    hidden = weights[0].shape[2]
    hid_step = min(256, hidden)
    out_step = 1280 if width % 1280 == 0 else width
    bf16 = jnp.bfloat16
    held_in, held_out = ([HBM] * 3, [VMEM] * 3) if loading else ([VMEM] * 3, [])
    load_scratch = [pltpu.VMEM((2, rows, hidden), jnp.float32)] + [pltpu.SemaphoreType.DMA((LOADS,))] * 3
    load_scratch = load_scratch if loading else []
    place = pltpu.HBM if loading else pltpu.VMEM
    outs = pl.pallas_call(
        functools.partial(expert_kernel, parts, hid_step, out_step, loading),
        in_specs=[SMEM] + [HBM] * (2 * parts) + [VMEM] + held_in,
        out_specs=[HBM] * (parts + 1) + held_out,
        out_shape=[jax.ShapeDtypeStruct((half, width), bf16)] * parts
        + [jax.ShapeDtypeStruct((half, model), bf16)]
        + [pltpu.VMEM(w.shape, w.dtype) for w in weights if loading],
        scratch_shapes=[
            pltpu.VMEM((rows, model), bf16),
            pltpu.VMEM((rows, hidden), bf16),
            pltpu.VMEM((parts, rows, width), bf16),
            pltpu.SemaphoreType.DMA((2, parts)),
            pltpu.SemaphoreType.DMA((2, parts)),
        ]
        + load_scratch,
        compiler_params=pltpu.CompilerParams(vmem_limit_bytes=16 * MIB),
        cost_estimate=pl.CostEstimate(
            flops=6 * rows * hidden * model,
            bytes_accessed=4 * rows * model,
            transcendentals=rows * hidden,
        ),
        name="expert_rows",
    )(info, *mine, *theirs, router_t, *[pltpu.with_memory_space_constraint(w, place) for w in weights])
    return outs[:parts], outs[parts], list(outs[parts + 1 :]) or weights


def settled(live):
    leaves, shape = jax.tree.flatten(live)
    return jax.tree.unflatten(shape, lax.optimization_barrier(leaves))


def after(value, *earlier):
    return lax.optimization_barrier((value, *earlier))[0]


def f32(value):
    return value.astype(jnp.float32)


def piece_rows(pieces, rows):
    extent = pieces[0].shape[0]
    n = rows.start // extent
    return pieces[n][rows.start - n * extent : rows.stop - n * extent]


def on_device(tokens, router, gate_weight, up_weight, down_weight, routes):
    experts = router.shape[1]
    slots = 2 * tokens.shape[0] // experts
    part_cols = tokens.shape[1]
    parts = lax.axis_size("tensor")
    expert = lax.axis_index("expert") // 2
    place = jnp.stack([lax.axis_index("tensor"), expert]).astype(jnp.int32)
    router_t = router.T
    blocks, column = pack(expert.astype(jnp.int32).reshape(1), routes, tokens, experts, slots)
    half = experts // (2 * CHUNKS)
    light, heavy = list(range(experts // 2))[::-1], list(range(experts // 2, experts))
    masks = [light[c * half : (c + 1) * half] + heavy[c * half : (c + 1) * half] for c in range(CHUNKS)]
    weights = [gate_weight, up_weight, down_weight]
    returned = {}

    def dispatch(m, value):
        with jax.named_scope(f"dispatch_{m}"):
            return to_expert(value, m)

    def joined(c):
        return jnp.concatenate([arrived[m] for m in masks[c]], axis=0)

    def features(c, own):
        mine = [own] + [None] * (parts - 1)
        with jax.named_scope(f"features_{c}"):
            for t in range(1, parts):
                mine[parts - t] = to_tensor(own, t)
        with jax.named_scope(f"pair_{c}"):
            return dict(mine=mine, pair=to_pair(own))

    def rows(c, chunk):
        nonlocal weights
        with jax.named_scope(f"pair_{c}"):
            theirs = [chunk["pair"]] + [to_pair(v) for v in chunk["mine"][1:]]
        with jax.named_scope(f"rows_{c}"):
            kept, given, weights = expert_chunk(
                place, chunk["mine"], theirs, router_t, weights, loading=c == 0
            )
        return dict(kept=kept, given=given)

    def pair_sum(c, chunk):
        kept, sums = chunk["kept"], []
        with jax.named_scope(f"partial_{c}"):
            given = to_pair(chunk["given"])
            for t in range(1, parts):
                other = given[:, t * part_cols : (t + 1) * part_cols]
                sums.append((f32(kept[t]) + f32(other)).astype(jnp.bfloat16))
        return dict(kept=kept[0], stay=given[:, :part_cols], sums=sums)

    def reduce(c, chunk, pieces):
        extent = chunk["sums"][0].shape[0] // pieces
        with jax.named_scope(f"reduce_{c}"):
            gathered = [
                [to_tensor(v[n * extent : (n + 1) * extent], t) for n in range(pieces)]
                for t, v in enumerate(chunk["sums"], start=1)
            ]
        return dict(kept=chunk["kept"], stay=chunk["stay"], gathered=gathered)

    def finished(chunk, n, *earlier):
        span = slice(n * slots, (n + 1) * slots)
        total = f32(after(chunk["kept"], *earlier)[span]) + f32(chunk["stay"][span])
        for pieces in chunk["gathered"]:
            total = total + f32(piece_rows(pieces, span))
        return total.astype(jnp.bfloat16)

    def home(c, outs):
        for m, value in reversed(list(zip(masks[c], outs))):
            with jax.named_scope(f"home_{m}"):
                returned[m] = to_expert(value, m)
        return [returned[m] for m in masks[c]]

    blocks = dict(enumerate(blocks))
    arrived = {}

    def landing(some):
        for m in some:
            arrived[m] = dispatch(m, blocks.pop(m))

    landing(reversed(masks[0]))
    own, blocks = settled((joined(0), blocks))
    x0 = features(0, own)
    landing(reversed(masks[1]))
    own, blocks, x0 = settled((joined(1), blocks, x0))
    x1 = features(1, own)
    landing(masks[2][half:] + masks[2][:half] + masks[3][:half])
    y0 = rows(0, x0)
    arrived, blocks, x1, y0 = settled((arrived, blocks, x1, y0))
    each = range(2 * half)
    x2 = features(2, joined(2))
    landing(masks[3][half:])
    z0 = reduce(0, pair_sum(0, y0), 1)
    y1 = rows(1, x1)
    arrived, x2, y1, z0 = settled((arrived, x2, y1, z0))
    x3 = features(3, joined(3))
    home(0, [finished(z0, n) for n in each])
    z1 = reduce(1, pair_sum(1, y1), 1)
    y2 = rows(2, x2)
    returned, x3, y2, z1 = settled((returned, x3, y2, z1))
    home(1, [finished(z1, n) for n in each])
    z2 = reduce(2, pair_sum(2, y2), 1)
    y3 = rows(3, x3)
    returned, y3, z2 = settled((returned, y3, z2))
    z3 = reduce(3, pair_sum(3, y3), PIECES)
    home(2, [finished(z2, n) for n in each])
    late = [finished(z3, n) for n in each[half:]]
    home(3, [finished(z3, n, *late) for n in each[:half]] + late)
    return unpack(column, returned, None)


def solution(mesh):
    return jax.shard_map(
        on_device,
        mesh=mesh,
        in_specs=(
            P("expert", "tensor"),
            P(),
            P("expert", None, "tensor"),
            P("expert", None, "tensor"),
            P("expert", "tensor", None),
            P("expert", None),
        ),
        out_specs=P("expert", "tensor"),
        check_vma=False,
    )
```
